256 devices in a mesh: seq: 64 (over z, y, core), dp: 4 (over x).
Axes of the slice: x: 4, y: 4, z: 8, core: 2. Of those that a mesh axis runs over, the one named last changes fastest.
Arguments:
- queries: bfloat16 [262144, 128], P(('dp', 'seq')), parts along dimension 0, may hold values from -150 to 150
- key_rows: bfloat16 [262144, 128], P(('dp', 'seq')), parts along dimension 0, may hold values from -5 to 5
- values: bfloat16 [262144, 128], P(('dp', 'seq')), parts along dimension 0, may hold values from -6 to 6
- out_grad: bfloat16 [262144, 128], P(('dp', 'seq')), parts along dimension 0, may hold values from -6 to 6
- cluster_id: int32 [4, 65536], P('dp', 'seq'), parts along dimension 0, may hold values from 0 to 1023, as said below
- cluster_owner: int32 [4, 1024], P('dp'), parts along dimension 0, may hold values from 0 to 1023, as said below
- old_centroids: float32 [4, 1024, 128], P('dp', 'seq'), parts along dimension 0, may hold values from -0.6 to 0.6
Outputs:
- attn_out: bfloat16 [262144, 128], P(('dp', 'seq')), parts along dimension 0
- grad_queries: bfloat16 [262144, 128], P(('dp', 'seq')), parts along dimension 0
- grad_keys: bfloat16 [262144, 128], P(('dp', 'seq')), parts along dimension 0
- grad_values: bfloat16 [262144, 128], P(('dp', 'seq')), parts along dimension 0
- new_centroids: float32 [4, 1024, 128], P('dp', 'seq'), parts along dimension 0
The draws below stay inside these ranges and needn't reach their ends.
There are 4 independent parts, one for each index of `dp`. The reference program is written for one: setup_inputs(seed, part) draws one part's arguments, and reference() takes and returns one part's arrays. A program takes and returns all parts, laid end to end along the dimension named above; each array names one. Nothing has to cross between parts.
Inputs may be any that keep to these rules, and one draw needn't show every extreme that they name: `cluster_id`: each cluster holds 128 tokens at most and 16 at least; the 16 clusters of one owner hold 1024 tokens together, and each owner has a cluster of exactly 128. The 1024 tokens of one device name clusters of one owner at most 32 times per head, and every device reaches that for some owner. `cluster_owner`: each head's row is a permutation; value v puts the cluster on device v // 16 of seq as its cluster v % 16.
All inputs are finite; a program needn't handle non-finite values.
Results may differ from the reference program's by a relative error of at most 0.0056.
Values may be sent and summed in bfloat16 or wider, within the bound.
A program may use at most 64 MiB of HBM per device.

```python
import math
import jax
import jax.numpy as jnp
from jax import lax

HEADS = 1
HD = 128
CL_DEV = 16
TOK_DEV = 1024
TOKENS = 65536
CLUSTERS = 1024
CAP = 128


def routing_plan(key):
    base = jax.random.fold_in(key, 101)
    seq_count = TOKENS // TOK_DEV
    block = TOK_DEV // seq_count
    mean_size = TOK_DEV // CL_DEV
    half = seq_count // 2
    half_clusters = CL_DEV // 2

    def one_head(head_key):
        parts = jax.random.split(head_key, 7)
        owner_perm = jax.random.permutation(parts[0], CLUSTERS).astype(jnp.int32)
        inverse = jnp.argsort(owner_perm, stable=True).astype(jnp.int32)
        shifts = jax.random.randint(parts[1], (half,), 0, block // 2 + 1)
        chosen = jax.random.randint(parts[2], (), 0, half)
        shifts = jnp.where(jnp.arange(half) == chosen, block, shifts)
        offsets = jnp.concatenate([shifts, -shifts])
        grid = (jnp.arange(seq_count)[None, :] - jnp.arange(seq_count)[:, None]) % seq_count
        counts = block + offsets[grid]
        row_ends = jnp.cumsum(counts, axis=1)
        row_starts = row_ends - counts
        col_starts = jnp.cumsum(counts, axis=0) - counts
        sender_rank = jax.vmap(lambda k: jax.random.permutation(k, TOK_DEV))(jax.random.split(parts[3], seq_count))
        target = jnp.sum((row_ends[:, None, :] <= sender_rank[:, :, None]).astype(jnp.int32), axis=-1)
        within = sender_rank - jnp.take_along_axis(row_starts, target, axis=1)
        arrival = jnp.take_along_axis(col_starts, target, axis=1) + within
        owner_table = jax.vmap(lambda k: jax.random.permutation(k, TOK_DEV))(jax.random.split(parts[4], seq_count))
        owner_rank = owner_table[target, arrival]
        base_sizes = jax.random.randint(parts[5], (seq_count, half_clusters), mean_size // 4, 7 * mean_size // 4 + 1)
        hot = jax.random.randint(parts[6], (seq_count, 1), 0, half_clusters)
        column = jnp.arange(half_clusters)[None, :]
        partner = (hot + 1) % half_clusters
        first = jnp.where(column == hot, 2 * mean_size, jnp.where(column == partner, 3 * mean_size // 4, base_sizes))
        second = jnp.where(column == hot, mean_size // 2, jnp.where(column == partner, 3 * mean_size // 4, 2 * mean_size - base_sizes))
        sizes = jnp.concatenate([first, second], axis=1)
        size_ends = jnp.cumsum(sizes, axis=1)
        local = jnp.sum((size_ends[target] <= owner_rank[:, :, None]).astype(jnp.int32), axis=-1)
        cluster = inverse[target * CL_DEV + local]
        return (owner_perm, cluster.reshape(TOKENS).astype(jnp.int32))
    return jax.vmap(one_head)(jax.random.split(base, HEADS))


def key_normals(key):
    base = jax.random.fold_in(key, 202)
    return jnp.clip(jax.random.normal(base, (TOKENS, HEADS * HD), jnp.float32), -5.0, 5.0)


def draw_cluster_id(key, part):
    plan = routing_plan(key)
    return plan[1]


def draw_cluster_owner(key, part):
    plan = routing_plan(key)
    return plan[0]


def draw_key_rows(key, part):
    normals = key_normals(key)
    return normals.astype(jnp.bfloat16)


def draw_queries(key, part):
    key = jax.random.fold_in(key, 14)
    first = jax.random.fold_in(key, 0)
    queries = jnp.clip(jax.random.normal(first, (TOKENS, HEADS * HD), jnp.float32), -6.0, 6.0)
    return queries.astype(jnp.bfloat16)


def steps_of(own_key, shape, cuts, smallest, high):
    loudness, own = 1.0, jax.random.fold_in(own_key, 6)
    for position, shards_of in cuts:
        steps = jnp.exp(jax.random.uniform(jax.random.fold_in(own, position), (shards_of,), jnp.float32, smallest / len(cuts), high / len(cuts)))
        loudness = loudness * jnp.repeat(steps, shape[position] // shards_of).reshape([-1 if axis == position else 1 for axis in range(len(shape))])
    return loudness


def scatter_about(rng, shape, deviation, reach, cuts=(), held_as=jnp.bfloat16):
    level = steps_of(rng, shape, cuts, -0.22, 0.18) if cuts else 1.0
    entries = jax.random.normal(rng, shape, jnp.float32) * deviation * level
    return jnp.minimum(jnp.maximum(entries, -reach), reach).astype(held_as)


def setup_inputs(seed: int = 0, part: int = 0) -> dict:
    splits = jax.random.split(jax.random.key(seed), 8)
    part_keys = jax.random.split(jax.random.fold_in(splits[7], part), 8)
    return {
        "queries": draw_queries(jax.random.fold_in(jax.random.fold_in(splits[7], part), 71), part),
        "key_rows": draw_key_rows(jax.random.fold_in(jax.random.fold_in(splits[7], part), 71), part),
        "values": scatter_about(part_keys[2], (TOKENS, HEADS * HD), 1.0, 6.0, ((0, 64),)),
        "out_grad": scatter_about(part_keys[3], (TOKENS, HEADS * HD), 1.0, 6.0, ((0, 64),)),
        "cluster_id": draw_cluster_id(jax.random.fold_in(jax.random.fold_in(splits[7], part), 71), part),
        "cluster_owner": draw_cluster_owner(jax.random.fold_in(jax.random.fold_in(splits[7], part), 71), part),
        "old_centroids": scatter_about(part_keys[6], (HEADS, CLUSTERS, HD), 0.1, 0.6, ((1, 64),), jnp.float32),
    }


def attend_block(blocks):
    query_c, key_c, value_c, grad_c, place_c = blocks
    score_scale = 1.0 / math.sqrt(HD)
    query_f = query_c.astype(jnp.float32)
    key_f = key_c.astype(jnp.float32)
    value_f = value_c.astype(jnp.float32)
    grad_f = grad_c.astype(jnp.float32)
    scores = jnp.einsum('cqd,ckd->cqk', query_f, key_f) * score_scale
    query_pos = place_c[:, :, None]
    key_pos = place_c[:, None, :]
    width_cap = place_c.shape[-1]
    diagonal = (jnp.arange(width_cap)[:, None] == jnp.arange(width_cap)[None, :])[None]
    allowed = (key_pos <= query_pos) & (query_pos < TOKENS) | diagonal
    scores = jnp.where(allowed, scores, jnp.float32(-1e+30))
    peak = lax.optimization_barrier(jnp.max(scores, axis=-1, keepdims=True))
    weights = jnp.where(allowed, jnp.exp(scores - peak), jnp.float32(0.0))
    probs = weights / lax.optimization_barrier(jnp.sum(weights, axis=-1, keepdims=True))
    probs_low = probs.astype(jnp.bfloat16)
    attn_low = jnp.einsum('cqk,ckd->cqd', probs_low.astype(jnp.float32), value_f).astype(jnp.bfloat16)
    delta = lax.optimization_barrier(jnp.sum(grad_f * attn_low.astype(jnp.float32), axis=-1))
    dprobs = jnp.einsum('cqd,ckd->cqk', grad_f, value_f)
    dscores = (probs * (dprobs - delta[..., None]) * score_scale).astype(jnp.bfloat16)
    dscores_f = dscores.astype(jnp.float32)
    grad_query = jnp.einsum('cqk,ckd->cqd', dscores_f, key_f).astype(jnp.bfloat16)
    grad_key = jnp.einsum('cqk,cqd->ckd', dscores_f, query_f).astype(jnp.bfloat16)
    grad_value = jnp.einsum('cqk,cqd->ckd', probs_low.astype(jnp.float32), grad_f).astype(jnp.bfloat16)
    return (attn_low, grad_query, grad_key, grad_value)

def reference(queries, key_rows, values, out_grad, cluster_id, cluster_owner, old_centroids):
    token_index = jnp.arange(TOKENS, dtype=jnp.int32)
    results_all = []
    centroid_all = []
    for head_index in range(HEADS):
        lower = head_index * HD
        upper = lower + HD
        query_h = queries[:, lower:upper]
        key_h = key_rows[:, lower:upper]
        value_h = values[:, lower:upper]
        grad_h = out_grad[:, lower:upper]
        owner_value = cluster_owner[head_index][cluster_id[head_index]].astype(jnp.int32)
        order = jnp.argsort(owner_value, stable=True).astype(jnp.int32)
        ordered = owner_value[order]
        starts = jnp.searchsorted(ordered, jnp.arange(CLUSTERS, dtype=jnp.int32)).astype(jnp.int32)
        ranks = (token_index - starts[ordered]).astype(jnp.int32)
        within = jnp.zeros((TOKENS,), jnp.int32).at[order].set(ranks)
        target_row = (owner_value * CAP + within).astype(jnp.int32)

        def layout(rows):
            filled = jnp.zeros((CLUSTERS * CAP, HD), rows.dtype).at[target_row].set(rows)
            return filled.reshape(CLUSTERS // CL_DEV, CL_DEV, CAP, HD)
        places = jnp.full((CLUSTERS * CAP,), TOKENS, jnp.int32).at[target_row].set(token_index)
        places = places.reshape(CLUSTERS // CL_DEV, CL_DEV, CAP)
        outcome = lax.map(attend_block, (layout(query_h), layout(key_h), layout(value_h), layout(grad_h), places))
        results_all.append(tuple((item.reshape(CLUSTERS * CAP, HD)[target_row] for item in outcome)))
        key_sum = jax.ops.segment_sum(key_h.astype(jnp.float32), owner_value, num_segments=CLUSTERS)
        member_count = jax.ops.segment_sum(jnp.ones((TOKENS,), jnp.float32), owner_value, num_segments=CLUSTERS)
        blended = 0.5 * old_centroids[head_index] + 0.5 * key_sum / member_count[:, None]
        centroid_all.append(blended / jnp.sqrt(lax.optimization_barrier(jnp.mean(blended * blended, axis=-1, keepdims=True)) + 1e-06))
    joined = [jnp.concatenate([results_all[h][j] for h in range(HEADS)], axis=1) for j in range(4)]
    return (joined[0], joined[1], joined[2], joined[3], jnp.stack(centroid_all))
```

```python
import functools
import math

import jax
import jax.numpy as jnp
from jax import lax
from jax.experimental import pallas as pl
from jax.experimental.pallas import tpu as pltpu
from jax.sharding import PartitionSpec as P

MESH = pl.DeviceIdType.MESH
HD = 128
CL_DEV = 16
TOK = 1024
DEVS = 64
ROOM = 32
PLANE = 8
PLANES = DEVS // PLANE
CHUNK = PLANE * ROOM
BLOCKS = TOK // 128
ORDER = (4, 1, 7, 3, 5, 2, 6, 0)
BF16 = jnp.bfloat16
F32 = jnp.float32


def dot(a, b):
    return jnp.dot(a, b, preferred_element_type=F32)


def dot_nt(a, b):
    return lax.dot_general(a, b, (((1,), (1,)), ((), ())), preferred_element_type=F32)


def dot_tn(a, b):
    return lax.dot_general(a, b, (((0,), (0,)), ((), ())), preferred_element_type=F32)


def iota(shape, dim):
    return lax.broadcasted_iota(jnp.int32, shape, dim).astype(F32)


def onehot(mask):
    return jnp.where(mask, 1.0, 0.0).astype(BF16)


def prefix_and_total():
    row = lax.broadcasted_iota(jnp.int32, (128, 256), 0)
    col = lax.broadcasted_iota(jnp.int32, (128, 256), 1)
    return onehot((row < col) | (col >= 128))


def token_slots(cluster_id, owner):
    ident = cluster_id[...]
    low = onehot(lax.broadcasted_iota(jnp.int32, (128, TOK), 0) == lax.rem(ident, 128))
    table = jnp.concatenate([owner[:, 128 * b : 128 * (b + 1)] for b in range(8)], axis=0)
    table_dev = lax.div(table, CL_DEV)
    table_loc = table - table_dev * CL_DEV
    tables = jnp.concatenate([table_dev, table_loc], axis=0).astype(F32).astype(BF16)
    found = dot(tables, low)
    high = lax.broadcasted_iota(jnp.int32, (8, TOK), 0) == lax.div(ident, 128)
    target = jnp.sum(jnp.where(high, found[:8], 0.0), axis=0, keepdims=True)
    local = jnp.sum(jnp.where(high, found[8:], 0.0), axis=0, keepdims=True)
    device = iota((DEVS, 128), 0)
    members = [device == target[:, 128 * b : 128 * (b + 1)] for b in range(BLOCKS)]
    counted = dot(jnp.concatenate([onehot(m) for m in members], axis=0), prefix_and_total())
    running = jnp.zeros((DEVS, 128), F32)
    ranks = []
    for b in range(BLOCKS):
        part = counted[DEVS * b : DEVS * (b + 1)]
        ranks.append(
            jnp.sum(jnp.where(members[b], part[:, :128] + running, 0.0), axis=0, keepdims=True)
        )
        running = running + part[:, 128:]
    rank = jnp.concatenate(ranks, axis=1)
    return target, local, rank


def turned(rows):
    n = rows.shape[0]
    return jnp.concatenate([rows, jnp.zeros((128 - n, 128), F32)], axis=0).T


def sorted_places(ids):
    hits = [ids == float(c + 1) for c in range(CL_DEV)]
    counted = dot(jnp.concatenate([onehot(h) for h in hits], axis=0), prefix_and_total())
    n = CL_DEV * 16
    below = onehot(
        lax.broadcasted_iota(jnp.int32, (n, n), 1) < lax.broadcasted_iota(jnp.int32, (n, n), 0)
    )
    offsets = dot(below, counted[:, 128:].astype(BF16))
    inside = counted[:, :128] + offsets
    place = jnp.full((16, 128), 4096.0, F32)
    starts = []
    for c in range(CL_DEV):
        place = jnp.where(hits[c], inside[16 * c : 16 * (c + 1)], place)
        starts.append(offsets[16 * c : 16 * c + 1])
    return place, starts


def kernel(
    q_ref, k_ref, v_ref, g_ref, id_ref, owner_ref, old_ref,
    o_ref, dq_ref, dk_ref, dv_ref, cent_ref,
    sbuf, rbuf, smeta, rmeta, xs, acc, res, sbuf2, rbuf2, final,
    fsend, frecv, msend, mrecv, bsend, brecv,
):
    me = lax.axis_index("seq")
    my_plane = me // PLANE
    my_place = lax.rem(me, PLANE)
    scale = 1.0 / math.sqrt(HD)

    barrier = pltpu.get_barrier_semaphore()

    def greet(i, carry):
        pl.semaphore_signal(
            barrier, inc=1, device_id={"seq": lax.rem(me + i, DEVS)}, device_id_type=MESH
        )
        return carry

    lax.fori_loop(1, DEVS, greet, 0)

    def remote(src, dst, send, recv, peer, slot):
        return pltpu.make_async_remote_copy(
            src_ref=src.at[peer], dst_ref=dst.at[slot], send_sem=send.at[peer],
            recv_sem=recv.at[slot], device_id={"seq": peer}, device_id_type=MESH,
        )

    def peer_at(k, j):
        return lax.rem(my_plane + k, PLANES) * PLANE + lax.rem(my_place + j, PLANE)

    def each_peer(k, step):
        def body(j, carry):
            step(peer_at(k, j))
            return carry

        lax.fori_loop(1 if k == 0 else 0, PLANE, body, 0)

    target, local, rank = token_slots(id_ref, owner_ref)
    slot = target * float(ROOM) + rank
    quarter = (lax.rem(me, 4) * ROOM).astype(F32)
    lane_of = onehot(iota((128, TOK), 0) == rank + quarter)
    labels = jnp.where(iota((DEVS, TOK), 0) == target, local + 1.0, 0.0).astype(BF16)
    smeta[...] = dot_nt(labels, lane_of).reshape(DEVS, 1, 128)

    rows = jnp.concatenate([q_ref[...], k_ref[...], v_ref[...], g_ref[...]], axis=1)

    def fill(p, carry):
        pick = onehot(iota((CHUNK, TOK), 0) + (p * CHUNK).astype(F32) == slot)
        block = dot(pick, rows).astype(BF16)
        sbuf[pl.ds(p * PLANE, PLANE)] = block.reshape(PLANE, ROOM, 4 * HD)
        return carry

    lax.fori_loop(0, PLANES, fill, 0)

    pl.semaphore_wait(barrier, DEVS - 1)
    for k in ORDER:
        each_peer(k, lambda d: remote(smeta, rmeta, msend, mrecv, d, me).start())
    for k in ORDER:
        each_peer(k, lambda d: remote(sbuf, rbuf, fsend, frecv, d, me).start())
    rbuf[me] = sbuf[me]
    rmeta[me] = smeta[me]

    acc[...] = jnp.zeros_like(acc)
    xs[pl.ds(0, 128)] = jnp.zeros((128, 4 * HD), BF16)
    for k in ORDER:
        each_peer(k, lambda d: remote(smeta, rmeta, msend, mrecv, d, d).wait_recv())
    ids = jnp.sum(rmeta[...].reshape(16, 4, 128), axis=1)
    place, starts = sorted_places(ids)
    place_cols = turned(place)
    place_ref_rows = place

    for k in ORDER:
        kb = (PLANES - k) % PLANES
        each_peer(kb, lambda d: remote(sbuf, rbuf, fsend, frecv, d, d).wait_recv())
        p = lax.rem(my_plane + kb, PLANES)
        chosen = iota((16, 128), 0)
        halves = []
        for h in range(2):
            row = jnp.sum(
                jnp.where(chosen == (2 * p + h).astype(F32), place_ref_rows, 0.0),
                axis=0, keepdims=True,
            )
            halves.append(iota((TOK, 128), 0) == row)
        pick = onehot(jnp.concatenate(halves, axis=1))
        block = rbuf[pl.ds(p * PLANE, PLANE)].reshape(CHUNK, 4 * HD)
        acc[...] += dot(pick, block)
    xs[pl.ds(128, TOK)] = acc[...].astype(BF16)

    at = iota((BLOCKS, 128), 0) * 128.0 + iota((BLOCKS, 128), 1)
    first = jnp.zeros((BLOCKS, 128), F32)
    for c in range(1, CL_DEV):
        first = jnp.where(at >= starts[c], starts[c], first)
    first_cols = turned(first)

    key_tail, value_tail = None, None
    for b in range(BLOCKS):
        mine = pl.ds(128 * (b + 1), 128)
        window = pl.ds(128 * b, 256)
        query = xs[mine, 0:HD]
        grad = xs[mine, 3 * HD : 4 * HD]
        keys = xs[window, HD : 2 * HD]
        vals = xs[window, 2 * HD : 3 * HD]
        scores = dot_nt(query, keys) * scale
        key_at = iota((128, 256), 1) + 128.0 * (b - 1)
        query_at = iota((128, 256), 0) + 128.0 * b
        allowed = (key_at <= query_at) & (key_at >= first_cols[:, b : b + 1])
        scores = jnp.where(allowed, scores, -1e30)
        weights = jnp.exp(scores - jnp.max(scores, axis=-1, keepdims=True))
        probs = weights / jnp.sum(weights, axis=-1, keepdims=True)
        probs_low = probs.astype(BF16)
        attn = dot(probs_low, vals).astype(BF16)
        delta = jnp.sum(grad.astype(F32) * attn.astype(F32), axis=-1, keepdims=True)
        dprobs = dot_nt(grad, vals)
        dscores = (probs * (dprobs - delta) * scale).astype(BF16)
        res[pl.ds(128 * b, 128), 0:HD] = attn
        res[pl.ds(128 * b, 128), HD : 2 * HD] = dot(dscores, keys).astype(BF16)
        dkeys = dot_tn(dscores, query)
        dvals = dot_tn(probs_low, grad)
        if b > 0:
            before = pl.ds(128 * (b - 1), 128)
            res[before, 2 * HD : 3 * HD] = (key_tail + dkeys[:128]).astype(BF16)
            res[before, 3 * HD : 4 * HD] = (value_tail + dvals[:128]).astype(BF16)
        key_tail, value_tail = dkeys[128:], dvals[128:]
    last = pl.ds(128 * (BLOCKS - 1), 128)
    res[last, 2 * HD : 3 * HD] = key_tail.astype(BF16)
    res[last, 3 * HD : 4 * HD] = value_tail.astype(BF16)

    results = res[...]
    for k in ORDER:
        p = lax.rem(my_plane + k, PLANES)
        chosen = iota((128, 128), 1)
        halves = []
        for h in range(2):
            col = jnp.sum(
                jnp.where(chosen == (2 * p + h).astype(F32), place_cols, 0.0),
                axis=1, keepdims=True,
            )
            halves.append(iota((128, TOK), 1) == col)
        pick = onehot(jnp.concatenate(halves, axis=0))
        block = dot(pick, results).astype(BF16)
        sbuf2[pl.ds(p * PLANE, PLANE)] = block.reshape(PLANE, ROOM, 4 * HD)
        each_peer(k, lambda d: remote(sbuf2, rbuf2, bsend, brecv, d, me).start())
    rbuf2[me] = sbuf2[me]

    start_rows = jnp.concatenate(starts, axis=0)
    end_rows = jnp.concatenate(starts[1:] + [jnp.full((1, 128), float(TOK), F32)], axis=0)
    sums = jnp.zeros((CL_DEV, HD), F32)
    for b in range(BLOCKS):
        row_at = iota((CL_DEV, 128), 1) + 128.0 * b
        owned = onehot((row_at >= start_rows) & (row_at < end_rows))
        sums = sums + dot(owned, xs[pl.ds(128 * (b + 1), 128), HD : 2 * HD])
    blended = 0.5 * old_ref[...] + 0.5 * sums / (end_rows - start_rows)
    power = jnp.mean(blended * blended, axis=-1, keepdims=True)
    cent_ref[...] = blended * lax.rsqrt(power + 1e-6)

    slot_cols = turned(jnp.concatenate([slot[:, 128 * b : 128 * (b + 1)] for b in range(8)], axis=0))
    slot_cols = [slot_cols[:, b : b + 1] for b in range(BLOCKS)]
    final[...] = jnp.zeros_like(final)
    for k in ORDER:
        kb = (PLANES - k) % PLANES
        each_peer(kb, lambda d: remote(sbuf2, rbuf2, bsend, brecv, d, d).wait_recv())
        p = lax.rem(my_plane + kb, PLANES)
        slot_at = iota((128, CHUNK), 1) + (p * CHUNK).astype(F32)
        pick = onehot(jnp.concatenate([slot_at == col for col in slot_cols], axis=0))
        block = rbuf2[pl.ds(p * PLANE, PLANE)].reshape(CHUNK, 4 * HD)
        final[...] += dot(pick, block)
    o_ref[...] = final[:, 0:HD].astype(BF16)
    dq_ref[...] = final[:, HD : 2 * HD].astype(BF16)
    dk_ref[...] = final[:, 2 * HD : 3 * HD].astype(BF16)
    dv_ref[...] = final[:, 3 * HD : 4 * HD].astype(BF16)

    for k in ORDER:
        each_peer(k, lambda d: remote(smeta, rmeta, msend, mrecv, d, me).wait_send())
        each_peer(k, lambda d: remote(sbuf, rbuf, fsend, frecv, d, me).wait_send())
        each_peer(k, lambda d: remote(sbuf2, rbuf2, bsend, brecv, d, me).wait_send())


def shards(queries, key_rows, values, out_grad, cluster_id, cluster_owner, old_centroids):
    vmem = pl.BlockSpec(memory_space=pltpu.VMEM)
    block = (DEVS, ROOM, 4 * HD)
    row_out = jax.ShapeDtypeStruct((TOK, HD), BF16)
    sems = pltpu.SemaphoreType.DMA((DEVS,))
    outs = pl.pallas_call(
        kernel,
        out_shape=(row_out, row_out, row_out, row_out, jax.ShapeDtypeStruct((CL_DEV, HD), F32)),
        in_specs=[vmem] * 7,
        out_specs=(vmem,) * 5,
        scratch_shapes=[
            pltpu.VMEM(block, BF16),
            pltpu.VMEM(block, BF16),
            pltpu.VMEM((DEVS, 1, 128), F32),
            pltpu.VMEM((DEVS, 1, 128), F32),
            pltpu.VMEM((TOK + 128, 4 * HD), BF16),
            pltpu.VMEM((TOK, 4 * HD), F32),
            pltpu.VMEM((TOK, 4 * HD), BF16),
            pltpu.VMEM(block, BF16),
            pltpu.VMEM(block, BF16),
            pltpu.VMEM((TOK, 4 * HD), F32),
            sems, sems, sems, sems, sems, sems,
        ],
        compiler_params=pltpu.CompilerParams(
            collective_id=0, has_side_effects=True, vmem_limit_bytes=56 << 20
        ),
    )(queries, key_rows, values, out_grad, cluster_id, cluster_owner, old_centroids[0])
    return outs[0], outs[1], outs[2], outs[3], outs[4][None]


def solution(mesh):
    return jax.shard_map(
        shards,
        mesh=mesh,
        in_specs=(
            P(("dp", "seq"), None),
            P(("dp", "seq"), None),
            P(("dp", "seq"), None),
            P(("dp", "seq"), None),
            P("dp", "seq"),
            P("dp", None),
            P("dp", "seq", None),
        ),
        out_specs=(
            P(("dp", "seq"), None),
            P(("dp", "seq"), None),
            P(("dp", "seq"), None),
            P(("dp", "seq"), None),
            P("dp", "seq", None),
        ),
        check_vma=False,
    )
```

```python
import functools
import math

import jax
import jax.numpy as jnp
from jax import lax
from jax.experimental import pallas as pl
from jax.experimental.pallas import tpu as pltpu
from jax.sharding import PartitionSpec as P

MESH = pl.DeviceIdType.MESH
HD = 128
CL_DEV = 16
TOK = 1024
DEVS = 64
ROOM = 32
PLANE = 8
PLANES = DEVS // PLANE
CHUNK = PLANE * ROOM
BLOCKS = TOK // 128
ORDER = (4, 1, 7, 3, 5, 2, 6, 0)
BF16 = jnp.bfloat16
F32 = jnp.float32


def dot(a, b):
    return jnp.dot(a, b, preferred_element_type=F32)


def dot_nt(a, b):
    return lax.dot_general(a, b, (((1,), (1,)), ((), ())), preferred_element_type=F32)


def dot_tn(a, b):
    return lax.dot_general(a, b, (((0,), (0,)), ((), ())), preferred_element_type=F32)


def iota(shape, dim):
    return lax.broadcasted_iota(jnp.int32, shape, dim).astype(F32)


def onehot(mask):
    return jnp.where(mask, 1.0, 0.0).astype(BF16)


def prefix_and_total():
    row = lax.broadcasted_iota(jnp.int32, (128, 256), 0)
    col = lax.broadcasted_iota(jnp.int32, (128, 256), 1)
    return onehot((row < col) | (col >= 128))


def token_slots(cluster_id, owner):
    ident = cluster_id[...]
    low = onehot(lax.broadcasted_iota(jnp.int32, (128, TOK), 0) == lax.rem(ident, 128))
    table = jnp.concatenate([owner[:, 128 * b : 128 * (b + 1)] for b in range(8)], axis=0)
    table_dev = lax.div(table, CL_DEV)
    table_loc = table - table_dev * CL_DEV
    tables = jnp.concatenate([table_dev, table_loc], axis=0).astype(F32).astype(BF16)
    found = dot(tables, low)
    high = lax.broadcasted_iota(jnp.int32, (8, TOK), 0) == lax.div(ident, 128)
    target = jnp.sum(jnp.where(high, found[:8], 0.0), axis=0, keepdims=True)
    local = jnp.sum(jnp.where(high, found[8:], 0.0), axis=0, keepdims=True)
    device = iota((DEVS, 128), 0)
    members = [device == target[:, 128 * b : 128 * (b + 1)] for b in range(BLOCKS)]
    counted = dot(jnp.concatenate([onehot(m) for m in members], axis=0), prefix_and_total())
    running = jnp.zeros((DEVS, 128), F32)
    ranks = []
    for b in range(BLOCKS):
        part = counted[DEVS * b : DEVS * (b + 1)]
        ranks.append(
            jnp.sum(jnp.where(members[b], part[:, :128] + running, 0.0), axis=0, keepdims=True)
        )
        running = running + part[:, 128:]
    rank = jnp.concatenate(ranks, axis=1)
    return target, local, rank


def turned(rows):
    n = rows.shape[0]
    return jnp.concatenate([rows, jnp.zeros((128 - n, 128), F32)], axis=0).T


def sorted_places(ids):
    hits = [ids == float(c + 1) for c in range(CL_DEV)]
    counted = dot(jnp.concatenate([onehot(h) for h in hits], axis=0), prefix_and_total())
    n = CL_DEV * 16
    below = onehot(
        lax.broadcasted_iota(jnp.int32, (n, n), 1) < lax.broadcasted_iota(jnp.int32, (n, n), 0)
    )
    offsets = dot(below, counted[:, 128:].astype(BF16))
    inside = counted[:, :128] + offsets
    place = jnp.full((16, 128), 4096.0, F32)
    starts = []
    for c in range(CL_DEV):
        place = jnp.where(hits[c], inside[16 * c : 16 * (c + 1)], place)
        starts.append(offsets[16 * c : 16 * c + 1])
    return place, starts


def plane_rows(place, p):
    at = lax.broadcasted_iota(jnp.int32, (16, 128), 0)
    return [
        jnp.sum(jnp.where(at == 2 * p + h, place, 0.0), axis=0, keepdims=True) for h in range(2)
    ]


def plane_cols(cols, p):
    at = lax.broadcasted_iota(jnp.int32, (128, 128), 1)
    return [jnp.sum(jnp.where(at == 2 * p + h, cols, 0.0), axis=1, keepdims=True) for h in range(2)]


def kernel(
    q_ref, k_ref, v_ref, g_ref, id_ref, owner_ref, old_ref,
    o_ref, dq_ref, dk_ref, dv_ref, cent_ref,
    smeta, rmeta, sqk, rqk, sv, rv, sg, rg, sa, ra, sd, rd,
    gather, ungather, final, xqk, xv, xg, acc, probs_ref, res,
    column_sem, send_sem, meta_sem, qk_sem, v_sem, g_sem, a_sem, d_sem,
):
    me = lax.axis_index("seq")
    my_plane = me // PLANE
    my_place = lax.rem(me, PLANE)
    scale = 1.0 / math.sqrt(HD)

    def peer_at(k, j):
        return lax.rem(my_plane + k, PLANES) * PLANE + lax.rem(my_place + j, PLANE)

    def signal(sem, k, j):
        pl.semaphore_signal(
            sem, inc=1, device_id={"seq": peer_at(k, j)}, device_id_type=MESH
        )

    barrier = pltpu.get_barrier_semaphore()
    for k in ORDER[:-1]:
        signal(barrier, k, 0)
    for j in range(1, PLANE):
        signal(barrier, 0, j)

    kinds = {
        "meta": (0, smeta, rmeta, meta_sem),
        "qk": (1, sqk, rqk, qk_sem),
        "v": (2, sv, rv, v_sem),
        "g": (3, sg, rg, g_sem),
        "a": (4, sa, ra, a_sem),
        "d": (5, sd, rd, d_sem),
    }

    def start(kind, k, first, last):
        index, src, dst, sem = kinds[kind]

        def body(j, carry):
            peer = peer_at(k, j)
            pltpu.make_async_remote_copy(
                src_ref=src.at[peer], dst_ref=dst.at[me], send_sem=send_sem.at[index],
                recv_sem=sem.at[my_plane], device_id={"seq": peer}, device_id_type=MESH,
            ).start()
            return carry

        lax.fori_loop(first, last, body, 0)

    def start_plane(kind, k):
        start(kind, k, 1 if k == 0 else 0, PLANE)

    def arrived(kind, k):
        _, _, dst, sem = kinds[kind]
        p = lax.rem(my_plane + k, PLANES)
        some = dst.at[pl.ds(p * PLANE, PLANE - 1 if k == 0 else PLANE)]
        pltpu.make_async_copy(some, some, sem.at[p]).wait()
        return p

    def sent(kind):
        index, src, _, _ = kinds[kind]
        some = src.at[pl.ds(0, DEVS - 1)]
        pltpu.make_async_copy(some, some, send_sem.at[index]).wait()

    def keep_own(kind):
        _, src, dst, _ = kinds[kind]
        dst[me] = src[me]

    def plane_of(ref, p):
        block = ref[pl.ds(p * PLANE, PLANE)]
        return block.reshape(CHUNK, block.shape[-1])

    def put_plane(ref, p, value):
        ref[pl.ds(p * PLANE, PLANE)] = value.astype(BF16).reshape(PLANE, ROOM, value.shape[-1])

    target, local, rank = token_slots(id_ref, owner_ref)
    slot = target * float(ROOM) + rank
    rows = jnp.concatenate([q_ref[...], k_ref[...], v_ref[...], g_ref[...]], axis=1)

    def fill(p, carry):
        pick = onehot(iota((CHUNK, TOK), 0) + (p * CHUNK).astype(F32) == slot)
        block = dot(pick, rows)
        put_plane(sqk, p, block[:, : 2 * HD])
        put_plane(sv, p, block[:, 2 * HD : 3 * HD])
        put_plane(sg, p, block[:, 3 * HD :])
        return carry

    lax.fori_loop(0, PLANES, fill, 0)

    quarter = (lax.rem(me, 4) * ROOM).astype(F32)
    lane_of = onehot(iota((128, TOK), 0) == rank + quarter)
    labels = jnp.where(iota((DEVS, TOK), 0) == target, local + 1.0, 0.0).astype(BF16)
    smeta[...] = dot_nt(labels, lane_of).reshape(DEVS, 1, 128)

    pl.semaphore_wait(barrier, 2 * PLANE - 2)
    for k in ORDER[:-1]:
        signal(column_sem, k, 0)
    for k in ORDER[:-1]:
        start("qk", k, 0, 1)
    pl.semaphore_wait(column_sem, PLANE - 1)
    for k in ORDER:
        start("qk", k, 1, PLANE)
    for kind in ("meta", "v", "g"):
        for k in ORDER:
            start_plane(kind, k)
    for kind in ("meta", "qk", "v", "g"):
        keep_own(kind)

    slot_cols = turned(jnp.concatenate([slot[:, 128 * b : 128 * (b + 1)] for b in range(8)], axis=0))
    slot_cols = [slot_cols[:, b : b + 1] for b in range(BLOCKS)]

    def build_final(p, carry):
        slot_at = iota((128, CHUNK), 1) + (p * CHUNK).astype(F32)
        final[p] = onehot(jnp.concatenate([slot_at == col for col in slot_cols], axis=0))
        return carry

    lax.fori_loop(0, PLANES, build_final, 0)

    for k in ORDER:
        arrived("meta", (PLANES - k) % PLANES)
    ids = jnp.sum(rmeta[...].reshape(16, 4, 128), axis=1)
    place, starts = sorted_places(ids)
    place_cols = turned(place)

    def build(p, carry):
        rows_of = plane_rows(place, p)
        gather[p] = onehot(jnp.concatenate([iota((TOK, 128), 0) == r for r in rows_of], axis=1))
        cols_of = plane_cols(place_cols, p)
        ungather[p] = onehot(jnp.concatenate([iota((128, TOK), 1) == c for c in cols_of], axis=0))
        return carry

    lax.fori_loop(0, PLANES, build, 0)

    at = iota((BLOCKS, 128), 0) * 128.0 + iota((BLOCKS, 128), 1)
    first = jnp.zeros((BLOCKS, 128), F32)
    for c in range(1, CL_DEV):
        first = jnp.where(at >= starts[c], starts[c], first)
    first_cols = turned(first)

    def collect(kind, matrix):
        _, _, dst, _ = kinds[kind]
        width = dst.shape[-1]
        for i, k in enumerate(ORDER):
            p = arrived(kind, (PLANES - k) % PLANES)
            part = dot(matrix[p], plane_of(dst, p))
            if i == PLANES - 1:
                return acc[:, :width] + part
            acc[:, :width] = part if i == 0 else acc[:, :width] + part

    front = pl.ds(0, 128)
    body = pl.ds(128, TOK)
    xqk[front] = jnp.zeros((128, 2 * HD), BF16)
    xv[front] = jnp.zeros((128, HD), BF16)

    xqk[body] = collect("qk", gather).astype(BF16)
    for b in range(BLOCKS):
        query = xqk[pl.ds(128 * (b + 1), 128), :HD]
        keys = xqk[pl.ds(128 * b, 256), HD:]
        scores = dot_nt(query, keys) * scale
        key_at = iota((128, 256), 1) + 128.0 * (b - 1)
        query_at = iota((128, 256), 0) + 128.0 * b
        allowed = (key_at <= query_at) & (key_at >= first_cols[:, b : b + 1])
        scores = jnp.where(allowed, scores, -1e30)
        weights = jnp.exp(scores - jnp.max(scores, axis=-1, keepdims=True))
        probs_ref[b] = weights / jnp.sum(weights, axis=-1, keepdims=True)

    start_rows = jnp.concatenate(starts, axis=0)
    end_rows = jnp.concatenate(starts[1:] + [jnp.full((1, 128), float(TOK), F32)], axis=0)
    sums = jnp.zeros((CL_DEV, HD), F32)
    for b in range(BLOCKS):
        row_at = iota((CL_DEV, 128), 1) + 128.0 * b
        owned = onehot((row_at >= start_rows) & (row_at < end_rows))
        sums = sums + dot(owned, xqk[pl.ds(128 * (b + 1), 128), HD:])
    blended = 0.5 * old_ref[...] + 0.5 * sums / (end_rows - start_rows)
    power = jnp.mean(blended * blended, axis=-1, keepdims=True)
    cent_ref[...] = blended * lax.rsqrt(power + 1e-6)

    xv[body] = collect("v", gather).astype(BF16)
    attn = [
        dot(probs_ref[b].astype(BF16), xv[pl.ds(128 * b, 256)]).astype(BF16) for b in range(BLOCKS)
    ]
    outs = jnp.concatenate(attn, axis=0)
    res[:, :HD] = outs
    for k in ORDER:
        p = lax.rem(my_plane + k, PLANES)
        put_plane(sa, p, dot(ungather[p], outs))
        start_plane("a", k)
    keep_own("a")

    xg[...] = collect("g", gather).astype(BF16)
    key_tail, value_tail = None, None
    for b in range(BLOCKS):
        mine = pl.ds(128 * b, 128)
        window = pl.ds(128 * b, 256)
        query = xqk[pl.ds(128 * (b + 1), 128), :HD]
        keys = xqk[window, HD:]
        grad = xg[mine]
        probs = probs_ref[b]
        delta = jnp.sum(
            grad.astype(F32) * res[mine, :HD].astype(F32), axis=-1, keepdims=True
        )
        dprobs = dot_nt(grad, xv[window])
        dscores = (probs * (dprobs - delta) * scale).astype(BF16)
        res[mine, HD : 2 * HD] = dot(dscores, keys).astype(BF16)
        dkeys = dot_tn(dscores, query)
        dvals = dot_tn(probs.astype(BF16), grad)
        if b > 0:
            before = pl.ds(128 * (b - 1), 128)
            res[before, 2 * HD : 3 * HD] = (key_tail + dkeys[:128]).astype(BF16)
            res[before, 3 * HD :] = (value_tail + dvals[:128]).astype(BF16)
        key_tail, value_tail = dkeys[128:], dvals[128:]
    last = pl.ds(128 * (BLOCKS - 1), 128)
    res[last, 2 * HD : 3 * HD] = key_tail.astype(BF16)
    res[last, 3 * HD :] = value_tail.astype(BF16)

    grads = res[:, HD:]
    for k in ORDER:
        p = lax.rem(my_plane + k, PLANES)
        put_plane(sd, p, dot(ungather[p], grads))
        start_plane("d", k)
    keep_own("d")
    for kind in ("meta", "qk", "v", "g"):
        sent(kind)

    o_ref[...] = collect("a", final).astype(BF16)
    sent("a")
    found = collect("d", final).astype(BF16)
    dq_ref[...] = found[:, :HD]
    dk_ref[...] = found[:, HD : 2 * HD]
    dv_ref[...] = found[:, 2 * HD :]
    sent("d")


def hand_over(*refs):
    n = len(refs) // 2
    for src, dst in zip(refs[:n], refs[n:]):
        dst[...] = src[...]


def shards(queries, key_rows, values, out_grad, cluster_id, cluster_owner, old_centroids):
    vmem = pl.BlockSpec(memory_space=pltpu.VMEM)
    anywhere = pl.BlockSpec(memory_space=pl.ANY)
    row_out = jax.ShapeDtypeStruct((TOK, HD), BF16)
    out_shape = (row_out, row_out, row_out, row_out, jax.ShapeDtypeStruct((CL_DEV, HD), F32))

    def pair(width):
        return [pltpu.VMEM((DEVS, ROOM, width), BF16)] * 2

    by_plane = pltpu.SemaphoreType.DMA((PLANES,))
    outs = pl.pallas_call(
        kernel,
        out_shape=out_shape,
        in_specs=[vmem] * 7,
        out_specs=(vmem,) * 5,
        scratch_shapes=[
            pltpu.VMEM((DEVS, 1, 128), F32),
            pltpu.VMEM((DEVS, 1, 128), F32),
            *pair(2 * HD), *pair(HD), *pair(HD), *pair(HD), *pair(3 * HD),
            pltpu.VMEM((PLANES, TOK, CHUNK), BF16),
            pltpu.VMEM((PLANES, CHUNK, TOK), BF16),
            pltpu.VMEM((PLANES, TOK, CHUNK), BF16),
            pltpu.VMEM((TOK + 128, 2 * HD), BF16),
            pltpu.VMEM((TOK + 128, HD), BF16),
            pltpu.VMEM((TOK, HD), BF16),
            pltpu.VMEM((TOK, 3 * HD), F32),
            pltpu.VMEM((BLOCKS, 128, 256), F32),
            pltpu.VMEM((TOK, 4 * HD), BF16),
            pltpu.SemaphoreType.REGULAR,
            pltpu.SemaphoreType.DMA((6,)),
            by_plane, by_plane, by_plane, by_plane, by_plane, by_plane,
        ],
        compiler_params=pltpu.CompilerParams(
            collective_id=0, has_side_effects=True, vmem_limit_bytes=56 << 20
        ),
    )(queries, key_rows, values, out_grad, cluster_id, cluster_owner, old_centroids[0])
    outs = pl.pallas_call(
        hand_over,
        out_shape=out_shape,
        in_specs=[vmem] * 5,
        out_specs=(vmem,) * 5,
    )(*outs)
    return outs[0], outs[1], outs[2], outs[3], outs[4][None]


def solution(mesh):
    return jax.shard_map(
        shards,
        mesh=mesh,
        in_specs=(
            P(("dp", "seq"), None),
            P(("dp", "seq"), None),
            P(("dp", "seq"), None),
            P(("dp", "seq"), None),
            P("dp", "seq"),
            P("dp", None),
            P("dp", "seq", None),
        ),
        out_specs=(
            P(("dp", "seq"), None),
            P(("dp", "seq"), None),
            P(("dp", "seq"), None),
            P(("dp", "seq"), None),
            P("dp", "seq", None),
        ),
        check_vma=False,
    )
```

```python
import functools
import math

import jax
import jax.numpy as jnp
from jax import lax
from jax.experimental import pallas as pl
from jax.experimental.pallas import tpu as pltpu
from jax.sharding import PartitionSpec as P

MESH = pl.DeviceIdType.MESH
HD = 128
CL_DEV = 16
TOK = 1024
DEVS = 64
ROOM = 32
PLANE = 8
PLANES = DEVS // PLANE
CHUNK = PLANE * ROOM
BLOCKS = TOK // 128
ORDER = (4, 1, 7, 3, 5, 2, 6, 0)
SEATS = 24
EXTRA = 16
PARTS = 4
BF16 = jnp.bfloat16
F32 = jnp.float32


def dot(a, b):
    return jnp.dot(a, b, preferred_element_type=F32)


def dot_nt(a, b):
    return lax.dot_general(a, b, (((1,), (1,)), ((), ())), preferred_element_type=F32)


def dot_tn(a, b):
    return lax.dot_general(a, b, (((0,), (0,)), ((), ())), preferred_element_type=F32)


def iota(shape, dim):
    return lax.broadcasted_iota(jnp.int32, shape, dim).astype(F32)


def onehot(mask):
    return jnp.where(mask, 1.0, 0.0).astype(BF16)


def prefix_and_total():
    row = lax.broadcasted_iota(jnp.int32, (128, 256), 0)
    col = lax.broadcasted_iota(jnp.int32, (128, 256), 1)
    return onehot((row < col) | (col >= 128))


def token_slots(cluster_id, owner):
    ident = cluster_id[...]
    low = onehot(lax.broadcasted_iota(jnp.int32, (128, TOK), 0) == lax.rem(ident, 128))
    table = jnp.concatenate([owner[:, 128 * b : 128 * (b + 1)] for b in range(8)], axis=0)
    table_dev = lax.div(table, CL_DEV)
    table_loc = table - table_dev * CL_DEV
    tables = jnp.concatenate([table_dev, table_loc], axis=0).astype(F32).astype(BF16)
    found = dot(tables, low)
    high = lax.broadcasted_iota(jnp.int32, (8, TOK), 0) == lax.div(ident, 128)
    target = jnp.sum(jnp.where(high, found[:8], 0.0), axis=0, keepdims=True)
    local = jnp.sum(jnp.where(high, found[8:], 0.0), axis=0, keepdims=True)
    device = iota((DEVS, 128), 0)
    members = [device == target[:, 128 * b : 128 * (b + 1)] for b in range(BLOCKS)]
    counted = dot(jnp.concatenate([onehot(m) for m in members], axis=0), prefix_and_total())
    running = jnp.zeros((DEVS, 128), F32)
    ranks = []
    for b in range(BLOCKS):
        part = counted[DEVS * b : DEVS * (b + 1)]
        ranks.append(
            jnp.sum(jnp.where(members[b], part[:, :128] + running, 0.0), axis=0, keepdims=True)
        )
        running = running + part[:, 128:]
    rank = jnp.concatenate(ranks, axis=1)
    return target, local, rank


def turned(rows):
    n = rows.shape[0]
    return jnp.concatenate([rows, jnp.zeros((128 - n, 128), F32)], axis=0).T


def sorted_places(ids):
    hits = [ids == float(c + 1) for c in range(CL_DEV)]
    counted = dot(jnp.concatenate([onehot(h) for h in hits], axis=0), prefix_and_total())
    n = CL_DEV * 16
    below = onehot(
        lax.broadcasted_iota(jnp.int32, (n, n), 1) < lax.broadcasted_iota(jnp.int32, (n, n), 0)
    )
    offsets = dot(below, counted[:, 128:].astype(BF16))
    inside = counted[:, :128] + offsets
    place = jnp.full((16, 128), 4096.0, F32)
    starts = []
    for c in range(CL_DEV):
        place = jnp.where(hits[c], inside[16 * c : 16 * (c + 1)], place)
        starts.append(offsets[16 * c : 16 * c + 1])
    return place, starts


def plane_rows(place, p):
    at = lax.broadcasted_iota(jnp.int32, (16, 128), 0)
    return [
        jnp.sum(jnp.where(at == 2 * p + h, place, 0.0), axis=0, keepdims=True) for h in range(2)
    ]


def plane_cols(cols, p):
    at = lax.broadcasted_iota(jnp.int32, (128, 128), 1)
    return [jnp.sum(jnp.where(at == 2 * p + h, cols, 0.0), axis=1, keepdims=True) for h in range(2)]


def kernel(
    q_ref, k_ref, v_ref, g_ref, id_ref, owner_ref, old_ref,
    o_ref, dq_ref, dk_ref, dv_ref, cent_ref,
    smeta, rmeta, sqk, rqk, sv, rv, sg, rg, sa, ra, sd, rd,
    gather, ungather, final, xqk, xv, xg, acc, probs_ref, res,
    column_sem, send_sem, meta_sem, qk_sem, v_sem, g_sem, a_sem, d_sem,
):
    me = lax.axis_index("seq")
    my_plane = me // PLANE
    my_place = lax.rem(me, PLANE)
    scale = 1.0 / math.sqrt(HD)

    def peer_at(k, j):
        return lax.rem(my_plane + k, PLANES) * PLANE + lax.rem(my_place + j, PLANE)

    def signal(sem, k, j):
        pl.semaphore_signal(
            sem, inc=1, device_id={"seq": peer_at(k, j)}, device_id_type=MESH
        )

    barrier = pltpu.get_barrier_semaphore()
    for k in ORDER[:-1]:
        signal(barrier, k, 0)
    for j in range(1, PLANE):
        signal(barrier, 0, j)

    kinds = {
        "meta": (0, smeta, rmeta, meta_sem),
        "qk": (1, sqk, rqk, qk_sem),
        "v": (2, sv, rv, v_sem),
        "g": (3, sg, rg, g_sem),
        "a": (4, sa, ra, a_sem),
        "d": (5, sd, rd, d_sem),
    }

    def start(kind, k, first, last):
        index, src, dst, sem = kinds[kind]

        def body(j, carry):
            peer = peer_at(k, j)
            pltpu.make_async_remote_copy(
                src_ref=src.at[peer], dst_ref=dst.at[me], send_sem=send_sem.at[index],
                recv_sem=sem.at[my_plane], device_id={"seq": peer}, device_id_type=MESH,
            ).start()
            return carry

        lax.fori_loop(first, last, body, 0)

    def start_plane(kind, k):
        start(kind, k, 1 if k == 0 else 0, PLANE)

    def arrived(kind, k):
        _, _, dst, sem = kinds[kind]
        p = lax.rem(my_plane + k, PLANES)
        some = dst.at[pl.ds(p * PLANE, PLANE - 1 if k == 0 else PLANE)]
        pltpu.make_async_copy(some, some, sem.at[p]).wait()
        return p

    def sent(kind):
        index, src, _, _ = kinds[kind]
        some = src.at[pl.ds(0, DEVS - 1)]
        pltpu.make_async_copy(some, some, send_sem.at[index]).wait()

    def keep_own(kind):
        _, src, dst, _ = kinds[kind]
        dst[me] = src[me]

    def plane_of(ref, p):
        block = ref[pl.ds(p * PLANE, PLANE)]
        return block.reshape(CHUNK, block.shape[-1])

    def put_plane(ref, p, value):
        ref[pl.ds(p * PLANE, PLANE)] = value.astype(BF16).reshape(PLANE, ROOM, value.shape[-1])

    target, local, rank = token_slots(id_ref, owner_ref)
    slot = target * float(ROOM) + rank
    rows = jnp.concatenate([q_ref[...], k_ref[...], v_ref[...], g_ref[...]], axis=1)

    def fill(p, carry):
        pick = onehot(iota((CHUNK, TOK), 0) + (p * CHUNK).astype(F32) == slot)
        block = dot(pick, rows)
        put_plane(sqk, p, block[:, : 2 * HD])
        put_plane(sv, p, block[:, 2 * HD : 3 * HD])
        put_plane(sg, p, block[:, 3 * HD :])
        return carry

    lax.fori_loop(0, PLANES, fill, 0)

    quarter = (lax.rem(me, 4) * ROOM).astype(F32)
    lane_of = onehot(iota((128, TOK), 0) == rank + quarter)
    labels = jnp.where(iota((DEVS, TOK), 0) == target, local + 1.0, 0.0).astype(BF16)
    smeta[...] = dot_nt(labels, lane_of).reshape(DEVS, 1, 128)

    pl.semaphore_wait(barrier, 2 * PLANE - 2)
    for k in ORDER[:-1]:
        signal(column_sem, k, 0)
    for k in ORDER[:-1]:
        start("qk", k, 0, 1)
    pl.semaphore_wait(column_sem, PLANE - 1)
    for k in ORDER:
        start("qk", k, 1, PLANE)
    for kind in ("meta", "v", "g"):
        for k in ORDER:
            start_plane(kind, k)
    for kind in ("meta", "qk", "v", "g"):
        keep_own(kind)

    slot_cols = turned(jnp.concatenate([slot[:, 128 * b : 128 * (b + 1)] for b in range(8)], axis=0))
    slot_cols = [slot_cols[:, b : b + 1] for b in range(BLOCKS)]

    def build_final(p, carry):
        slot_at = iota((128, CHUNK), 1) + (p * CHUNK).astype(F32)
        final[p] = onehot(jnp.concatenate([slot_at == col for col in slot_cols], axis=0))
        return carry

    lax.fori_loop(0, PLANES, build_final, 0)

    for k in ORDER:
        arrived("meta", (PLANES - k) % PLANES)
    ids = jnp.sum(rmeta[...].reshape(16, 4, 128), axis=1)
    place, starts = sorted_places(ids)
    place_cols = turned(place)

    def build(p, carry):
        rows_of = plane_rows(place, p)
        gather[p] = onehot(jnp.concatenate([iota((TOK, 128), 0) == r for r in rows_of], axis=1))
        cols_of = plane_cols(place_cols, p)
        ungather[p] = onehot(jnp.concatenate([iota((128, TOK), 1) == c for c in cols_of], axis=0))
        return carry

    lax.fori_loop(0, PLANES, build, 0)

    at = iota((BLOCKS, 128), 0) * 128.0 + iota((BLOCKS, 128), 1)
    first = jnp.zeros((BLOCKS, 128), F32)
    for c in range(1, CL_DEV):
        first = jnp.where(at >= starts[c], starts[c], first)
    first_cols = turned(first)

    def collect(kind, matrix):
        _, _, dst, _ = kinds[kind]
        width = dst.shape[-1]
        for i, k in enumerate(ORDER):
            p = arrived(kind, (PLANES - k) % PLANES)
            part = dot(matrix[p], plane_of(dst, p))
            if i == PLANES - 1:
                return acc[:, :width] + part
            acc[:, :width] = part if i == 0 else acc[:, :width] + part

    front = pl.ds(0, 128)
    body = pl.ds(128, TOK)
    xqk[front] = jnp.zeros((128, 2 * HD), BF16)
    xv[front] = jnp.zeros((128, HD), BF16)

    xqk[body] = collect("qk", gather).astype(BF16)
    for b in range(BLOCKS):
        query = xqk[pl.ds(128 * (b + 1), 128), :HD]
        keys = xqk[pl.ds(128 * b, 256), HD:]
        scores = dot_nt(query, keys) * scale
        key_at = iota((128, 256), 1) + 128.0 * (b - 1)
        query_at = iota((128, 256), 0) + 128.0 * b
        allowed = (key_at <= query_at) & (key_at >= first_cols[:, b : b + 1])
        scores = jnp.where(allowed, scores, -1e30)
        weights = jnp.exp(scores - jnp.max(scores, axis=-1, keepdims=True))
        probs_ref[b] = weights / jnp.sum(weights, axis=-1, keepdims=True)

    start_rows = jnp.concatenate(starts, axis=0)
    end_rows = jnp.concatenate(starts[1:] + [jnp.full((1, 128), float(TOK), F32)], axis=0)
    sums = jnp.zeros((CL_DEV, HD), F32)
    for b in range(BLOCKS):
        row_at = iota((CL_DEV, 128), 1) + 128.0 * b
        owned = onehot((row_at >= start_rows) & (row_at < end_rows))
        sums = sums + dot(owned, xqk[pl.ds(128 * (b + 1), 128), HD:])
    blended = 0.5 * old_ref[...] + 0.5 * sums / (end_rows - start_rows)
    power = jnp.mean(blended * blended, axis=-1, keepdims=True)
    cent_ref[...] = blended * lax.rsqrt(power + 1e-6)

    xv[body] = collect("v", gather).astype(BF16)
    attn = [
        dot(probs_ref[b].astype(BF16), xv[pl.ds(128 * b, 256)]).astype(BF16) for b in range(BLOCKS)
    ]
    outs = jnp.concatenate(attn, axis=0)
    res[:, :HD] = outs
    for k in ORDER:
        p = lax.rem(my_plane + k, PLANES)
        put_plane(sa, p, dot(ungather[p], outs))
        start_plane("a", k)
    keep_own("a")

    xg[...] = collect("g", gather).astype(BF16)
    key_tail, value_tail = None, None
    for b in range(BLOCKS):
        mine = pl.ds(128 * b, 128)
        window = pl.ds(128 * b, 256)
        query = xqk[pl.ds(128 * (b + 1), 128), :HD]
        keys = xqk[window, HD:]
        grad = xg[mine]
        probs = probs_ref[b]
        delta = jnp.sum(
            grad.astype(F32) * res[mine, :HD].astype(F32), axis=-1, keepdims=True
        )
        dprobs = dot_nt(grad, xv[window])
        dscores = (probs * (dprobs - delta) * scale).astype(BF16)
        res[mine, HD : 2 * HD] = dot(dscores, keys).astype(BF16)
        dkeys = dot_tn(dscores, query)
        dvals = dot_tn(probs.astype(BF16), grad)
        if b > 0:
            before = pl.ds(128 * (b - 1), 128)
            res[before, 2 * HD : 3 * HD] = (key_tail + dkeys[:128]).astype(BF16)
            res[before, 3 * HD :] = (value_tail + dvals[:128]).astype(BF16)
        key_tail, value_tail = dkeys[128:], dvals[128:]
    last = pl.ds(128 * (BLOCKS - 1), 128)
    res[last, 2 * HD : 3 * HD] = key_tail.astype(BF16)
    res[last, 3 * HD :] = value_tail.astype(BF16)

    grads = res[:, HD:]
    for k in ORDER:
        p = lax.rem(my_plane + k, PLANES)
        put_plane(sd, p, dot(ungather[p], grads))
        start_plane("d", k)
    keep_own("d")
    for kind in ("meta", "qk", "v", "g"):
        sent(kind)

    o_ref[...] = collect("a", final).astype(BF16)
    sent("a")
    found = collect("d", final).astype(BF16)
    dq_ref[...] = found[:, :HD]
    dk_ref[...] = found[:, HD : 2 * HD]
    dv_ref[...] = found[:, 2 * HD :]
    sent("d")


def seated_rank(seats, member):
    n = seats
    counted = dot(jnp.concatenate([onehot(m) for m in member], axis=0), prefix_and_total())
    running = jnp.zeros((n, 128), F32)
    ranks = []
    for b in range(BLOCKS):
        part = counted[n * b : n * (b + 1)]
        ranks.append(
            jnp.sum(jnp.where(member[b], part[:, :128] + running, 0.0), axis=0, keepdims=True)
        )
        running = running + part[:, 128:]
    return jnp.concatenate(ranks, axis=1)


def split_features(block, rows):
    f = block.shape[1] // HD
    return [block[:, HD * j : HD * (j + 1)].reshape(-1, rows, HD) for j in range(f)]


def kernel_fast(
    q_ref, k_ref, v_ref, g_ref, id_ref, owner_ref, old_ref,
    o_ref, dq_ref, dk_ref, dv_ref, cent_ref, flag_ref,
    smeta, rmeta, smx, rmx, sx, rx, sbuf, rbuf, sa, ra, sd, rd, sy, ry, sw, rw, sflag, rflag,
    gather, ungather, final, xgather, xungather, wide, xqk, xv, xg, acc, probs_ref, res,
    column_sem, send_sem, meta_sem, qk_sem, v_sem, g_sem, a_sem, d_sem, one_sem,
):
    me = lax.axis_index("seq")
    my_part = lax.axis_index("dp")
    my_plane = me // PLANE
    my_place = lax.rem(me, PLANE)
    scale = 1.0 / math.sqrt(HD)
    UNIT = 65536.0
    NONE = 8388608.0

    def peer_at(k, j):
        return lax.rem(my_plane + k, PLANES) * PLANE + lax.rem(my_place + j, PLANE)

    def part_at(i):
        return lax.rem(my_part + i, PARTS)

    def signal(sem, k, j):
        pl.semaphore_signal(sem, inc=1, device_id={"seq": peer_at(k, j)}, device_id_type=MESH)

    barrier = pltpu.get_barrier_semaphore()
    for k in ORDER[:-1]:
        signal(barrier, k, 0)
    for j in range(1, PLANE):
        signal(barrier, 0, j)
    for i in range(1, PARTS):
        pl.semaphore_signal(barrier, inc=1, device_id={"dp": part_at(i)}, device_id_type=MESH)

    kinds = {
        "meta": (0, smeta, rmeta, meta_sem, 0, 1),
        "qk": (1, sbuf, rbuf, qk_sem, 0, 2 * SEATS),
        "v": (2, sbuf, rbuf, v_sem, 2 * SEATS, 32),
        "g": (3, sbuf, rbuf, g_sem, 2 * SEATS + 32, 16),
        "a": (4, sa, ra, a_sem, 0, 16),
        "d": (5, sd, rd, d_sem, 0, 4 * SEATS - 16),
    }

    def start(kind, k, first, last):
        index, src, dst, sem, low, count = kinds[kind]
        some = pl.ds(low, count)

        def body(j, carry):
            peer = peer_at(k, j)
            pltpu.make_async_remote_copy(
                src_ref=src.at[peer, some], dst_ref=dst.at[me, some],
                send_sem=send_sem.at[index], recv_sem=sem.at[my_plane],
                device_id={"seq": peer}, device_id_type=MESH,
            ).start()
            return carry

        lax.fori_loop(first, last, body, 0)

    def start_plane(kind, k):
        start(kind, k, 1 if k == 0 else 0, PLANE)

    def arrived(kind, k):
        _, _, dst, sem, low, count = kinds[kind]
        p = lax.rem(my_plane + k, PLANES)
        some = dst.at[pl.ds(p * PLANE, PLANE - 1 if k == 0 else PLANE), pl.ds(low, count)]
        pltpu.make_async_copy(some, some, sem.at[p]).wait()
        return p

    def sent(kind):
        index, src, _, _, low, count = kinds[kind]
        some = src.at[pl.ds(0, DEVS - 1), pl.ds(low, count)]
        pltpu.make_async_copy(some, some, send_sem.at[index]).wait()

    ones = {
        "x": (6, sx, rx.at[my_place], 0),
        "mx": (7, smx, rmx.at[my_place], 1),
        "fx": (8, rx, rx, 2),
        "fm": (9, rmx, rmx, 3),
        "y": (10, sy, ry, 4),
        "w": (11, sw, rw, 5),
        "flag": (12, sflag, rflag, 6),
    }

    def column(kind):
        index, src, dst, sem = ones[kind]
        for k in ORDER[:-1]:
            p = lax.rem(my_plane + k, PLANES)
            pltpu.make_async_remote_copy(
                src_ref=src.at[p], dst_ref=dst.at[my_plane], send_sem=send_sem.at[index],
                recv_sem=one_sem.at[sem], device_id={"seq": peer_at(k, 0)}, device_id_type=MESH,
            ).start()

    def across(kind, forward, first=0, last=PLANES):
        index, src, dst, sem = ones[kind]
        some = pl.ds(first, last - first)
        for j in range(1, PLANE):
            seat = lax.rem(my_place + j, PLANE)
            pltpu.make_async_remote_copy(
                src_ref=src.at[my_place if forward else seat, some],
                dst_ref=dst.at[my_place, some],
                send_sem=send_sem.at[index], recv_sem=one_sem.at[sem],
                device_id={"seq": peer_at(0, j)}, device_id_type=MESH,
            ).start()

    def one_wait(kind, n, sending):
        index, src, dst, sem = ones[kind]
        some = (src if sending else dst).at[pl.ds(0, n)]
        pltpu.make_async_copy(
            some, some, send_sem.at[index] if sending else one_sem.at[sem]
        ).wait()

    target, local, rank = token_slots(id_ref, owner_ref)
    plane_row = jnp.floor(target * (1.0 / PLANE))
    seat_row = target - plane_row * float(PLANE)
    direct = rank < float(SEATS)
    slot = jnp.where(direct, target * float(SEATS) + rank, -1.0)
    member = [
        (iota((PLANES, 128), 0) == plane_row[:, 128 * b : 128 * (b + 1)])
        & (rank[:, 128 * b : 128 * (b + 1)] >= float(SEATS))
        for b in range(BLOCKS)
    ]
    extra = seated_rank(PLANES, member)
    fits = (rank >= float(SEATS)) & (extra < float(EXTRA))
    xslot = jnp.where(fits, plane_row * float(EXTRA) + extra, -1.0)
    lost = jnp.max(jnp.where(extra >= float(EXTRA), 1.0, 0.0), axis=1, keepdims=True)

    rows = jnp.concatenate([q_ref[...], k_ref[...], v_ref[...], g_ref[...]], axis=1)
    block = dot(onehot(iota((PLANES * EXTRA, TOK), 0) == xslot), rows)
    sx[...] = jnp.concatenate(split_features(block, EXTRA), axis=1).astype(BF16)

    def fill(p, carry):
        pick = onehot(iota((PLANE * SEATS, TOK), 0) + (p * PLANE * SEATS).astype(F32) == slot)
        parts = split_features(dot(pick, rows), SEATS)
        sbuf[pl.ds(p * PLANE, PLANE)] = jnp.concatenate(parts, axis=1).astype(BF16)
        return carry

    lax.fori_loop(0, PLANES, fill, 0)

    when = iota((1, TOK), 1)
    when_high = jnp.floor(when * (1.0 / 32))
    when_low = when - 32.0 * when_high
    here = (me * TOK).astype(F32)

    def keys_of(rows_at, label, lanes_at):
        n = rows_at.shape[0]
        stack = [jnp.where(rows_at, r, 0.0) for r in (label, when_high, when_low)]
        found = dot_nt(jnp.concatenate(stack, axis=0).astype(BF16), onehot(lanes_at))
        label = found[:n]
        key = label * UNIT + 32.0 * found[n : 2 * n] + found[2 * n :]
        return key + jnp.where(label > 0.0, here, 0.0)

    lane = jnp.where(direct, rank + (my_place * SEATS).astype(F32), -1.0)
    key = keys_of(iota((DEVS, TOK), 0) == target, local + 1.0, iota((256, TOK), 0) == lane)
    key = jnp.where(iota((DEVS, 256), 1) == 255.0, lost, key)
    smeta[...] = key.reshape(DEVS, 1, 256)
    lane = jnp.where(fits, extra + (my_plane * EXTRA).astype(F32), -1.0)
    label = local + 1.0 + seat_row * float(CL_DEV)
    key = keys_of(iota((PLANES, TOK), 0) == plane_row, label, iota((128, TOK), 0) == lane)
    smx[...] = key.reshape(PLANES, 1, 128)

    pl.semaphore_wait(barrier, 2 * PLANE - 2 + PARTS - 1)
    for k in ORDER[:-1]:
        signal(column_sem, k, 0)
    column("x")
    column("mx")
    rx[my_place, my_plane] = sx[my_plane]
    rmx[my_place, my_plane] = smx[my_plane]
    for k in ORDER[:-1]:
        start("qk", k, 0, 1)
    pl.semaphore_wait(column_sem, PLANE - 1)
    for k in ORDER:
        start_plane("meta", k)
    for k in ORDER[:3]:
        start("qk", k, 1, PLANE)
    rbuf[me] = sbuf[me]
    rmeta[me] = smeta[me]
    one_wait("x", PLANES - 1, False)
    one_wait("mx", PLANES - 1, False)
    across("fm", True)
    for k, first, last in zip(ORDER[3:], (0, 2, 4, 6, 7), (2, 4, 6, 7, 8)):
        start("qk", k, 1, PLANE)
        across("fx", True, first, last)
    for kind in ("v", "g"):
        for k in ORDER:
            start_plane(kind, k)

    slot_cols = turned(jnp.concatenate([slot[:, 128 * b : 128 * (b + 1)] for b in range(8)], axis=0))
    slot_cols = [slot_cols[:, b : b + 1] for b in range(BLOCKS)]

    def build_final(p, carry):
        slot_at = iota((128, 256), 1) + (p * PLANE * SEATS).astype(F32)
        final[p] = onehot(jnp.concatenate([slot_at == col for col in slot_cols], axis=0))
        return carry

    lax.fori_loop(0, PLANES, build_final, 0)

    for k in ORDER:
        arrived("meta", (PLANES - k) % PLANES)
    got = jnp.sum(rmeta[...].reshape(PLANES, PLANE, 256), axis=1)
    lost_any = jnp.max(got[:, 255:256], axis=0, keepdims=True)
    sflag[0] = jnp.broadcast_to(lost_any, (1, 128))
    for i in range(1, PARTS):
        pltpu.make_async_remote_copy(
            src_ref=sflag.at[0], dst_ref=rflag.at[my_part], send_sem=send_sem.at[12],
            recv_sem=one_sem.at[6], device_id={"dp": part_at(i)}, device_id_type=MESH,
        ).start()
    rflag[my_part] = sflag[0]

    one_wait("fm", PLANE - 1, False)
    got_extra = jnp.sum(rmx[...].reshape(PLANE, PLANES, 128), axis=1)
    base = (my_place * CL_DEV).astype(F32) * UNIT
    got_extra = got_extra - base
    mine = (got_extra >= UNIT) & (got_extra < (1.0 + CL_DEV) * UNIT)
    got_extra = jnp.where(mine, got_extra, 0.0)
    tail = jnp.where(iota((PLANES, 128), 1) < 64.0, got[:, 128:], 0.0)
    keys_all = jnp.concatenate([got[:, :128], tail, got_extra], axis=0)
    keys_all = jnp.where(keys_all < UNIT, NONE, keys_all)
    key_cols = turned(keys_all)
    n_rows = 3 * PLANES
    for r in range(n_rows):
        wide[r] = jnp.broadcast_to(key_cols[:, r : r + 1], (128, 128))

    def count(r, sums):
        less = wide[r]
        out = []
        for c in range(n_rows):
            hit = jnp.where(less < keys_all[c : c + 1], 1.0, 0.0)
            out.append(sums[c] + jnp.sum(hit.reshape(16, 8, 128), axis=0))
        return tuple(out)

    zero = jnp.zeros((8, 128), F32)
    counts = lax.fori_loop(0, n_rows, count, (zero,) * n_rows)
    place = jnp.concatenate([jnp.sum(c, axis=0, keepdims=True) for c in counts], axis=0)
    place = jnp.where(keys_all == NONE, 4096.0, place)
    place_cols = turned(place)
    starts = [jnp.zeros((1, 128), F32)]
    for c in range(1, CL_DEV):
        below = jnp.where(keys_all < (1.0 + c) * UNIT, 1.0, 0.0)
        below = jnp.sum(jnp.sum(below, axis=0, keepdims=True), axis=1, keepdims=True)
        starts.append(jnp.broadcast_to(below, (1, 128)))

    def build(p, carry):
        at = lax.broadcasted_iota(jnp.int32, (n_rows, 128), 0)
        first, second = (
            jnp.sum(jnp.where(at == p + PLANES * h, place, 0.0), axis=0, keepdims=True)
            for h in range(2)
        )
        gather[p] = onehot(
            jnp.concatenate(
                [iota((TOK, 128), 0) == first, iota((TOK, 128), 0) == second], axis=1
            )
        )
        at = lax.broadcasted_iota(jnp.int32, (128, 128), 1)
        first, second = (
            jnp.sum(jnp.where(at == p + PLANES * h, place_cols, 0.0), axis=1, keepdims=True)
            for h in range(2)
        )
        ungather[p, 0:128] = onehot(iota((128, TOK), 1) == first)
        ungather[p, 128:192] = onehot(iota((64, TOK), 1) == second[:64])
        return carry

    lax.fori_loop(0, PLANES, build, 0)
    for u in range(PLANE):
        r = 2 * PLANES + u
        xgather[:, 128 * u : 128 * (u + 1)] = onehot(iota((TOK, 128), 0) == place[r : r + 1])
        xungather[128 * u : 128 * (u + 1)] = onehot(iota((128, TOK), 1) == place_cols[:, r : r + 1])

    at = iota((BLOCKS, 128), 0) * 128.0 + iota((BLOCKS, 128), 1)
    first = jnp.zeros((BLOCKS, 128), F32)
    for c in range(1, CL_DEV):
        first = jnp.where(at >= starts[c], starts[c], first)
    first_cols = turned(first)

    def together(parts):
        return jnp.concatenate([p.reshape(-1, HD) for p in parts], axis=1).astype(BF16)

    def extras(ref, features):
        return jnp.concatenate(
            [
                ref[:, :, EXTRA * f : EXTRA * (f + 1)].reshape(PLANE * PLANES * EXTRA, HD)
                for f in features
            ],
            axis=1,
        )

    def collect(kind, features, cut):
        width = HD * len(features)
        acc[:, :width] = dot(xgather[...], extras(rx, features))
        for k in ORDER:
            p = arrived(kind, (PLANES - k) % PLANES)
            part = dot(gather[p, :, : PLANE * SEATS], together(cut(pl.ds(p * PLANE, PLANE))))
            if k == ORDER[-1]:
                return acc[:, :width] + part
            acc[:, :width] += part

    def cut_qk(at):
        block = rbuf[at, 0 : 2 * SEATS].astype(F32)
        return [block[:, :SEATS], block[:, SEATS:]]

    def cut_v(at):
        return [rbuf[at, 2 * SEATS : 2 * SEATS + 32].astype(F32)[:, :SEATS]]

    def cut_g(at):
        return [rbuf[at, 4 * SEATS - 32 : 4 * SEATS].astype(F32)[:, 32 - SEATS :]]

    front = pl.ds(0, 128)
    body = pl.ds(128, TOK)
    xqk[front] = jnp.zeros((128, 2 * HD), BF16)
    xv[front] = jnp.zeros((128, HD), BF16)

    one_wait("fx", PLANE - 1, False)
    xqk[body] = collect("qk", (0, 1), cut_qk).astype(BF16)
    for b in range(BLOCKS):
        query = xqk[pl.ds(128 * (b + 1), 128), :HD]
        keys = xqk[pl.ds(128 * b, 256), HD:]
        scores = dot_nt(query, keys) * scale
        key_at = iota((128, 256), 1) + 128.0 * (b - 1)
        query_at = iota((128, 256), 0) + 128.0 * b
        allowed = (key_at <= query_at) & (key_at >= first_cols[:, b : b + 1])
        scores = jnp.where(allowed, scores, -1e30)
        weights = jnp.exp(scores - jnp.max(scores, axis=-1, keepdims=True))
        probs_ref[b] = weights / jnp.sum(weights, axis=-1, keepdims=True)

    start_rows = jnp.concatenate(starts, axis=0)
    end_rows = jnp.concatenate(starts[1:] + [jnp.full((1, 128), float(TOK), F32)], axis=0)
    sums = jnp.zeros((CL_DEV, HD), F32)
    for b in range(BLOCKS):
        row_at = iota((CL_DEV, 128), 1) + 128.0 * b
        owned = onehot((row_at >= start_rows) & (row_at < end_rows))
        sums = sums + dot(owned, xqk[pl.ds(128 * (b + 1), 128), HD:])
    blended = 0.5 * old_ref[...] + 0.5 * sums / (end_rows - start_rows)
    power = jnp.mean(blended * blended, axis=-1, keepdims=True)
    cent_ref[...] = blended * lax.rsqrt(power + 1e-6)

    xv[body] = collect("v", (2,), cut_v).astype(BF16)
    attn = [
        dot(probs_ref[b].astype(BF16), xv[pl.ds(128 * b, 256)]).astype(BF16) for b in range(BLOCKS)
    ]
    outs = jnp.concatenate(attn, axis=0)
    res[:, :HD] = outs
    for k in ORDER:
        p = lax.rem(my_plane + k, PLANES)
        block = dot(ungather[p], outs).reshape(PLANE, SEATS, HD)
        sa[pl.ds(p * PLANE, PLANE)] = block[:, :16].astype(BF16)
        start_plane("a", k)
    ra[me] = sa[me]

    xg[...] = collect("g", (3,), cut_g).astype(BF16)
    key_tail, value_tail = None, None
    for b in range(BLOCKS):
        mine = pl.ds(128 * b, 128)
        window = pl.ds(128 * b, 256)
        query = xqk[pl.ds(128 * (b + 1), 128), :HD]
        keys = xqk[window, HD:]
        grad = xg[mine]
        probs = probs_ref[b]
        delta = jnp.sum(grad.astype(F32) * res[mine, :HD].astype(F32), axis=-1, keepdims=True)
        dprobs = dot_nt(grad, xv[window])
        dscores = (probs * (dprobs - delta) * scale).astype(BF16)
        res[mine, HD : 2 * HD] = dot(dscores, keys).astype(BF16)
        dkeys = dot_tn(dscores, query)
        dvals = dot_tn(probs.astype(BF16), grad)
        if b > 0:
            before = pl.ds(128 * (b - 1), 128)
            res[before, 2 * HD : 3 * HD] = (key_tail + dkeys[:128]).astype(BF16)
            res[before, 3 * HD :] = (value_tail + dvals[:128]).astype(BF16)
        key_tail, value_tail = dkeys[128:], dvals[128:]
    last = pl.ds(128 * (BLOCKS - 1), 128)
    res[last, 2 * HD : 3 * HD] = key_tail.astype(BF16)
    res[last, 3 * HD :] = value_tail.astype(BF16)

    results = res[...]
    back = dot(xungather[...], results)
    back = [
        back[:, HD * f : HD * (f + 1)].reshape(PLANE, PLANES, EXTRA, HD).astype(BF16)
        for f in range(4)
    ]
    sy[...] = jnp.concatenate(back, axis=2)
    ry[my_place] = sy[my_place]
    for i, k in enumerate(ORDER):
        p = lax.rem(my_plane + k, PLANES)
        parts = split_features(dot(ungather[p], results), SEATS)
        parts[0] = parts[0][:, 16:]
        sd[pl.ds(p * PLANE, PLANE)] = jnp.concatenate(parts, axis=1).astype(BF16)
        start_plane("d", k)
        if i < 4:
            across("y", False, 2 * i, 2 * i + 2)
    rd[me] = sd[me]
    one_wait("y", PLANE - 1, False)
    sw[...] = jnp.sum(ry[...].astype(F32), axis=0).astype(BF16)
    column("w")
    rw[my_plane] = sw[my_plane]

    for kind in ("meta", "qk", "v", "g", "a"):
        sent(kind)
    for kind, n in (("x", 7), ("mx", 7), ("fx", 7), ("fm", 7), ("y", 7)):
        one_wait(kind, n, True)

    one_wait("flag", PARTS - 1, False)
    flag_ref[...] = jnp.max(rflag[...], axis=0)
    one_wait("flag", PARTS - 1, True)

    def cut_back(at):
        head = ra[at].astype(F32)
        rest = rd[at].astype(F32)
        cuts = [rest[:, SEATS * f - 16 : SEATS * (f + 1) - 16] for f in range(1, 4)]
        return [jnp.concatenate([head, rest[:, : SEATS - 16]], axis=1)] + cuts

    for k in ORDER:
        arrived("a", (PLANES - k) % PLANES)
    for k in ORDER:
        p = arrived("d", (PLANES - k) % PLANES)
        part = dot(final[p, :, : PLANE * SEATS], together(cut_back(pl.ds(p * PLANE, PLANE))))
        if k == ORDER[0]:
            acc[...] = part
        else:
            acc[...] += part
    xslot_cols = turned(
        jnp.concatenate([xslot[:, 128 * b : 128 * (b + 1)] for b in range(8)], axis=0)
    )
    pick = onehot(
        jnp.concatenate(
            [iota((128, 128), 1) == xslot_cols[:, b : b + 1] for b in range(BLOCKS)], axis=0
        )
    )
    one_wait("w", PLANES - 1, False)
    late = jnp.concatenate(
        [rw[:, EXTRA * f : EXTRA * (f + 1)].reshape(PLANES * EXTRA, HD) for f in range(4)], axis=1
    )
    found = (acc[...] + dot(pick, late)).astype(BF16)
    o_ref[...] = found[:, :HD]
    dq_ref[...] = found[:, HD : 2 * HD]
    dk_ref[...] = found[:, 2 * HD : 3 * HD]
    dv_ref[...] = found[:, 3 * HD :]
    sent("d")
    one_wait("w", 7, True)


def hand_over(*refs):
    n = len(refs) // 2
    for src, dst in zip(refs[:n], refs[n:]):
        dst[...] = src[...]


def shards(queries, key_rows, values, out_grad, cluster_id, cluster_owner, old_centroids):
    vmem = pl.BlockSpec(memory_space=pltpu.VMEM)
    row_out = jax.ShapeDtypeStruct((TOK, HD), BF16)
    out_shape = (row_out, row_out, row_out, row_out, jax.ShapeDtypeStruct((CL_DEV, HD), F32))
    by_plane = [pltpu.SemaphoreType.DMA((PLANES,))] * 6
    args = (queries, key_rows, values, out_grad, cluster_id, cluster_owner, old_centroids[0])

    def pair(rows, width, n=DEVS, dtype=BF16):
        return [pltpu.VMEM((n, rows, width), dtype)] * 2

    def params(ident):
        return pltpu.CompilerParams(
            collective_id=ident, has_side_effects=True, vmem_limit_bytes=56 << 20
        )

    sorted_rows = [
        pltpu.VMEM((TOK + 128, 2 * HD), BF16),
        pltpu.VMEM((TOK + 128, HD), BF16),
        pltpu.VMEM((TOK, HD), BF16),
    ]
    work = [
        pltpu.VMEM((BLOCKS, 128, 256), F32),
        pltpu.VMEM((TOK, 4 * HD), BF16),
        pltpu.SemaphoreType.REGULAR,
    ]

    def general(*args):
        return pl.pallas_call(
            kernel,
            out_shape=out_shape,
            in_specs=[vmem] * 7,
            out_specs=(vmem,) * 5,
            scratch_shapes=[
                *pair(1, 128, dtype=F32),
                *pair(ROOM, 2 * HD), *pair(ROOM, HD), *pair(ROOM, HD),
                *pair(ROOM, HD), *pair(ROOM, 3 * HD),
                pltpu.VMEM((PLANES, TOK, CHUNK), BF16),
                pltpu.VMEM((PLANES, CHUNK, TOK), BF16),
                pltpu.VMEM((PLANES, TOK, CHUNK), BF16),
                *sorted_rows,
                pltpu.VMEM((TOK, 3 * HD), F32),
                *work,
                pltpu.SemaphoreType.DMA((6,)),
                *by_plane,
            ],
            compiler_params=params(1),
        )(*args)

    extra_rows = pltpu.VMEM((PLANE, PLANES, 4 * EXTRA, HD), BF16)
    *outs, flag = pl.pallas_call(
        kernel_fast,
        out_shape=out_shape + (jax.ShapeDtypeStruct((1, 128), F32),),
        in_specs=[vmem] * 7,
        out_specs=(vmem,) * 6,
        scratch_shapes=[
            *pair(1, 256, dtype=F32),
            pltpu.VMEM((PLANES, 1, 128), F32),
            pltpu.VMEM((PLANE, PLANES, 1, 128), F32),
            pltpu.VMEM((PLANES, 4 * EXTRA, HD), BF16),
            extra_rows,
            *pair(4 * SEATS, HD), *pair(16, HD), *pair(4 * SEATS - 16, HD),
            extra_rows, extra_rows,
            *pair(4 * EXTRA, HD, PLANES),
            *pair(1, 128, PARTS, F32),
            pltpu.VMEM((PLANES, TOK, 256), BF16),
            pltpu.VMEM((PLANES, PLANE * SEATS, TOK), BF16),
            pltpu.VMEM((PLANES, TOK, 256), BF16),
            pltpu.VMEM((TOK, TOK), BF16),
            pltpu.VMEM((TOK, TOK), BF16),
            pltpu.VMEM((3 * PLANES, 128, 128), F32),
            *sorted_rows,
            pltpu.VMEM((TOK, 4 * HD), F32),
            *work,
            pltpu.SemaphoreType.DMA((13,)),
            *by_plane,
            pltpu.SemaphoreType.DMA((7,)),
        ],
        compiler_params=params(0),
    )(*args)

    outs = lax.cond(
        flag[0, 0] > 0.0, lambda args, outs: general(*args), lambda args, outs: outs, args, tuple(outs)
    )
    outs = pl.pallas_call(
        hand_over, out_shape=out_shape, in_specs=[vmem] * 5, out_specs=(vmem,) * 5
    )(*outs)
    return outs[0], outs[1], outs[2], outs[3], outs[4][None]


def solution(mesh):
    return jax.shard_map(
        shards,
        mesh=mesh,
        in_specs=(
            P(("dp", "seq"), None),
            P(("dp", "seq"), None),
            P(("dp", "seq"), None),
            P(("dp", "seq"), None),
            P("dp", "seq"),
            P("dp", None),
            P("dp", "seq", None),
        ),
        out_specs=(
            P(("dp", "seq"), None),
            P(("dp", "seq"), None),
            P(("dp", "seq"), None),
            P(("dp", "seq"), None),
            P("dp", "seq", None),
        ),
        check_vma=False,
    )
```

```python
import functools
import math

import jax
import jax.numpy as jnp
from jax import lax
from jax.experimental import pallas as pl
from jax.experimental.pallas import tpu as pltpu
from jax.sharding import PartitionSpec as P

MESH = pl.DeviceIdType.MESH
HD = 128
CL_DEV = 16
TOK = 1024
DEVS = 64
ROOM = 32
PLANE = 8
PLANES = DEVS // PLANE
CHUNK = PLANE * ROOM
BLOCKS = TOK // 128
ORDER = (4, 1, 7, 3, 5, 2, 6, 0)
SEATS = 24
EXTRA = 8
PARTS = 4
BF16 = jnp.bfloat16
F32 = jnp.float32


def dot(a, b):
    return jnp.dot(a, b, preferred_element_type=F32)


def dot_nt(a, b):
    return lax.dot_general(a, b, (((1,), (1,)), ((), ())), preferred_element_type=F32)


def dot_tn(a, b):
    return lax.dot_general(a, b, (((0,), (0,)), ((), ())), preferred_element_type=F32)


def iota(shape, dim):
    return lax.broadcasted_iota(jnp.int32, shape, dim).astype(F32)


def onehot(mask):
    return jnp.where(mask, 1.0, 0.0).astype(BF16)


def prefix_and_total():
    row = lax.broadcasted_iota(jnp.int32, (128, 256), 0)
    col = lax.broadcasted_iota(jnp.int32, (128, 256), 1)
    return onehot((row < col) | (col >= 128))


def token_slots(cluster_id, owner):
    ident = cluster_id[...]
    low = onehot(lax.broadcasted_iota(jnp.int32, (128, TOK), 0) == lax.rem(ident, 128))
    table = jnp.concatenate([owner[:, 128 * b : 128 * (b + 1)] for b in range(8)], axis=0)
    table_dev = lax.div(table, CL_DEV)
    table_loc = table - table_dev * CL_DEV
    tables = jnp.concatenate([table_dev, table_loc], axis=0).astype(F32).astype(BF16)
    found = dot(tables, low)
    high = lax.broadcasted_iota(jnp.int32, (8, TOK), 0) == lax.div(ident, 128)
    target = jnp.sum(jnp.where(high, found[:8], 0.0), axis=0, keepdims=True)
    local = jnp.sum(jnp.where(high, found[8:], 0.0), axis=0, keepdims=True)
    device = iota((DEVS, 128), 0)
    members = [device == target[:, 128 * b : 128 * (b + 1)] for b in range(BLOCKS)]
    counted = dot(jnp.concatenate([onehot(m) for m in members], axis=0), prefix_and_total())
    running = jnp.zeros((DEVS, 128), F32)
    ranks = []
    for b in range(BLOCKS):
        part = counted[DEVS * b : DEVS * (b + 1)]
        ranks.append(
            jnp.sum(jnp.where(members[b], part[:, :128] + running, 0.0), axis=0, keepdims=True)
        )
        running = running + part[:, 128:]
    rank = jnp.concatenate(ranks, axis=1)
    return target, local, rank


def turned(rows):
    n = rows.shape[0]
    return jnp.concatenate([rows, jnp.zeros((128 - n, 128), F32)], axis=0).T


def sorted_places(ids):
    hits = [ids == float(c + 1) for c in range(CL_DEV)]
    counted = dot(jnp.concatenate([onehot(h) for h in hits], axis=0), prefix_and_total())
    n = CL_DEV * 16
    below = onehot(
        lax.broadcasted_iota(jnp.int32, (n, n), 1) < lax.broadcasted_iota(jnp.int32, (n, n), 0)
    )
    offsets = dot(below, counted[:, 128:].astype(BF16))
    inside = counted[:, :128] + offsets
    place = jnp.full((16, 128), 4096.0, F32)
    starts = []
    for c in range(CL_DEV):
        place = jnp.where(hits[c], inside[16 * c : 16 * (c + 1)], place)
        starts.append(offsets[16 * c : 16 * c + 1])
    return place, starts


def plane_rows(place, p):
    at = lax.broadcasted_iota(jnp.int32, (16, 128), 0)
    return [
        jnp.sum(jnp.where(at == 2 * p + h, place, 0.0), axis=0, keepdims=True) for h in range(2)
    ]


def plane_cols(cols, p):
    at = lax.broadcasted_iota(jnp.int32, (128, 128), 1)
    return [jnp.sum(jnp.where(at == 2 * p + h, cols, 0.0), axis=1, keepdims=True) for h in range(2)]


def kernel(
    q_ref, k_ref, v_ref, g_ref, id_ref, owner_ref, old_ref,
    o_ref, dq_ref, dk_ref, dv_ref, cent_ref,
    smeta, rmeta, sqk, rqk, sv, rv, sg, rg, sa, ra, sd, rd,
    gather, ungather, final, xqk, xv, xg, acc, probs_ref, res,
    column_sem, send_sem, meta_sem, qk_sem, v_sem, g_sem, a_sem, d_sem,
):
    me = lax.axis_index("seq")
    my_plane = me // PLANE
    my_place = lax.rem(me, PLANE)
    scale = 1.0 / math.sqrt(HD)

    def peer_at(k, j):
        return lax.rem(my_plane + k, PLANES) * PLANE + lax.rem(my_place + j, PLANE)

    def signal(sem, k, j):
        pl.semaphore_signal(
            sem, inc=1, device_id={"seq": peer_at(k, j)}, device_id_type=MESH
        )

    barrier = pltpu.get_barrier_semaphore()
    for k in ORDER[:-1]:
        signal(barrier, k, 0)
    for j in range(1, PLANE):
        signal(barrier, 0, j)

    kinds = {
        "meta": (0, smeta, rmeta, meta_sem),
        "qk": (1, sqk, rqk, qk_sem),
        "v": (2, sv, rv, v_sem),
        "g": (3, sg, rg, g_sem),
        "a": (4, sa, ra, a_sem),
        "d": (5, sd, rd, d_sem),
    }

    def start(kind, k, first, last):
        index, src, dst, sem = kinds[kind]

        def body(j, carry):
            peer = peer_at(k, j)
            pltpu.make_async_remote_copy(
                src_ref=src.at[peer], dst_ref=dst.at[me], send_sem=send_sem.at[index],
                recv_sem=sem.at[my_plane], device_id={"seq": peer}, device_id_type=MESH,
            ).start()
            return carry

        lax.fori_loop(first, last, body, 0)

    def start_plane(kind, k):
        start(kind, k, 1 if k == 0 else 0, PLANE)

    def arrived(kind, k):
        _, _, dst, sem = kinds[kind]
        p = lax.rem(my_plane + k, PLANES)
        some = dst.at[pl.ds(p * PLANE, PLANE - 1 if k == 0 else PLANE)]
        pltpu.make_async_copy(some, some, sem.at[p]).wait()
        return p

    def sent(kind):
        index, src, _, _ = kinds[kind]
        some = src.at[pl.ds(0, DEVS - 1)]
        pltpu.make_async_copy(some, some, send_sem.at[index]).wait()

    def keep_own(kind):
        _, src, dst, _ = kinds[kind]
        dst[me] = src[me]

    def plane_of(ref, p):
        block = ref[pl.ds(p * PLANE, PLANE)]
        return block.reshape(CHUNK, block.shape[-1])

    def put_plane(ref, p, value):
        ref[pl.ds(p * PLANE, PLANE)] = value.astype(BF16).reshape(PLANE, ROOM, value.shape[-1])

    target, local, rank = token_slots(id_ref, owner_ref)
    slot = target * float(ROOM) + rank
    rows = jnp.concatenate([q_ref[...], k_ref[...], v_ref[...], g_ref[...]], axis=1)

    def fill(p, carry):
        pick = onehot(iota((CHUNK, TOK), 0) + (p * CHUNK).astype(F32) == slot)
        block = dot(pick, rows)
        put_plane(sqk, p, block[:, : 2 * HD])
        put_plane(sv, p, block[:, 2 * HD : 3 * HD])
        put_plane(sg, p, block[:, 3 * HD :])
        return carry

    lax.fori_loop(0, PLANES, fill, 0)

    quarter = (lax.rem(me, 4) * ROOM).astype(F32)
    lane_of = onehot(iota((128, TOK), 0) == rank + quarter)
    labels = jnp.where(iota((DEVS, TOK), 0) == target, local + 1.0, 0.0).astype(BF16)
    smeta[...] = dot_nt(labels, lane_of).reshape(DEVS, 1, 128)

    pl.semaphore_wait(barrier, 2 * PLANE - 2)
    for k in ORDER[:-1]:
        signal(column_sem, k, 0)
    for k in ORDER[:-1]:
        start("qk", k, 0, 1)
    pl.semaphore_wait(column_sem, PLANE - 1)
    for k in ORDER:
        start("qk", k, 1, PLANE)
    for kind in ("meta", "v", "g"):
        for k in ORDER:
            start_plane(kind, k)
    for kind in ("meta", "qk", "v", "g"):
        keep_own(kind)

    slot_cols = turned(jnp.concatenate([slot[:, 128 * b : 128 * (b + 1)] for b in range(8)], axis=0))
    slot_cols = [slot_cols[:, b : b + 1] for b in range(BLOCKS)]

    def build_final(p, carry):
        slot_at = iota((128, CHUNK), 1) + (p * CHUNK).astype(F32)
        final[p] = onehot(jnp.concatenate([slot_at == col for col in slot_cols], axis=0))
        return carry

    lax.fori_loop(0, PLANES, build_final, 0)

    for k in ORDER:
        arrived("meta", (PLANES - k) % PLANES)
    ids = jnp.sum(rmeta[...].reshape(16, 4, 128), axis=1)
    place, starts = sorted_places(ids)
    place_cols = turned(place)

    def build(p, carry):
        rows_of = plane_rows(place, p)
        gather[p] = onehot(jnp.concatenate([iota((TOK, 128), 0) == r for r in rows_of], axis=1))
        cols_of = plane_cols(place_cols, p)
        ungather[p] = onehot(jnp.concatenate([iota((128, TOK), 1) == c for c in cols_of], axis=0))
        return carry

    lax.fori_loop(0, PLANES, build, 0)

    at = iota((BLOCKS, 128), 0) * 128.0 + iota((BLOCKS, 128), 1)
    first = jnp.zeros((BLOCKS, 128), F32)
    for c in range(1, CL_DEV):
        first = jnp.where(at >= starts[c], starts[c], first)
    first_cols = turned(first)

    def collect(kind, matrix):
        _, _, dst, _ = kinds[kind]
        width = dst.shape[-1]
        for i, k in enumerate(ORDER):
            p = arrived(kind, (PLANES - k) % PLANES)
            part = dot(matrix[p], plane_of(dst, p))
            if i == PLANES - 1:
                return acc[:, :width] + part
            acc[:, :width] = part if i == 0 else acc[:, :width] + part

    front = pl.ds(0, 128)
    body = pl.ds(128, TOK)
    xqk[front] = jnp.zeros((128, 2 * HD), BF16)
    xv[front] = jnp.zeros((128, HD), BF16)

    xqk[body] = collect("qk", gather).astype(BF16)
    for b in range(BLOCKS):
        query = xqk[pl.ds(128 * (b + 1), 128), :HD]
        keys = xqk[pl.ds(128 * b, 256), HD:]
        scores = dot_nt(query, keys) * scale
        key_at = iota((128, 256), 1) + 128.0 * (b - 1)
        query_at = iota((128, 256), 0) + 128.0 * b
        allowed = (key_at <= query_at) & (key_at >= first_cols[:, b : b + 1])
        scores = jnp.where(allowed, scores, -1e30)
        weights = jnp.exp(scores - jnp.max(scores, axis=-1, keepdims=True))
        probs_ref[b] = weights / jnp.sum(weights, axis=-1, keepdims=True)

    start_rows = jnp.concatenate(starts, axis=0)
    end_rows = jnp.concatenate(starts[1:] + [jnp.full((1, 128), float(TOK), F32)], axis=0)
    sums = jnp.zeros((CL_DEV, HD), F32)
    for b in range(BLOCKS):
        row_at = iota((CL_DEV, 128), 1) + 128.0 * b
        owned = onehot((row_at >= start_rows) & (row_at < end_rows))
        sums = sums + dot(owned, xqk[pl.ds(128 * (b + 1), 128), HD:])
    blended = 0.5 * old_ref[...] + 0.5 * sums / (end_rows - start_rows)
    power = jnp.mean(blended * blended, axis=-1, keepdims=True)
    cent_ref[...] = blended * lax.rsqrt(power + 1e-6)

    xv[body] = collect("v", gather).astype(BF16)
    attn = [
        dot(probs_ref[b].astype(BF16), xv[pl.ds(128 * b, 256)]).astype(BF16) for b in range(BLOCKS)
    ]
    outs = jnp.concatenate(attn, axis=0)
    res[:, :HD] = outs
    for k in ORDER:
        p = lax.rem(my_plane + k, PLANES)
        put_plane(sa, p, dot(ungather[p], outs))
        start_plane("a", k)
    keep_own("a")

    xg[...] = collect("g", gather).astype(BF16)
    key_tail, value_tail = None, None
    for b in range(BLOCKS):
        mine = pl.ds(128 * b, 128)
        window = pl.ds(128 * b, 256)
        query = xqk[pl.ds(128 * (b + 1), 128), :HD]
        keys = xqk[window, HD:]
        grad = xg[mine]
        probs = probs_ref[b]
        delta = jnp.sum(
            grad.astype(F32) * res[mine, :HD].astype(F32), axis=-1, keepdims=True
        )
        dprobs = dot_nt(grad, xv[window])
        dscores = (probs * (dprobs - delta) * scale).astype(BF16)
        res[mine, HD : 2 * HD] = dot(dscores, keys).astype(BF16)
        dkeys = dot_tn(dscores, query)
        dvals = dot_tn(probs.astype(BF16), grad)
        if b > 0:
            before = pl.ds(128 * (b - 1), 128)
            res[before, 2 * HD : 3 * HD] = (key_tail + dkeys[:128]).astype(BF16)
            res[before, 3 * HD :] = (value_tail + dvals[:128]).astype(BF16)
        key_tail, value_tail = dkeys[128:], dvals[128:]
    last = pl.ds(128 * (BLOCKS - 1), 128)
    res[last, 2 * HD : 3 * HD] = key_tail.astype(BF16)
    res[last, 3 * HD :] = value_tail.astype(BF16)

    grads = res[:, HD:]
    for k in ORDER:
        p = lax.rem(my_plane + k, PLANES)
        put_plane(sd, p, dot(ungather[p], grads))
        start_plane("d", k)
    keep_own("d")
    for kind in ("meta", "qk", "v", "g"):
        sent(kind)

    o_ref[...] = collect("a", final).astype(BF16)
    sent("a")
    found = collect("d", final).astype(BF16)
    dq_ref[...] = found[:, :HD]
    dk_ref[...] = found[:, HD : 2 * HD]
    dv_ref[...] = found[:, 2 * HD :]
    sent("d")


def seated_rank(seats, member):
    n = seats
    counted = dot(jnp.concatenate([onehot(m) for m in member], axis=0), prefix_and_total())
    running = jnp.zeros((n, 128), F32)
    ranks = []
    for b in range(BLOCKS):
        part = counted[n * b : n * (b + 1)]
        ranks.append(
            jnp.sum(jnp.where(member[b], part[:, :128] + running, 0.0), axis=0, keepdims=True)
        )
        running = running + part[:, 128:]
    return jnp.concatenate(ranks, axis=1)


def split_features(block, rows):
    f = block.shape[1] // HD
    return [block[:, HD * j : HD * (j + 1)].reshape(-1, rows, HD) for j in range(f)]


def kernel_fast(
    q_ref, k_ref, v_ref, g_ref, id_ref, owner_ref, old_ref,
    o_ref, dq_ref, dk_ref, dv_ref, cent_ref, flag_ref,
    smeta, rmeta, smx, rmx, sx, rx, sbuf, rbuf, sa, ra, sd, rd, sy, ry, sw, rw, sflag, rflag,
    gather, ungather, final, xgather, xungather, wide, xqk, xv, xg, acc, probs_ref, res,
    column_sem, send_sem, meta_sem, qk_sem, v_sem, g_sem, a_sem, d_sem, one_sem,
):
    me = lax.axis_index("seq")
    my_part = lax.axis_index("dp")
    my_plane = me // PLANE
    my_place = lax.rem(me, PLANE)
    scale = 1.0 / math.sqrt(HD)
    UNIT = 65536.0
    NONE = 8388608.0

    def peer_at(k, j):
        return lax.rem(my_plane + k, PLANES) * PLANE + lax.rem(my_place + j, PLANE)

    def part_at(i):
        return lax.rem(my_part + i, PARTS)

    def signal(sem, k, j):
        pl.semaphore_signal(sem, inc=1, device_id={"seq": peer_at(k, j)}, device_id_type=MESH)

    barrier = pltpu.get_barrier_semaphore()
    for k in ORDER[:-1]:
        signal(barrier, k, 0)
    for j in range(1, PLANE):
        signal(barrier, 0, j)
    for i in range(1, PARTS):
        pl.semaphore_signal(barrier, inc=1, device_id={"dp": part_at(i)}, device_id_type=MESH)

    kinds = {
        "meta": (0, smeta, rmeta, meta_sem, 0, 1),
        "qk": (1, sbuf, rbuf, qk_sem, 0, 2 * SEATS),
        "v": (2, sbuf, rbuf, v_sem, 2 * SEATS, 32),
        "g": (3, sbuf, rbuf, g_sem, 2 * SEATS + 32, 16),
        "a": (4, sa, ra, a_sem, 0, 16),
        "d": (5, sd, rd, d_sem, 0, 4 * SEATS - 16),
    }

    def start(kind, k, first, last):
        index, src, dst, sem, low, count = kinds[kind]
        some = pl.ds(low, count)

        def body(j, carry):
            peer = peer_at(k, j)
            pltpu.make_async_remote_copy(
                src_ref=src.at[peer, some], dst_ref=dst.at[me, some],
                send_sem=send_sem.at[index], recv_sem=sem.at[my_plane],
                device_id={"seq": peer}, device_id_type=MESH,
            ).start()
            return carry

        lax.fori_loop(first, last, body, 0)

    def start_plane(kind, k):
        start(kind, k, 1 if k == 0 else 0, PLANE)

    def arrived(kind, k):
        _, _, dst, sem, low, count = kinds[kind]
        p = lax.rem(my_plane + k, PLANES)
        some = dst.at[pl.ds(p * PLANE, PLANE - 1 if k == 0 else PLANE), pl.ds(low, count)]
        pltpu.make_async_copy(some, some, sem.at[p]).wait()
        return p

    def sent(kind):
        index, src, _, _, low, count = kinds[kind]
        some = src.at[pl.ds(0, DEVS - 1), pl.ds(low, count)]
        pltpu.make_async_copy(some, some, send_sem.at[index]).wait()

    ones = {
        "x": (6, sx, rx.at[my_place], 0),
        "mx": (7, smx, rmx.at[my_place], 1),
        "fx": (8, rx, rx, 2),
        "fm": (9, rmx, rmx, 3),
        "y": (10, sy, ry, 4),
        "w": (11, sw, rw, 5),
        "flag": (12, sflag, rflag, 6),
    }

    def column(kind):
        index, src, dst, sem = ones[kind]
        for k in ORDER[:-1]:
            p = lax.rem(my_plane + k, PLANES)
            pltpu.make_async_remote_copy(
                src_ref=src.at[p], dst_ref=dst.at[my_plane], send_sem=send_sem.at[index],
                recv_sem=one_sem.at[sem], device_id={"seq": peer_at(k, 0)}, device_id_type=MESH,
            ).start()

    def across(kind, forward, first=0, last=PLANES):
        index, src, dst, sem = ones[kind]
        some = pl.ds(first, last - first)
        for j in range(1, PLANE):
            seat = lax.rem(my_place + j, PLANE)
            pltpu.make_async_remote_copy(
                src_ref=src.at[my_place if forward else seat, some],
                dst_ref=dst.at[my_place, some],
                send_sem=send_sem.at[index], recv_sem=one_sem.at[sem],
                device_id={"seq": peer_at(0, j)}, device_id_type=MESH,
            ).start()

    def one_wait(kind, n, sending):
        index, src, dst, sem = ones[kind]
        some = (src if sending else dst).at[pl.ds(0, n)]
        pltpu.make_async_copy(
            some, some, send_sem.at[index] if sending else one_sem.at[sem]
        ).wait()

    target, local, rank = token_slots(id_ref, owner_ref)
    plane_row = jnp.floor(target * (1.0 / PLANE))
    seat_row = target - plane_row * float(PLANE)
    direct = rank < float(SEATS)
    slot = jnp.where(direct, target * float(SEATS) + rank, -1.0)
    member = [
        (iota((PLANES, 128), 0) == plane_row[:, 128 * b : 128 * (b + 1)])
        & (rank[:, 128 * b : 128 * (b + 1)] >= float(SEATS))
        for b in range(BLOCKS)
    ]
    extra = seated_rank(PLANES, member)
    fits = (rank >= float(SEATS)) & (extra < float(EXTRA))
    xslot = jnp.where(fits, plane_row * float(EXTRA) + extra, -1.0)
    lost = jnp.max(jnp.where(extra >= float(EXTRA), 1.0, 0.0), axis=1, keepdims=True)

    rows = jnp.concatenate([q_ref[...], k_ref[...], v_ref[...], g_ref[...]], axis=1)

    def fill(k):
        p = lax.rem(my_plane + k, PLANES)
        pick = onehot(iota((PLANE * SEATS, TOK), 0) + (p * PLANE * SEATS).astype(F32) == slot)
        parts = split_features(dot(pick, rows), SEATS)
        sbuf[pl.ds(p * PLANE, PLANE)] = jnp.concatenate(parts, axis=1).astype(BF16)

    fill(ORDER[0])
    pl.semaphore_wait(barrier, 2 * PLANE - 2 + PARTS - 1)
    for k in ORDER[:-1]:
        signal(column_sem, k, 0)
    for i, k in enumerate(ORDER[:-1]):
        for kind in ("qk", "v", "g"):
            start(kind, k, 0, 1)
        fill(ORDER[i + 1])
    block = dot(onehot(iota((PLANES * EXTRA, TOK), 0) == xslot), rows)
    sx[...] = jnp.concatenate(split_features(block, EXTRA), axis=1).astype(BF16)
    column("x")
    rx[my_place, my_plane] = sx[my_plane]

    when = iota((1, TOK), 1)
    when_high = jnp.floor(when * (1.0 / 32))
    when_low = when - 32.0 * when_high
    here = (me * TOK).astype(F32)

    def keys_of(rows_at, label, lanes_at):
        n = rows_at.shape[0]
        stack = [jnp.where(rows_at, r, 0.0) for r in (label, when_high, when_low)]
        found = dot_nt(jnp.concatenate(stack, axis=0).astype(BF16), onehot(lanes_at))
        label = found[:n]
        key = label * UNIT + 32.0 * found[n : 2 * n] + found[2 * n :]
        return key + jnp.where(label > 0.0, here, 0.0)

    lane = jnp.where(direct, rank + (my_place * SEATS).astype(F32), -1.0)
    key = keys_of(iota((DEVS, TOK), 0) == target, local + 1.0, iota((256, TOK), 0) == lane)
    key = jnp.where(iota((DEVS, 256), 1) == 255.0, lost, key)
    smeta[...] = key.reshape(DEVS, 1, 256)
    first_lane = my_plane * EXTRA + lax.rem(my_place, 2) * 64
    lane = jnp.where(fits, extra + first_lane.astype(F32), -1.0)
    label = local + 1.0 + seat_row * float(CL_DEV)
    key = keys_of(iota((PLANES, TOK), 0) == plane_row, label, iota((128, TOK), 0) == lane)
    smx[...] = key.reshape(PLANES, 1, 128)

    column("mx")
    rmx[my_place, my_plane] = smx[my_plane]
    pl.semaphore_wait(column_sem, PLANE - 1)
    for k in ORDER:
        start_plane("meta", k)
    for k in ORDER[:3]:
        start("qk", k, 1, PLANE)
    rbuf[me] = sbuf[me]
    rmeta[me] = smeta[me]
    one_wait("x", PLANES - 1, False)
    one_wait("mx", PLANES - 1, False)
    across("fm", True)
    for k, first, last in zip(ORDER[3:], (0, 2, 4, 6, 7), (2, 4, 6, 7, 8)):
        start("qk", k, 1, PLANE)
        across("fx", True, first, last)
    for kind in ("v", "g"):
        for k in ORDER:
            start(kind, k, 1, PLANE)

    slot_cols = turned(jnp.concatenate([slot[:, 128 * b : 128 * (b + 1)] for b in range(8)], axis=0))
    slot_cols = [slot_cols[:, b : b + 1] for b in range(BLOCKS)]

    def build_final(p, carry):
        slot_at = iota((128, 256), 1) + (p * PLANE * SEATS).astype(F32)
        final[p] = onehot(jnp.concatenate([slot_at == col for col in slot_cols], axis=0))
        return carry

    lax.fori_loop(0, PLANES, build_final, 0)

    for k in ORDER:
        arrived("meta", (PLANES - k) % PLANES)
    got = jnp.sum(rmeta[...].reshape(PLANES, PLANE, 256), axis=1)
    lost_any = jnp.max(got[:, 255:256], axis=0, keepdims=True)
    sflag[0] = jnp.broadcast_to(lost_any, (1, 128))
    for i in range(1, PARTS):
        pltpu.make_async_remote_copy(
            src_ref=sflag.at[0], dst_ref=rflag.at[my_part], send_sem=send_sem.at[12],
            recv_sem=one_sem.at[6], device_id={"dp": part_at(i)}, device_id_type=MESH,
        ).start()
    rflag[my_part] = sflag[0]

    one_wait("fm", PLANE - 1, False)
    got_extra = jnp.sum(rmx[...].reshape(PLANE, PLANES, 128), axis=1)
    base = (my_place * CL_DEV).astype(F32) * UNIT
    got_extra = got_extra - base
    mine = (got_extra >= UNIT) & (got_extra < (1.0 + CL_DEV) * UNIT)
    got_extra = jnp.where(mine, got_extra, 0.0)
    got_extra = jnp.sum(got_extra.reshape(PLANE // 2, 2, 128), axis=1)
    tail = jnp.where(iota((PLANES, 128), 1) < 64.0, got[:, 128:], 0.0)
    keys_all = jnp.concatenate([got[:, :128], tail, got_extra], axis=0)
    keys_all = jnp.where(keys_all < UNIT, NONE, keys_all)
    key_cols = turned(keys_all)
    n_rows = 2 * PLANES + PLANE // 2
    for r in range(n_rows):
        wide[r] = jnp.broadcast_to(key_cols[:, r : r + 1], (128, 128))

    def count(r, sums):
        less = wide[r]
        out = []
        for c in range(n_rows):
            hit = jnp.where(less < keys_all[c : c + 1], 1.0, 0.0)
            out.append(sums[c] + jnp.sum(hit.reshape(16, 8, 128), axis=0))
        return tuple(out)

    zero = jnp.zeros((8, 128), F32)
    counts = lax.fori_loop(0, n_rows, count, (zero,) * n_rows)
    place = jnp.concatenate([jnp.sum(c, axis=0, keepdims=True) for c in counts], axis=0)
    place = jnp.where(keys_all == NONE, 4096.0, place)
    place_cols = turned(place)
    starts = [jnp.zeros((1, 128), F32)]
    for c in range(1, CL_DEV):
        below = jnp.where(keys_all < (1.0 + c) * UNIT, 1.0, 0.0)
        below = jnp.sum(jnp.sum(below, axis=0, keepdims=True), axis=1, keepdims=True)
        starts.append(jnp.broadcast_to(below, (1, 128)))

    def build(p, carry):
        at = lax.broadcasted_iota(jnp.int32, (n_rows, 128), 0)
        first, second = (
            jnp.sum(jnp.where(at == p + PLANES * h, place, 0.0), axis=0, keepdims=True)
            for h in range(2)
        )
        gather[p] = onehot(
            jnp.concatenate(
                [iota((TOK, 128), 0) == first, iota((TOK, 128), 0) == second], axis=1
            )
        )
        at = lax.broadcasted_iota(jnp.int32, (128, 128), 1)
        first, second = (
            jnp.sum(jnp.where(at == p + PLANES * h, place_cols, 0.0), axis=1, keepdims=True)
            for h in range(2)
        )
        ungather[p, 0:128] = onehot(iota((128, TOK), 1) == first)
        ungather[p, 128:192] = onehot(iota((64, TOK), 1) == second[:64])
        return carry

    lax.fori_loop(0, PLANES, build, 0)
    for u in range(PLANE // 2):
        r = 2 * PLANES + u
        xgather[:, 128 * u : 128 * (u + 1)] = onehot(iota((TOK, 128), 0) == place[r : r + 1])
        xungather[128 * u : 128 * (u + 1)] = onehot(iota((128, TOK), 1) == place_cols[:, r : r + 1])

    at = iota((BLOCKS, 128), 0) * 128.0 + iota((BLOCKS, 128), 1)
    first = jnp.zeros((BLOCKS, 128), F32)
    for c in range(1, CL_DEV):
        first = jnp.where(at >= starts[c], starts[c], first)
    first_cols = turned(first)

    def together(parts):
        return jnp.concatenate([p.reshape(-1, HD) for p in parts], axis=1).astype(BF16)

    def extras(ref, features):
        low = EXTRA * features[0] // 16 * 16
        block = ref[:, :, low : max(low + 16, EXTRA * (features[-1] + 1))].astype(F32)
        cuts = [block[:, :, EXTRA * f - low : EXTRA * (f + 1) - low] for f in features]
        return together(cuts)

    def collect(kind, features, cut):
        width = HD * len(features)
        acc[:, :width] = dot(xgather[...], extras(rx, features))
        for k in ORDER:
            p = arrived(kind, (PLANES - k) % PLANES)
            part = dot(gather[p, :, : PLANE * SEATS], together(cut(pl.ds(p * PLANE, PLANE))))
            if k == ORDER[-1]:
                return acc[:, :width] + part
            acc[:, :width] += part

    def cut_qk(at):
        block = rbuf[at, 0 : 2 * SEATS].astype(F32)
        return [block[:, :SEATS], block[:, SEATS:]]

    def cut_v(at):
        return [rbuf[at, 2 * SEATS : 2 * SEATS + 32].astype(F32)[:, :SEATS]]

    def cut_g(at):
        return [rbuf[at, 4 * SEATS - 32 : 4 * SEATS].astype(F32)[:, 32 - SEATS :]]

    front = pl.ds(0, 128)
    body = pl.ds(128, TOK)
    xqk[front] = jnp.zeros((128, 2 * HD), BF16)
    xv[front] = jnp.zeros((128, HD), BF16)

    one_wait("fx", PLANE - 1, False)
    xqk[body] = collect("qk", (0, 1), cut_qk).astype(BF16)
    for b in range(BLOCKS):
        query = xqk[pl.ds(128 * (b + 1), 128), :HD]
        keys = xqk[pl.ds(128 * b, 256), HD:]
        scores = dot_nt(query, keys) * scale
        key_at = iota((128, 256), 1) + 128.0 * (b - 1)
        query_at = iota((128, 256), 0) + 128.0 * b
        allowed = (key_at <= query_at) & (key_at >= first_cols[:, b : b + 1])
        scores = jnp.where(allowed, scores, -1e30)
        weights = jnp.exp(scores - jnp.max(scores, axis=-1, keepdims=True))
        probs_ref[b] = weights / jnp.sum(weights, axis=-1, keepdims=True)

    start_rows = jnp.concatenate(starts, axis=0)
    end_rows = jnp.concatenate(starts[1:] + [jnp.full((1, 128), float(TOK), F32)], axis=0)
    sums = jnp.zeros((CL_DEV, HD), F32)
    for b in range(BLOCKS):
        row_at = iota((CL_DEV, 128), 1) + 128.0 * b
        owned = onehot((row_at >= start_rows) & (row_at < end_rows))
        sums = sums + dot(owned, xqk[pl.ds(128 * (b + 1), 128), HD:])
    blended = 0.5 * old_ref[...] + 0.5 * sums / (end_rows - start_rows)
    power = jnp.mean(blended * blended, axis=-1, keepdims=True)
    cent_ref[...] = blended * lax.rsqrt(power + 1e-6)

    xv[body] = collect("v", (2,), cut_v).astype(BF16)
    attn = [
        dot(probs_ref[b].astype(BF16), xv[pl.ds(128 * b, 256)]).astype(BF16) for b in range(BLOCKS)
    ]
    outs = jnp.concatenate(attn, axis=0)
    res[:, :HD] = outs
    for k in ORDER:
        p = lax.rem(my_plane + k, PLANES)
        block = dot(ungather[p], outs).reshape(PLANE, SEATS, HD)
        sa[pl.ds(p * PLANE, PLANE)] = block[:, :16].astype(BF16)
        start_plane("a", k)
    ra[me] = sa[me]

    xg[...] = collect("g", (3,), cut_g).astype(BF16)
    key_tail, value_tail = None, None
    for b in range(BLOCKS):
        mine = pl.ds(128 * b, 128)
        window = pl.ds(128 * b, 256)
        query = xqk[pl.ds(128 * (b + 1), 128), :HD]
        keys = xqk[window, HD:]
        grad = xg[mine]
        probs = probs_ref[b]
        delta = jnp.sum(grad.astype(F32) * res[mine, :HD].astype(F32), axis=-1, keepdims=True)
        dprobs = dot_nt(grad, xv[window])
        dscores = (probs * (dprobs - delta) * scale).astype(BF16)
        res[mine, HD : 2 * HD] = dot(dscores, keys).astype(BF16)
        dkeys = dot_tn(dscores, query)
        dvals = dot_tn(probs.astype(BF16), grad)
        if b > 0:
            before = pl.ds(128 * (b - 1), 128)
            res[before, 2 * HD : 3 * HD] = (key_tail + dkeys[:128]).astype(BF16)
            res[before, 3 * HD :] = (value_tail + dvals[:128]).astype(BF16)
        key_tail, value_tail = dkeys[128:], dvals[128:]
    last = pl.ds(128 * (BLOCKS - 1), 128)
    res[last, 2 * HD : 3 * HD] = key_tail.astype(BF16)
    res[last, 3 * HD :] = value_tail.astype(BF16)

    results = res[...]
    for i, k in enumerate(ORDER):
        if i == 2:
            back = dot(xungather[...], results)
            back = [
                back[:, HD * f : HD * (f + 1)].reshape(PLANE, PLANES, EXTRA, HD) for f in range(4)
            ]
            sy[...] = jnp.concatenate(back, axis=2).astype(BF16)
            ry[my_place] = sy[my_place]
        p = lax.rem(my_plane + k, PLANES)
        parts = split_features(dot(ungather[p], results), SEATS)
        parts[0] = parts[0][:, 16:]
        sd[pl.ds(p * PLANE, PLANE)] = jnp.concatenate(parts, axis=1).astype(BF16)
        start_plane("d", k)
        if 2 <= i < 6:
            across("y", False, 2 * i - 4, 2 * i - 2)
    rd[me] = sd[me]
    one_wait("y", PLANE - 1, False)
    sw[...] = jnp.sum(ry[...].astype(F32), axis=0).astype(BF16)
    column("w")
    rw[my_plane] = sw[my_plane]

    for kind in ("meta", "qk", "v", "g", "a"):
        sent(kind)
    for kind, n in (("x", 7), ("mx", 7), ("fx", 7), ("fm", 7), ("y", 7)):
        one_wait(kind, n, True)

    one_wait("flag", PARTS - 1, False)
    flag_ref[...] = jnp.max(rflag[...], axis=0)
    one_wait("flag", PARTS - 1, True)

    def cut_back(at):
        head = ra[at].astype(F32)
        rest = rd[at].astype(F32)
        cuts = [rest[:, SEATS * f - 16 : SEATS * (f + 1) - 16] for f in range(1, 4)]
        return [jnp.concatenate([head, rest[:, : SEATS - 16]], axis=1)] + cuts

    for k in ORDER:
        arrived("a", (PLANES - k) % PLANES)
    for k in ORDER:
        p = arrived("d", (PLANES - k) % PLANES)
        part = dot(final[p, :, : PLANE * SEATS], together(cut_back(pl.ds(p * PLANE, PLANE))))
        if k == ORDER[0]:
            acc[...] = part
        else:
            acc[...] += part
    xslot_cols = turned(
        jnp.concatenate([xslot[:, 128 * b : 128 * (b + 1)] for b in range(8)], axis=0)
    )
    pick = onehot(
        jnp.concatenate(
            [iota((128, PLANES * EXTRA), 1) == xslot_cols[:, b : b + 1] for b in range(BLOCKS)],
            axis=0,
        )
    )
    one_wait("w", PLANES - 1, False)
    block = rw[...].astype(F32)
    late = together([block[:, EXTRA * f : EXTRA * (f + 1)] for f in range(4)])
    found = (acc[...] + dot(pick, late)).astype(BF16)
    o_ref[...] = found[:, :HD]
    dq_ref[...] = found[:, HD : 2 * HD]
    dk_ref[...] = found[:, 2 * HD : 3 * HD]
    dv_ref[...] = found[:, 3 * HD :]
    sent("d")
    one_wait("w", 7, True)


def hand_over(*refs):
    n = len(refs) // 2
    for src, dst in zip(refs[:n], refs[n:]):
        dst[...] = src[...]


def shards(queries, key_rows, values, out_grad, cluster_id, cluster_owner, old_centroids):
    vmem = pl.BlockSpec(memory_space=pltpu.VMEM)
    row_out = jax.ShapeDtypeStruct((TOK, HD), BF16)
    out_shape = (row_out, row_out, row_out, row_out, jax.ShapeDtypeStruct((CL_DEV, HD), F32))
    by_plane = [pltpu.SemaphoreType.DMA((PLANES,))] * 6
    args = (queries, key_rows, values, out_grad, cluster_id, cluster_owner, old_centroids[0])

    def pair(rows, width, n=DEVS, dtype=BF16):
        return [pltpu.VMEM((n, rows, width), dtype)] * 2

    def params(ident):
        return pltpu.CompilerParams(
            collective_id=ident, has_side_effects=True, vmem_limit_bytes=56 << 20
        )

    sorted_rows = [
        pltpu.VMEM((TOK + 128, 2 * HD), BF16),
        pltpu.VMEM((TOK + 128, HD), BF16),
        pltpu.VMEM((TOK, HD), BF16),
    ]
    work = [
        pltpu.VMEM((BLOCKS, 128, 256), F32),
        pltpu.VMEM((TOK, 4 * HD), BF16),
        pltpu.SemaphoreType.REGULAR,
    ]

    def general(*args):
        return pl.pallas_call(
            kernel,
            out_shape=out_shape,
            in_specs=[vmem] * 7,
            out_specs=(vmem,) * 5,
            scratch_shapes=[
                *pair(1, 128, dtype=F32),
                *pair(ROOM, 2 * HD), *pair(ROOM, HD), *pair(ROOM, HD),
                *pair(ROOM, HD), *pair(ROOM, 3 * HD),
                pltpu.VMEM((PLANES, TOK, CHUNK), BF16),
                pltpu.VMEM((PLANES, CHUNK, TOK), BF16),
                pltpu.VMEM((PLANES, TOK, CHUNK), BF16),
                *sorted_rows,
                pltpu.VMEM((TOK, 3 * HD), F32),
                *work,
                pltpu.SemaphoreType.DMA((6,)),
                *by_plane,
            ],
            compiler_params=params(1),
        )(*args)

    extra_rows = pltpu.VMEM((PLANE, PLANES, 4 * EXTRA, HD), BF16)
    *outs, flag = pl.pallas_call(
        kernel_fast,
        out_shape=out_shape + (jax.ShapeDtypeStruct((1, 128), F32),),
        in_specs=[vmem] * 7,
        out_specs=(vmem,) * 6,
        scratch_shapes=[
            *pair(1, 256, dtype=F32),
            pltpu.VMEM((PLANES, 1, 128), F32),
            pltpu.VMEM((PLANE, PLANES, 1, 128), F32),
            pltpu.VMEM((PLANES, 4 * EXTRA, HD), BF16),
            extra_rows,
            *pair(4 * SEATS, HD), *pair(16, HD), *pair(4 * SEATS - 16, HD),
            extra_rows, extra_rows,
            *pair(4 * EXTRA, HD, PLANES),
            *pair(1, 128, PARTS, F32),
            pltpu.VMEM((PLANES, TOK, 256), BF16),
            pltpu.VMEM((PLANES, PLANE * SEATS, TOK), BF16),
            pltpu.VMEM((PLANES, TOK, 256), BF16),
            pltpu.VMEM((TOK, DEVS * EXTRA), BF16),
            pltpu.VMEM((DEVS * EXTRA, TOK), BF16),
            pltpu.VMEM((2 * PLANES + PLANE // 2, 128, 128), F32),
            *sorted_rows,
            pltpu.VMEM((TOK, 4 * HD), F32),
            *work,
            pltpu.SemaphoreType.DMA((13,)),
            *by_plane,
            pltpu.SemaphoreType.DMA((7,)),
        ],
        compiler_params=params(0),
    )(*args)

    outs = lax.cond(
        flag[0, 0] > 0.0, lambda args, outs: general(*args), lambda args, outs: outs, args, tuple(outs)
    )
    outs = pl.pallas_call(
        hand_over, out_shape=out_shape, in_specs=[vmem] * 5, out_specs=(vmem,) * 5
    )(*outs)
    return outs[0], outs[1], outs[2], outs[3], outs[4][None]


def solution(mesh):
    return jax.shard_map(
        shards,
        mesh=mesh,
        in_specs=(
            P(("dp", "seq"), None),
            P(("dp", "seq"), None),
            P(("dp", "seq"), None),
            P(("dp", "seq"), None),
            P("dp", "seq"),
            P("dp", None),
            P("dp", "seq", None),
        ),
        out_specs=(
            P(("dp", "seq"), None),
            P(("dp", "seq"), None),
            P(("dp", "seq"), None),
            P(("dp", "seq"), None),
            P("dp", "seq", None),
        ),
        check_vma=False,
    )
```

```python
import functools
import math

import jax
import jax.numpy as jnp
from jax import lax
from jax.experimental import pallas as pl
from jax.experimental.pallas import tpu as pltpu
from jax.sharding import PartitionSpec as P

MESH = pl.DeviceIdType.MESH
HD = 128
CL_DEV = 16
TOK = 1024
DEVS = 64
ROOM = 32
PLANE = 8
PLANES = DEVS // PLANE
CHUNK = PLANE * ROOM
BLOCKS = TOK // 128
ORDER = (4, 3, 5, 2, 6, 1, 7, 0)
SEATS = 24
EXTRA = 8
PARTS = 4
BF16 = jnp.bfloat16
F32 = jnp.float32


def dot(a, b):
    return jnp.dot(a, b, preferred_element_type=F32)


def dot_nt(a, b):
    return lax.dot_general(a, b, (((1,), (1,)), ((), ())), preferred_element_type=F32)


def dot_tn(a, b):
    return lax.dot_general(a, b, (((0,), (0,)), ((), ())), preferred_element_type=F32)


def iota(shape, dim):
    return lax.broadcasted_iota(jnp.int32, shape, dim).astype(F32)


def onehot(mask):
    return jnp.where(mask, 1.0, 0.0).astype(BF16)


def prefix_and_total():
    row = lax.broadcasted_iota(jnp.int32, (128, 256), 0)
    col = lax.broadcasted_iota(jnp.int32, (128, 256), 1)
    return onehot((row < col) | (col >= 128))


def token_slots(cluster_id, owner):
    ident = cluster_id[...]
    low = onehot(lax.broadcasted_iota(jnp.int32, (128, TOK), 0) == lax.rem(ident, 128))
    table = jnp.concatenate([owner[:, 128 * b : 128 * (b + 1)] for b in range(8)], axis=0)
    table_dev = lax.div(table, CL_DEV)
    table_loc = table - table_dev * CL_DEV
    tables = jnp.concatenate([table_dev, table_loc], axis=0).astype(F32).astype(BF16)
    found = dot(tables, low)
    high = lax.broadcasted_iota(jnp.int32, (8, TOK), 0) == lax.div(ident, 128)
    target = jnp.sum(jnp.where(high, found[:8], 0.0), axis=0, keepdims=True)
    local = jnp.sum(jnp.where(high, found[8:], 0.0), axis=0, keepdims=True)
    device = iota((DEVS, 128), 0)
    members = [device == target[:, 128 * b : 128 * (b + 1)] for b in range(BLOCKS)]
    counted = dot(jnp.concatenate([onehot(m) for m in members], axis=0), prefix_and_total())
    running = jnp.zeros((DEVS, 128), F32)
    ranks = []
    for b in range(BLOCKS):
        part = counted[DEVS * b : DEVS * (b + 1)]
        ranks.append(
            jnp.sum(jnp.where(members[b], part[:, :128] + running, 0.0), axis=0, keepdims=True)
        )
        running = running + part[:, 128:]
    rank = jnp.concatenate(ranks, axis=1)
    return target, local, rank


def turned(rows):
    n = rows.shape[0]
    return jnp.concatenate([rows, jnp.zeros((128 - n, 128), F32)], axis=0).T


def sorted_places(ids):
    hits = [ids == float(c + 1) for c in range(CL_DEV)]
    counted = dot(jnp.concatenate([onehot(h) for h in hits], axis=0), prefix_and_total())
    n = CL_DEV * 16
    below = onehot(
        lax.broadcasted_iota(jnp.int32, (n, n), 1) < lax.broadcasted_iota(jnp.int32, (n, n), 0)
    )
    offsets = dot(below, counted[:, 128:].astype(BF16))
    inside = counted[:, :128] + offsets
    place = jnp.full((16, 128), 4096.0, F32)
    starts = []
    for c in range(CL_DEV):
        place = jnp.where(hits[c], inside[16 * c : 16 * (c + 1)], place)
        starts.append(offsets[16 * c : 16 * c + 1])
    return place, starts


def plane_rows(place, p):
    at = lax.broadcasted_iota(jnp.int32, (16, 128), 0)
    return [
        jnp.sum(jnp.where(at == 2 * p + h, place, 0.0), axis=0, keepdims=True) for h in range(2)
    ]


def plane_cols(cols, p):
    at = lax.broadcasted_iota(jnp.int32, (128, 128), 1)
    return [jnp.sum(jnp.where(at == 2 * p + h, cols, 0.0), axis=1, keepdims=True) for h in range(2)]


def kernel(
    q_ref, k_ref, v_ref, g_ref, id_ref, owner_ref, old_ref,
    o_ref, dq_ref, dk_ref, dv_ref, cent_ref,
    smeta, rmeta, sqk, rqk, sv, rv, sg, rg, sa, ra, sd, rd,
    gather, ungather, final, xqk, xv, xg, acc, probs_ref, res,
    column_sem, send_sem, meta_sem, qk_sem, v_sem, g_sem, a_sem, d_sem,
):
    me = lax.axis_index("seq")
    my_plane = me // PLANE
    my_place = lax.rem(me, PLANE)
    scale = 1.0 / math.sqrt(HD)

    def peer_at(k, j):
        return lax.rem(my_plane + k, PLANES) * PLANE + lax.rem(my_place + j, PLANE)

    def signal(sem, k, j):
        pl.semaphore_signal(
            sem, inc=1, device_id={"seq": peer_at(k, j)}, device_id_type=MESH
        )

    barrier = pltpu.get_barrier_semaphore()
    for k in ORDER[:-1]:
        signal(barrier, k, 0)
    for j in range(1, PLANE):
        signal(barrier, 0, j)

    kinds = {
        "meta": (0, smeta, rmeta, meta_sem),
        "qk": (1, sqk, rqk, qk_sem),
        "v": (2, sv, rv, v_sem),
        "g": (3, sg, rg, g_sem),
        "a": (4, sa, ra, a_sem),
        "d": (5, sd, rd, d_sem),
    }

    def start(kind, k, first, last):
        index, src, dst, sem = kinds[kind]

        def body(j, carry):
            peer = peer_at(k, j)
            pltpu.make_async_remote_copy(
                src_ref=src.at[peer], dst_ref=dst.at[me], send_sem=send_sem.at[index],
                recv_sem=sem.at[my_plane], device_id={"seq": peer}, device_id_type=MESH,
            ).start()
            return carry

        lax.fori_loop(first, last, body, 0)

    def start_plane(kind, k):
        start(kind, k, 1 if k == 0 else 0, PLANE)

    def arrived(kind, k):
        _, _, dst, sem = kinds[kind]
        p = lax.rem(my_plane + k, PLANES)
        some = dst.at[pl.ds(p * PLANE, PLANE - 1 if k == 0 else PLANE)]
        pltpu.make_async_copy(some, some, sem.at[p]).wait()
        return p

    def sent(kind):
        index, src, _, _ = kinds[kind]
        some = src.at[pl.ds(0, DEVS - 1)]
        pltpu.make_async_copy(some, some, send_sem.at[index]).wait()

    def keep_own(kind):
        _, src, dst, _ = kinds[kind]
        dst[me] = src[me]

    def plane_of(ref, p):
        block = ref[pl.ds(p * PLANE, PLANE)]
        return block.reshape(CHUNK, block.shape[-1])

    def put_plane(ref, p, value):
        ref[pl.ds(p * PLANE, PLANE)] = value.astype(BF16).reshape(PLANE, ROOM, value.shape[-1])

    target, local, rank = token_slots(id_ref, owner_ref)
    slot = target * float(ROOM) + rank
    rows = jnp.concatenate([q_ref[...], k_ref[...], v_ref[...], g_ref[...]], axis=1)

    def fill(p, carry):
        pick = onehot(iota((CHUNK, TOK), 0) + (p * CHUNK).astype(F32) == slot)
        block = dot(pick, rows)
        put_plane(sqk, p, block[:, : 2 * HD])
        put_plane(sv, p, block[:, 2 * HD : 3 * HD])
        put_plane(sg, p, block[:, 3 * HD :])
        return carry

    lax.fori_loop(0, PLANES, fill, 0)

    quarter = (lax.rem(me, 4) * ROOM).astype(F32)
    lane_of = onehot(iota((128, TOK), 0) == rank + quarter)
    labels = jnp.where(iota((DEVS, TOK), 0) == target, local + 1.0, 0.0).astype(BF16)
    smeta[...] = dot_nt(labels, lane_of).reshape(DEVS, 1, 128)

    pl.semaphore_wait(barrier, 2 * PLANE - 2)
    for k in ORDER[:-1]:
        signal(column_sem, k, 0)
    for k in ORDER[:-1]:
        start("qk", k, 0, 1)
    pl.semaphore_wait(column_sem, PLANE - 1)
    for k in ORDER:
        start("qk", k, 1, PLANE)
    for kind in ("meta", "v", "g"):
        for k in ORDER:
            start_plane(kind, k)
    for kind in ("meta", "qk", "v", "g"):
        keep_own(kind)

    slot_cols = turned(jnp.concatenate([slot[:, 128 * b : 128 * (b + 1)] for b in range(8)], axis=0))
    slot_cols = [slot_cols[:, b : b + 1] for b in range(BLOCKS)]

    def build_final(p, carry):
        slot_at = iota((128, CHUNK), 1) + (p * CHUNK).astype(F32)
        final[p] = onehot(jnp.concatenate([slot_at == col for col in slot_cols], axis=0))
        return carry

    lax.fori_loop(0, PLANES, build_final, 0)

    for k in ORDER:
        arrived("meta", (PLANES - k) % PLANES)
    ids = jnp.sum(rmeta[...].reshape(16, 4, 128), axis=1)
    place, starts = sorted_places(ids)
    place_cols = turned(place)

    def build(p, carry):
        rows_of = plane_rows(place, p)
        gather[p] = onehot(jnp.concatenate([iota((TOK, 128), 0) == r for r in rows_of], axis=1))
        cols_of = plane_cols(place_cols, p)
        ungather[p] = onehot(jnp.concatenate([iota((128, TOK), 1) == c for c in cols_of], axis=0))
        return carry

    lax.fori_loop(0, PLANES, build, 0)

    at = iota((BLOCKS, 128), 0) * 128.0 + iota((BLOCKS, 128), 1)
    first = jnp.zeros((BLOCKS, 128), F32)
    for c in range(1, CL_DEV):
        first = jnp.where(at >= starts[c], starts[c], first)
    first_cols = turned(first)

    def collect(kind, matrix):
        _, _, dst, _ = kinds[kind]
        width = dst.shape[-1]
        for i, k in enumerate(ORDER):
            p = arrived(kind, (PLANES - k) % PLANES)
            part = dot(matrix[p], plane_of(dst, p))
            if i == PLANES - 1:
                return acc[:, :width] + part
            acc[:, :width] = part if i == 0 else acc[:, :width] + part

    front = pl.ds(0, 128)
    body = pl.ds(128, TOK)
    xqk[front] = jnp.zeros((128, 2 * HD), BF16)
    xv[front] = jnp.zeros((128, HD), BF16)

    xqk[body] = collect("qk", gather).astype(BF16)
    for b in range(BLOCKS):
        query = xqk[pl.ds(128 * (b + 1), 128), :HD]
        keys = xqk[pl.ds(128 * b, 256), HD:]
        scores = dot_nt(query, keys) * scale
        key_at = iota((128, 256), 1) + 128.0 * (b - 1)
        query_at = iota((128, 256), 0) + 128.0 * b
        allowed = (key_at <= query_at) & (key_at >= first_cols[:, b : b + 1])
        scores = jnp.where(allowed, scores, -1e30)
        weights = jnp.exp(scores - jnp.max(scores, axis=-1, keepdims=True))
        probs_ref[b] = weights / jnp.sum(weights, axis=-1, keepdims=True)

    start_rows = jnp.concatenate(starts, axis=0)
    end_rows = jnp.concatenate(starts[1:] + [jnp.full((1, 128), float(TOK), F32)], axis=0)
    sums = jnp.zeros((CL_DEV, HD), F32)
    for b in range(BLOCKS):
        row_at = iota((CL_DEV, 128), 1) + 128.0 * b
        owned = onehot((row_at >= start_rows) & (row_at < end_rows))
        sums = sums + dot(owned, xqk[pl.ds(128 * (b + 1), 128), HD:])
    blended = 0.5 * old_ref[...] + 0.5 * sums / (end_rows - start_rows)
    power = jnp.mean(blended * blended, axis=-1, keepdims=True)
    cent_ref[...] = blended * lax.rsqrt(power + 1e-6)

    xv[body] = collect("v", gather).astype(BF16)
    attn = [
        dot(probs_ref[b].astype(BF16), xv[pl.ds(128 * b, 256)]).astype(BF16) for b in range(BLOCKS)
    ]
    outs = jnp.concatenate(attn, axis=0)
    res[:, :HD] = outs
    for k in ORDER:
        p = lax.rem(my_plane + k, PLANES)
        put_plane(sa, p, dot(ungather[p], outs))
        start_plane("a", k)
    keep_own("a")

    xg[...] = collect("g", gather).astype(BF16)
    key_tail, value_tail = None, None
    for b in range(BLOCKS):
        mine = pl.ds(128 * b, 128)
        window = pl.ds(128 * b, 256)
        query = xqk[pl.ds(128 * (b + 1), 128), :HD]
        keys = xqk[window, HD:]
        grad = xg[mine]
        probs = probs_ref[b]
        delta = jnp.sum(
            grad.astype(F32) * res[mine, :HD].astype(F32), axis=-1, keepdims=True
        )
        dprobs = dot_nt(grad, xv[window])
        dscores = (probs * (dprobs - delta) * scale).astype(BF16)
        res[mine, HD : 2 * HD] = dot(dscores, keys).astype(BF16)
        dkeys = dot_tn(dscores, query)
        dvals = dot_tn(probs.astype(BF16), grad)
        if b > 0:
            before = pl.ds(128 * (b - 1), 128)
            res[before, 2 * HD : 3 * HD] = (key_tail + dkeys[:128]).astype(BF16)
            res[before, 3 * HD :] = (value_tail + dvals[:128]).astype(BF16)
        key_tail, value_tail = dkeys[128:], dvals[128:]
    last = pl.ds(128 * (BLOCKS - 1), 128)
    res[last, 2 * HD : 3 * HD] = key_tail.astype(BF16)
    res[last, 3 * HD :] = value_tail.astype(BF16)

    grads = res[:, HD:]
    for k in ORDER:
        p = lax.rem(my_plane + k, PLANES)
        put_plane(sd, p, dot(ungather[p], grads))
        start_plane("d", k)
    keep_own("d")
    for kind in ("meta", "qk", "v", "g"):
        sent(kind)

    o_ref[...] = collect("a", final).astype(BF16)
    sent("a")
    found = collect("d", final).astype(BF16)
    dq_ref[...] = found[:, :HD]
    dk_ref[...] = found[:, HD : 2 * HD]
    dv_ref[...] = found[:, 2 * HD :]
    sent("d")


def seated_rank(seats, member):
    n = seats
    counted = dot(jnp.concatenate([onehot(m) for m in member], axis=0), prefix_and_total())
    running = jnp.zeros((n, 128), F32)
    ranks = []
    for b in range(BLOCKS):
        part = counted[n * b : n * (b + 1)]
        ranks.append(
            jnp.sum(jnp.where(member[b], part[:, :128] + running, 0.0), axis=0, keepdims=True)
        )
        running = running + part[:, 128:]
    return jnp.concatenate(ranks, axis=1)


def split_features(block, rows):
    f = block.shape[1] // HD
    return [block[:, HD * j : HD * (j + 1)].reshape(-1, rows, HD) for j in range(f)]


def kernel_fast(
    q_ref, k_ref, v_ref, g_ref, id_ref, owner_ref, old_ref,
    o_ref, dq_ref, dk_ref, dv_ref, cent_ref, flag_ref,
    rows_in, load_sem, smeta, rmeta, smx, rmx, sx, rx, sbuf, rbuf, sa, ra, sc, rc, sd, rd, sy, ry, sw, rw, sflag, rflag,
    gather, ungather, final, xgather, xungather, wide, xqk, xv, xg, acc, probs_ref, res,
    column_sem, send_sem, meta_sem, qk_sem, v_sem, g_sem, a_sem, c_sem, d_sem, one_sem,
):
    me = lax.axis_index("seq")
    my_part = lax.axis_index("dp")
    my_plane = me // PLANE
    my_place = lax.rem(me, PLANE)
    scale = 1.0 / math.sqrt(HD)
    UNIT = 65536.0
    NONE = 8388608.0

    def peer_at(k, j):
        return lax.rem(my_plane + k, PLANES) * PLANE + lax.rem(my_place + j, PLANE)

    def part_at(i):
        return lax.rem(my_part + i, PARTS)

    def signal(sem, k, j):
        pl.semaphore_signal(sem, inc=1, device_id={"seq": peer_at(k, j)}, device_id_type=MESH)

    loads = [
        pltpu.make_async_copy(ref, rows_in.at[:, pl.ds(HD * f, HD)], load_sem.at[f])
        for f, ref in enumerate((q_ref, k_ref, v_ref, g_ref))
    ]
    for load in loads:
        load.start()
    barrier = pltpu.get_barrier_semaphore()
    for k in ORDER[:-1]:
        signal(barrier, k, 0)
    for j in range(1, PLANE):
        signal(barrier, 0, j)
    for i in range(1, PARTS):
        pl.semaphore_signal(barrier, inc=1, device_id={"dp": part_at(i)}, device_id_type=MESH)

    kinds = {
        "meta": (0, smeta, rmeta, meta_sem, 0, 1),
        "qk": (1, sbuf, rbuf, qk_sem, 0, 2 * SEATS),
        "v": (2, sbuf, rbuf, v_sem, 2 * SEATS, 32),
        "g": (3, sbuf, rbuf, g_sem, 2 * SEATS + 32, 16),
        "a": (4, sa, ra, a_sem, 0, 16),
        "c": (13, sc, rc, c_sem, 0, 2 * SEATS - 16),
        "d": (5, sd, rd, d_sem, 0, 2 * SEATS),
    }

    def start(kind, k, first, last):
        index, src, dst, sem, low, count = kinds[kind]
        some = pl.ds(low, count)

        def body(j, carry):
            peer = peer_at(k, j)
            pltpu.make_async_remote_copy(
                src_ref=src.at[peer, some], dst_ref=dst.at[me, some],
                send_sem=send_sem.at[index], recv_sem=sem.at[my_plane],
                device_id={"seq": peer}, device_id_type=MESH,
            ).start()
            return carry

        lax.fori_loop(first, last, body, 0)

    def start_plane(kind, k):
        start(kind, k, 1 if k == 0 else 0, PLANE)

    def arrived(kind, k):
        _, _, dst, sem, low, count = kinds[kind]
        p = lax.rem(my_plane + k, PLANES)
        some = dst.at[pl.ds(p * PLANE, PLANE - 1 if k == 0 else PLANE), pl.ds(low, count)]
        pltpu.make_async_copy(some, some, sem.at[p]).wait()
        return p

    def sent(kind):
        index, src, _, _, low, count = kinds[kind]
        some = src.at[pl.ds(0, DEVS - 1), pl.ds(low, count)]
        pltpu.make_async_copy(some, some, send_sem.at[index]).wait()

    ones = {
        "x": (6, sx, rx.at[my_place], 0),
        "mx": (7, smx, rmx.at[my_place], 1),
        "fx": (8, rx, rx, 2),
        "fm": (9, rmx, rmx, 3),
        "y": (10, sy, ry, 4),
        "w": (11, sw, rw, 5),
        "flag": (12, sflag, rflag, 6),
    }

    def column(kind):
        index, src, dst, sem = ones[kind]
        for k in ORDER[:-1]:
            p = lax.rem(my_plane + k, PLANES)
            pltpu.make_async_remote_copy(
                src_ref=src.at[p], dst_ref=dst.at[my_plane], send_sem=send_sem.at[index],
                recv_sem=one_sem.at[sem], device_id={"seq": peer_at(k, 0)}, device_id_type=MESH,
            ).start()

    def across(kind, forward, first=0, last=PLANES):
        index, src, dst, sem = ones[kind]
        some = pl.ds(first, last - first)
        for j in range(1, PLANE):
            seat = lax.rem(my_place + j, PLANE)
            pltpu.make_async_remote_copy(
                src_ref=src.at[my_place if forward else seat, some],
                dst_ref=dst.at[my_place, some],
                send_sem=send_sem.at[index], recv_sem=one_sem.at[sem],
                device_id={"seq": peer_at(0, j)}, device_id_type=MESH,
            ).start()

    def one_wait(kind, n, sending):
        index, src, dst, sem = ones[kind]
        some = (src if sending else dst).at[pl.ds(0, n)]
        pltpu.make_async_copy(
            some, some, send_sem.at[index] if sending else one_sem.at[sem]
        ).wait()

    target, local, rank = token_slots(id_ref, owner_ref)
    plane_row = jnp.floor(target * (1.0 / PLANE))
    seat_row = target - plane_row * float(PLANE)
    direct = rank < float(SEATS)
    slot = jnp.where(direct, target * float(SEATS) + rank, -1.0)
    member = [
        (iota((PLANES, 128), 0) == plane_row[:, 128 * b : 128 * (b + 1)])
        & (rank[:, 128 * b : 128 * (b + 1)] >= float(SEATS))
        for b in range(BLOCKS)
    ]
    extra = seated_rank(PLANES, member)
    fits = (rank >= float(SEATS)) & (extra < float(EXTRA))
    xslot = jnp.where(fits, plane_row * float(EXTRA) + extra, -1.0)
    lost = jnp.max(jnp.where(extra >= float(EXTRA), 1.0, 0.0), axis=1, keepdims=True)

    for load in loads:
        load.wait()
    rows = rows_in[...]

    def fill(k):
        p = lax.rem(my_plane + k, PLANES)
        pick = onehot(iota((PLANE * SEATS, TOK), 0) + (p * PLANE * SEATS).astype(F32) == slot)
        parts = split_features(dot(pick, rows), SEATS)
        sbuf[pl.ds(p * PLANE, PLANE)] = jnp.concatenate(parts, axis=1).astype(BF16)

    fill(ORDER[0])
    pl.semaphore_wait(barrier, 2 * PLANE - 2 + PARTS - 1)
    for k in ORDER[:-1]:
        signal(column_sem, k, 0)
    for i, k in enumerate(ORDER[:-1]):
        for kind in ("qk", "v", "g"):
            start(kind, k, 0, 1)
        fill(ORDER[i + 1])
    block = dot(onehot(iota((PLANES * EXTRA, TOK), 0) == xslot), rows)
    sx[...] = jnp.concatenate(split_features(block, EXTRA), axis=1).astype(BF16)
    column("x")
    rx[my_place, my_plane] = sx[my_plane]

    when = iota((1, TOK), 1)
    when_high = jnp.floor(when * (1.0 / 32))
    when_low = when - 32.0 * when_high
    here = (me * TOK).astype(F32)

    def keys_of(rows_at, label, lanes_at):
        n = rows_at.shape[0]
        stack = [jnp.where(rows_at, r, 0.0) for r in (label, when_high, when_low)]
        found = dot_nt(jnp.concatenate(stack, axis=0).astype(BF16), onehot(lanes_at))
        label = found[:n]
        key = label * UNIT + 32.0 * found[n : 2 * n] + found[2 * n :]
        return key + jnp.where(label > 0.0, here, 0.0)

    lane = jnp.where(direct, rank + (my_place * SEATS).astype(F32), -1.0)
    key = keys_of(iota((DEVS, TOK), 0) == target, local + 1.0, iota((256, TOK), 0) == lane)
    key = jnp.where(iota((DEVS, 256), 1) == 255.0, lost, key)
    smeta[...] = key.reshape(DEVS, 1, 256)
    first_lane = my_plane * EXTRA + lax.rem(my_place, 2) * 64
    lane = jnp.where(fits, extra + first_lane.astype(F32), -1.0)
    label = local + 1.0 + seat_row * float(CL_DEV)
    key = keys_of(iota((PLANES, TOK), 0) == plane_row, label, iota((128, TOK), 0) == lane)
    smx[...] = key.reshape(PLANES, 1, 128)

    column("mx")
    rmx[my_place, my_plane] = smx[my_plane]
    pl.semaphore_wait(column_sem, PLANE - 1)
    for k in ORDER:
        start_plane("meta", k)
    for k in ORDER[:3]:
        start("qk", k, 1, PLANE)
    rbuf[me] = sbuf[me]
    rmeta[me] = smeta[me]
    one_wait("x", PLANES - 1, False)
    one_wait("mx", PLANES - 1, False)
    across("fm", True)
    for k, first, last in zip(ORDER[3:], (0, 2, 4, 6, 7), (2, 4, 6, 7, 8)):
        start("qk", k, 1, PLANE)
        across("fx", True, first, last)
    for kind in ("v", "g"):
        for k in ORDER:
            start(kind, k, 1, PLANE)

    slot_cols = turned(jnp.concatenate([slot[:, 128 * b : 128 * (b + 1)] for b in range(8)], axis=0))
    slot_cols = [slot_cols[:, b : b + 1] for b in range(BLOCKS)]

    def build_final(p, carry):
        slot_at = iota((128, 256), 1) + (p * PLANE * SEATS).astype(F32)
        final[p] = onehot(jnp.concatenate([slot_at == col for col in slot_cols], axis=0))
        return carry

    lax.fori_loop(0, PLANES, build_final, 0)

    for k in ORDER:
        arrived("meta", (PLANES - k) % PLANES)
    got = jnp.sum(rmeta[...].reshape(PLANES, PLANE, 256), axis=1)
    lost_any = jnp.max(got[:, 255:256], axis=0, keepdims=True)
    sflag[0] = jnp.broadcast_to(lost_any, (1, 128))
    for i in range(1, PARTS):
        pltpu.make_async_remote_copy(
            src_ref=sflag.at[0], dst_ref=rflag.at[my_part], send_sem=send_sem.at[12],
            recv_sem=one_sem.at[6], device_id={"dp": part_at(i)}, device_id_type=MESH,
        ).start()
    rflag[my_part] = sflag[0]

    one_wait("fm", PLANE - 1, False)
    got_extra = jnp.sum(rmx[...].reshape(PLANE, PLANES, 128), axis=1)
    base = (my_place * CL_DEV).astype(F32) * UNIT
    got_extra = got_extra - base
    mine = (got_extra >= UNIT) & (got_extra < (1.0 + CL_DEV) * UNIT)
    got_extra = jnp.where(mine, got_extra, 0.0)
    got_extra = jnp.sum(got_extra.reshape(PLANE // 2, 2, 128), axis=1)
    tail = jnp.where(iota((PLANES, 128), 1) < 64.0, got[:, 128:], 0.0)
    keys_all = jnp.concatenate([got[:, :128], tail, got_extra], axis=0)
    keys_all = jnp.where(keys_all < UNIT, NONE, keys_all)
    key_cols = turned(keys_all)
    n_rows = 2 * PLANES + PLANE // 2
    for r in range(n_rows):
        wide[r] = jnp.broadcast_to(key_cols[:, r : r + 1], (128, 128))

    def count(r, sums):
        less = wide[r]
        out = []
        for c in range(n_rows):
            hit = jnp.where(less < keys_all[c : c + 1], 1.0, 0.0)
            out.append(sums[c] + jnp.sum(hit.reshape(16, 8, 128), axis=0))
        return tuple(out)

    zero = jnp.zeros((8, 128), F32)
    counts = lax.fori_loop(0, n_rows, count, (zero,) * n_rows)
    place = jnp.concatenate([jnp.sum(c, axis=0, keepdims=True) for c in counts], axis=0)
    place = jnp.where(keys_all == NONE, 4096.0, place)
    place_cols = turned(place)
    starts = [jnp.zeros((1, 128), F32)]
    for c in range(1, CL_DEV):
        below = jnp.where(keys_all < (1.0 + c) * UNIT, 1.0, 0.0)
        below = jnp.sum(jnp.sum(below, axis=0, keepdims=True), axis=1, keepdims=True)
        starts.append(jnp.broadcast_to(below, (1, 128)))

    def build(p, carry):
        at = lax.broadcasted_iota(jnp.int32, (n_rows, 128), 0)
        first, second = (
            jnp.sum(jnp.where(at == p + PLANES * h, place, 0.0), axis=0, keepdims=True)
            for h in range(2)
        )
        gather[p] = onehot(
            jnp.concatenate(
                [iota((TOK, 128), 0) == first, iota((TOK, 128), 0) == second], axis=1
            )
        )
        at = lax.broadcasted_iota(jnp.int32, (128, 128), 1)
        first, second = (
            jnp.sum(jnp.where(at == p + PLANES * h, place_cols, 0.0), axis=1, keepdims=True)
            for h in range(2)
        )
        ungather[p, 0:128] = onehot(iota((128, TOK), 1) == first)
        ungather[p, 128:192] = onehot(iota((64, TOK), 1) == second[:64])
        return carry

    lax.fori_loop(0, PLANES, build, 0)
    for u in range(PLANE // 2):
        r = 2 * PLANES + u
        xgather[:, 128 * u : 128 * (u + 1)] = onehot(iota((TOK, 128), 0) == place[r : r + 1])
        xungather[128 * u : 128 * (u + 1)] = onehot(iota((128, TOK), 1) == place_cols[:, r : r + 1])

    at = iota((BLOCKS, 128), 0) * 128.0 + iota((BLOCKS, 128), 1)
    first = jnp.zeros((BLOCKS, 128), F32)
    for c in range(1, CL_DEV):
        first = jnp.where(at >= starts[c], starts[c], first)
    first_cols = turned(first)

    def together(parts):
        return jnp.concatenate([p.reshape(-1, HD) for p in parts], axis=1).astype(BF16)

    def extras(ref, features):
        low = EXTRA * features[0] // 16 * 16
        block = ref[:, :, low : max(low + 16, EXTRA * (features[-1] + 1))].astype(F32)
        cuts = [block[:, :, EXTRA * f - low : EXTRA * (f + 1) - low] for f in features]
        return together(cuts)

    def collect(kind, features, cut):
        width = HD * len(features)
        acc[:, :width] = dot(xgather[...], extras(rx, features))
        for k in ORDER:
            p = arrived(kind, (PLANES - k) % PLANES)
            part = dot(gather[p, :, : PLANE * SEATS], together(cut(pl.ds(p * PLANE, PLANE))))
            if k == ORDER[-1]:
                return acc[:, :width] + part
            acc[:, :width] += part

    def cut_qk(at):
        block = rbuf[at, 0 : 2 * SEATS].astype(F32)
        return [block[:, :SEATS], block[:, SEATS:]]

    def cut_v(at):
        return [rbuf[at, 2 * SEATS : 2 * SEATS + 32].astype(F32)[:, :SEATS]]

    def cut_g(at):
        return [rbuf[at, 4 * SEATS - 32 : 4 * SEATS].astype(F32)[:, 32 - SEATS :]]

    front = pl.ds(0, 128)
    body = pl.ds(128, TOK)
    xqk[front] = jnp.zeros((128, 2 * HD), BF16)
    xv[front] = jnp.zeros((128, HD), BF16)

    one_wait("fx", PLANE - 1, False)
    xqk[body] = collect("qk", (0, 1), cut_qk).astype(BF16)
    for b in range(BLOCKS):
        query = xqk[pl.ds(128 * (b + 1), 128), :HD]
        keys = xqk[pl.ds(128 * b, 256), HD:]
        scores = dot_nt(query, keys) * scale
        key_at = iota((128, 256), 1) + 128.0 * (b - 1)
        query_at = iota((128, 256), 0) + 128.0 * b
        allowed = (key_at <= query_at) & (key_at >= first_cols[:, b : b + 1])
        scores = jnp.where(allowed, scores, -1e30)
        weights = jnp.exp(scores - jnp.max(scores, axis=-1, keepdims=True))
        probs_ref[b] = weights / jnp.sum(weights, axis=-1, keepdims=True)

    start_rows = jnp.concatenate(starts, axis=0)
    end_rows = jnp.concatenate(starts[1:] + [jnp.full((1, 128), float(TOK), F32)], axis=0)
    sums = jnp.zeros((CL_DEV, HD), F32)
    for b in range(BLOCKS):
        row_at = iota((CL_DEV, 128), 1) + 128.0 * b
        owned = onehot((row_at >= start_rows) & (row_at < end_rows))
        sums = sums + dot(owned, xqk[pl.ds(128 * (b + 1), 128), HD:])
    blended = 0.5 * old_ref[...] + 0.5 * sums / (end_rows - start_rows)
    power = jnp.mean(blended * blended, axis=-1, keepdims=True)
    cent_ref[...] = blended * lax.rsqrt(power + 1e-6)

    xv[body] = collect("v", (2,), cut_v).astype(BF16)
    attn = [
        dot(probs_ref[b].astype(BF16), xv[pl.ds(128 * b, 256)]).astype(BF16) for b in range(BLOCKS)
    ]
    outs = jnp.concatenate(attn, axis=0)
    res[:, :HD] = outs
    for k in ORDER:
        p = lax.rem(my_plane + k, PLANES)
        block = dot(ungather[p], outs).reshape(PLANE, SEATS, HD)
        sa[pl.ds(p * PLANE, PLANE)] = block[:, :16].astype(BF16)
        start_plane("a", k)
    ra[me] = sa[me]

    xg[...] = collect("g", (3,), cut_g).astype(BF16)
    value_tail = None
    for b in range(BLOCKS):
        dvals = dot_tn(probs_ref[b].astype(BF16), xg[pl.ds(128 * b, 128)])
        if b > 0:
            res[pl.ds(128 * (b - 1), 128), 3 * HD :] = (value_tail + dvals[:128]).astype(BF16)
        value_tail = dvals[128:]
    res[pl.ds(128 * (BLOCKS - 1), 128), 3 * HD :] = value_tail.astype(BF16)

    for k in ORDER:
        p = lax.rem(my_plane + k, PLANES)
        parts = [
            dot(ungather[p], res[:, at]).reshape(PLANE, SEATS, HD)
            for at in (slice(0, HD), slice(3 * HD, 4 * HD))
        ]
        block = jnp.concatenate([parts[0][:, 16:], parts[1]], axis=1).astype(BF16)
        sc[pl.ds(p * PLANE, PLANE)] = block
        start_plane("c", k)

    key_tail = None
    for b in range(BLOCKS):
        mine = pl.ds(128 * b, 128)
        window = pl.ds(128 * b, 256)
        query = xqk[pl.ds(128 * (b + 1), 128), :HD]
        keys = xqk[window, HD:]
        grad = xg[mine]
        probs = probs_ref[b]
        delta = jnp.sum(grad.astype(F32) * res[mine, :HD].astype(F32), axis=-1, keepdims=True)
        dprobs = dot_nt(grad, xv[window])
        dscores = (probs * (dprobs - delta) * scale).astype(BF16)
        res[mine, HD : 2 * HD] = dot(dscores, keys).astype(BF16)
        dkeys = dot_tn(dscores, query)
        if b > 0:
            before = pl.ds(128 * (b - 1), 128)
            res[before, 2 * HD : 3 * HD] = (key_tail + dkeys[:128]).astype(BF16)
        key_tail = dkeys[128:]
    last = pl.ds(128 * (BLOCKS - 1), 128)
    res[last, 2 * HD : 3 * HD] = key_tail.astype(BF16)

    for i, k in enumerate(ORDER):
        if i == 2:
            back = dot(xungather[...], res[...])
            back = [
                back[:, HD * f : HD * (f + 1)].reshape(PLANE, PLANES, EXTRA, HD) for f in range(4)
            ]
            sy[...] = jnp.concatenate(back, axis=2).astype(BF16)
            ry[my_place] = sy[my_place]
        p = lax.rem(my_plane + k, PLANES)
        parts = split_features(dot(ungather[p], res[:, HD : 3 * HD]), SEATS)
        block = jnp.concatenate(parts, axis=1).astype(BF16)
        sd[pl.ds(p * PLANE, PLANE)] = block
        start_plane("d", k)
        if 2 <= i < 6:
            across("y", False, 2 * i - 4, 2 * i - 2)
    rc[me] = sc[me]
    rd[me] = sd[me]
    one_wait("y", PLANE - 1, False)
    sw[...] = jnp.sum(ry[...].astype(F32), axis=0).astype(BF16)
    column("w")
    rw[my_plane] = sw[my_plane]

    for kind in ("meta", "qk", "v", "g", "a", "c"):
        sent(kind)
    for kind, n in (("x", 7), ("mx", 7), ("fx", 7), ("fm", 7), ("y", 7)):
        one_wait(kind, n, True)

    one_wait("flag", PARTS - 1, False)
    flag_ref[...] = jnp.max(rflag[...], axis=0)
    one_wait("flag", PARTS - 1, True)

    def cut_back(at):
        head = ra[at].astype(F32)
        rest = rc[at].astype(F32)
        keys = rd[at].astype(F32)
        outs = jnp.concatenate([head, rest[:, : SEATS - 16]], axis=1)
        return [outs, keys[:, :SEATS], keys[:, SEATS:], rest[:, SEATS - 16 :]]

    for kind in ("a", "c"):
        for k in ORDER:
            arrived(kind, (PLANES - k) % PLANES)
    for k in ORDER:
        p = arrived("d", (PLANES - k) % PLANES)
        part = dot(final[p, :, : PLANE * SEATS], together(cut_back(pl.ds(p * PLANE, PLANE))))
        if k == ORDER[0]:
            acc[...] = part
        else:
            acc[...] += part
    xslot_cols = turned(
        jnp.concatenate([xslot[:, 128 * b : 128 * (b + 1)] for b in range(8)], axis=0)
    )
    pick = onehot(
        jnp.concatenate(
            [iota((128, PLANES * EXTRA), 1) == xslot_cols[:, b : b + 1] for b in range(BLOCKS)],
            axis=0,
        )
    )
    one_wait("w", PLANES - 1, False)
    block = rw[...].astype(F32)
    late = together([block[:, EXTRA * f : EXTRA * (f + 1)] for f in range(4)])
    found = (acc[...] + dot(pick, late)).astype(BF16)
    o_ref[...] = found[:, :HD]
    dq_ref[...] = found[:, HD : 2 * HD]
    dk_ref[...] = found[:, 2 * HD : 3 * HD]
    dv_ref[...] = found[:, 3 * HD :]
    sent("d")
    one_wait("w", 7, True)


def hand_over(*refs):
    n = len(refs) // 2
    for src, dst in zip(refs[:n], refs[n:]):
        dst[...] = src[...]


def shards(queries, key_rows, values, out_grad, cluster_id, cluster_owner, old_centroids):
    vmem = pl.BlockSpec(memory_space=pltpu.VMEM)
    row_out = jax.ShapeDtypeStruct((TOK, HD), BF16)
    out_shape = (row_out, row_out, row_out, row_out, jax.ShapeDtypeStruct((CL_DEV, HD), F32))
    by_plane = [pltpu.SemaphoreType.DMA((PLANES,))] * 7
    args = (queries, key_rows, values, out_grad, cluster_id, cluster_owner, old_centroids[0])

    def pair(rows, width, n=DEVS, dtype=BF16):
        return [pltpu.VMEM((n, rows, width), dtype)] * 2

    def params(ident):
        return pltpu.CompilerParams(
            collective_id=ident, has_side_effects=True, vmem_limit_bytes=56 << 20
        )

    sorted_rows = [
        pltpu.VMEM((TOK + 128, 2 * HD), BF16),
        pltpu.VMEM((TOK + 128, HD), BF16),
        pltpu.VMEM((TOK, HD), BF16),
    ]
    work = [
        pltpu.VMEM((BLOCKS, 128, 256), F32),
        pltpu.VMEM((TOK, 4 * HD), BF16),
        pltpu.SemaphoreType.REGULAR,
    ]

    def general(*args):
        return pl.pallas_call(
            kernel,
            out_shape=out_shape,
            in_specs=[vmem] * 7,
            out_specs=(vmem,) * 5,
            scratch_shapes=[
                *pair(1, 128, dtype=F32),
                *pair(ROOM, 2 * HD), *pair(ROOM, HD), *pair(ROOM, HD),
                *pair(ROOM, HD), *pair(ROOM, 3 * HD),
                pltpu.VMEM((PLANES, TOK, CHUNK), BF16),
                pltpu.VMEM((PLANES, CHUNK, TOK), BF16),
                pltpu.VMEM((PLANES, TOK, CHUNK), BF16),
                *sorted_rows,
                pltpu.VMEM((TOK, 3 * HD), F32),
                *work,
                pltpu.SemaphoreType.DMA((6,)),
                *by_plane[:6],
            ],
            compiler_params=params(1),
        )(*args)

    extra_rows = pltpu.VMEM((PLANE, PLANES, 4 * EXTRA, HD), BF16)
    *outs, flag = pl.pallas_call(
        kernel_fast,
        out_shape=out_shape + (jax.ShapeDtypeStruct((1, 128), F32),),
        in_specs=[pl.BlockSpec(memory_space=pl.ANY)] * 4 + [vmem] * 3,
        out_specs=(vmem,) * 6,
        scratch_shapes=[
            pltpu.VMEM((TOK, 4 * HD), BF16),
            pltpu.SemaphoreType.DMA((4,)),
            *pair(1, 256, dtype=F32),
            pltpu.VMEM((PLANES, 1, 128), F32),
            pltpu.VMEM((PLANE, PLANES, 1, 128), F32),
            pltpu.VMEM((PLANES, 4 * EXTRA, HD), BF16),
            extra_rows,
            *pair(4 * SEATS, HD), *pair(16, HD),
            *pair(2 * SEATS - 16, HD), *pair(2 * SEATS, HD),
            extra_rows, extra_rows,
            *pair(4 * EXTRA, HD, PLANES),
            *pair(1, 128, PARTS, F32),
            pltpu.VMEM((PLANES, TOK, 256), BF16),
            pltpu.VMEM((PLANES, PLANE * SEATS, TOK), BF16),
            pltpu.VMEM((PLANES, TOK, 256), BF16),
            pltpu.VMEM((TOK, DEVS * EXTRA), BF16),
            pltpu.VMEM((DEVS * EXTRA, TOK), BF16),
            pltpu.VMEM((2 * PLANES + PLANE // 2, 128, 128), F32),
            *sorted_rows,
            pltpu.VMEM((TOK, 4 * HD), F32),
            *work,
            pltpu.SemaphoreType.DMA((14,)),
            *by_plane,
            pltpu.SemaphoreType.DMA((7,)),
        ],
        compiler_params=params(0),
    )(*args)

    outs = lax.cond(
        flag[0, 0] > 0.0, lambda args, outs: general(*args), lambda args, outs: outs, args, tuple(outs)
    )
    outs = pl.pallas_call(
        hand_over, out_shape=out_shape, in_specs=[vmem] * 5, out_specs=(vmem,) * 5
    )(*outs)
    return outs[0], outs[1], outs[2], outs[3], outs[4][None]


def solution(mesh):
    return jax.shard_map(
        shards,
        mesh=mesh,
        in_specs=(
            P(("dp", "seq"), None),
            P(("dp", "seq"), None),
            P(("dp", "seq"), None),
            P(("dp", "seq"), None),
            P("dp", "seq"),
            P("dp", None),
            P("dp", "seq", None),
        ),
        out_specs=(
            P(("dp", "seq"), None),
            P(("dp", "seq"), None),
            P(("dp", "seq"), None),
            P(("dp", "seq"), None),
            P("dp", "seq", None),
        ),
        check_vma=False,
    )
```

```python
import functools
import math

import jax
import jax.numpy as jnp
from jax import lax
from jax.experimental import pallas as pl
from jax.experimental.pallas import tpu as pltpu
from jax.sharding import PartitionSpec as P

MESH = pl.DeviceIdType.MESH
HD = 128
CL_DEV = 16
TOK = 1024
DEVS = 64
ROOM = 32
PLANE = 8
PLANES = DEVS // PLANE
CHUNK = PLANE * ROOM
BLOCKS = TOK // 128
ORDER = (4, 3, 5, 2, 6, 1, 7, 0)
LATE = (4, 3, 5, 0, 2, 6, 1, 7)
SEATS = 24
EXTRA = 8
PARTS = 4
BF16 = jnp.bfloat16
F32 = jnp.float32


def dot(a, b):
    return jnp.dot(a, b, preferred_element_type=F32)


def dot_nt(a, b):
    return lax.dot_general(a, b, (((1,), (1,)), ((), ())), preferred_element_type=F32)


def dot_tn(a, b):
    return lax.dot_general(a, b, (((0,), (0,)), ((), ())), preferred_element_type=F32)


def iota(shape, dim):
    return lax.broadcasted_iota(jnp.int32, shape, dim).astype(F32)


def onehot(mask):
    return jnp.where(mask, 1.0, 0.0).astype(BF16)


def prefix_and_total():
    row = lax.broadcasted_iota(jnp.int32, (128, 256), 0)
    col = lax.broadcasted_iota(jnp.int32, (128, 256), 1)
    return onehot((row < col) | (col >= 128))


def token_slots(cluster_id, owner):
    ident = cluster_id[...]
    low = onehot(lax.broadcasted_iota(jnp.int32, (128, TOK), 0) == lax.rem(ident, 128))
    table = jnp.concatenate([owner[:, 128 * b : 128 * (b + 1)] for b in range(8)], axis=0)
    table_dev = lax.div(table, CL_DEV)
    table_loc = table - table_dev * CL_DEV
    tables = jnp.concatenate([table_dev, table_loc], axis=0).astype(F32).astype(BF16)
    found = dot(tables, low)
    high = lax.broadcasted_iota(jnp.int32, (8, TOK), 0) == lax.div(ident, 128)
    target = jnp.sum(jnp.where(high, found[:8], 0.0), axis=0, keepdims=True)
    local = jnp.sum(jnp.where(high, found[8:], 0.0), axis=0, keepdims=True)
    device = iota((DEVS, 128), 0)
    members = [device == target[:, 128 * b : 128 * (b + 1)] for b in range(BLOCKS)]
    counted = dot(jnp.concatenate([onehot(m) for m in members], axis=0), prefix_and_total())
    running = jnp.zeros((DEVS, 128), F32)
    ranks = []
    for b in range(BLOCKS):
        part = counted[DEVS * b : DEVS * (b + 1)]
        ranks.append(
            jnp.sum(jnp.where(members[b], part[:, :128] + running, 0.0), axis=0, keepdims=True)
        )
        running = running + part[:, 128:]
    rank = jnp.concatenate(ranks, axis=1)
    return target, local, rank


def turned(rows):
    n = rows.shape[0]
    return jnp.concatenate([rows, jnp.zeros((128 - n, 128), F32)], axis=0).T


def sorted_places(ids):
    hits = [ids == float(c + 1) for c in range(CL_DEV)]
    counted = dot(jnp.concatenate([onehot(h) for h in hits], axis=0), prefix_and_total())
    n = CL_DEV * 16
    below = onehot(
        lax.broadcasted_iota(jnp.int32, (n, n), 1) < lax.broadcasted_iota(jnp.int32, (n, n), 0)
    )
    offsets = dot(below, counted[:, 128:].astype(BF16))
    inside = counted[:, :128] + offsets
    place = jnp.full((16, 128), 4096.0, F32)
    starts = []
    for c in range(CL_DEV):
        place = jnp.where(hits[c], inside[16 * c : 16 * (c + 1)], place)
        starts.append(offsets[16 * c : 16 * c + 1])
    return place, starts


def plane_rows(place, p):
    at = lax.broadcasted_iota(jnp.int32, (16, 128), 0)
    return [
        jnp.sum(jnp.where(at == 2 * p + h, place, 0.0), axis=0, keepdims=True) for h in range(2)
    ]


def plane_cols(cols, p):
    at = lax.broadcasted_iota(jnp.int32, (128, 128), 1)
    return [jnp.sum(jnp.where(at == 2 * p + h, cols, 0.0), axis=1, keepdims=True) for h in range(2)]


def kernel(
    q_ref, k_ref, v_ref, g_ref, id_ref, owner_ref, old_ref,
    o_ref, dq_ref, dk_ref, dv_ref, cent_ref,
    smeta, rmeta, sqk, rqk, sv, rv, sg, rg, sa, ra, sd, rd,
    gather, ungather, final, xqk, xv, xg, acc, probs_ref, res,
    column_sem, send_sem, meta_sem, qk_sem, v_sem, g_sem, a_sem, d_sem,
):
    me = lax.axis_index("seq")
    my_plane = me // PLANE
    my_place = lax.rem(me, PLANE)
    scale = 1.0 / math.sqrt(HD)

    def peer_at(k, j):
        return lax.rem(my_plane + k, PLANES) * PLANE + lax.rem(my_place + j, PLANE)

    def signal(sem, k, j):
        pl.semaphore_signal(
            sem, inc=1, device_id={"seq": peer_at(k, j)}, device_id_type=MESH
        )

    barrier = pltpu.get_barrier_semaphore()
    for k in ORDER[:-1]:
        signal(barrier, k, 0)
    for j in range(1, PLANE):
        signal(barrier, 0, j)

    kinds = {
        "meta": (0, smeta, rmeta, meta_sem),
        "qk": (1, sqk, rqk, qk_sem),
        "v": (2, sv, rv, v_sem),
        "g": (3, sg, rg, g_sem),
        "a": (4, sa, ra, a_sem),
        "d": (5, sd, rd, d_sem),
    }

    def start(kind, k, first, last):
        index, src, dst, sem = kinds[kind]

        def body(j, carry):
            peer = peer_at(k, j)
            pltpu.make_async_remote_copy(
                src_ref=src.at[peer], dst_ref=dst.at[me], send_sem=send_sem.at[index],
                recv_sem=sem.at[my_plane], device_id={"seq": peer}, device_id_type=MESH,
            ).start()
            return carry

        lax.fori_loop(first, last, body, 0)

    def start_plane(kind, k):
        start(kind, k, 1 if k == 0 else 0, PLANE)

    def arrived(kind, k):
        _, _, dst, sem = kinds[kind]
        p = lax.rem(my_plane + k, PLANES)
        some = dst.at[pl.ds(p * PLANE, PLANE - 1 if k == 0 else PLANE)]
        pltpu.make_async_copy(some, some, sem.at[p]).wait()
        return p

    def sent(kind):
        index, src, _, _ = kinds[kind]
        some = src.at[pl.ds(0, DEVS - 1)]
        pltpu.make_async_copy(some, some, send_sem.at[index]).wait()

    def keep_own(kind):
        _, src, dst, _ = kinds[kind]
        dst[me] = src[me]

    def plane_of(ref, p):
        block = ref[pl.ds(p * PLANE, PLANE)]
        return block.reshape(CHUNK, block.shape[-1])

    def put_plane(ref, p, value):
        ref[pl.ds(p * PLANE, PLANE)] = value.astype(BF16).reshape(PLANE, ROOM, value.shape[-1])

    target, local, rank = token_slots(id_ref, owner_ref)
    slot = target * float(ROOM) + rank
    rows = jnp.concatenate([q_ref[...], k_ref[...], v_ref[...], g_ref[...]], axis=1)

    def fill(p, carry):
        pick = onehot(iota((CHUNK, TOK), 0) + (p * CHUNK).astype(F32) == slot)
        block = dot(pick, rows)
        put_plane(sqk, p, block[:, : 2 * HD])
        put_plane(sv, p, block[:, 2 * HD : 3 * HD])
        put_plane(sg, p, block[:, 3 * HD :])
        return carry

    lax.fori_loop(0, PLANES, fill, 0)

    quarter = (lax.rem(me, 4) * ROOM).astype(F32)
    lane_of = onehot(iota((128, TOK), 0) == rank + quarter)
    labels = jnp.where(iota((DEVS, TOK), 0) == target, local + 1.0, 0.0).astype(BF16)
    smeta[...] = dot_nt(labels, lane_of).reshape(DEVS, 1, 128)

    pl.semaphore_wait(barrier, 2 * PLANE - 2)
    for k in ORDER[:-1]:
        signal(column_sem, k, 0)
    for k in ORDER[:-1]:
        start("qk", k, 0, 1)
    pl.semaphore_wait(column_sem, PLANE - 1)
    for k in ORDER:
        start("qk", k, 1, PLANE)
    for kind in ("meta", "v", "g"):
        for k in ORDER:
            start_plane(kind, k)
    for kind in ("meta", "qk", "v", "g"):
        keep_own(kind)

    slot_cols = turned(jnp.concatenate([slot[:, 128 * b : 128 * (b + 1)] for b in range(8)], axis=0))
    slot_cols = [slot_cols[:, b : b + 1] for b in range(BLOCKS)]

    def build_final(p, carry):
        slot_at = iota((128, CHUNK), 1) + (p * CHUNK).astype(F32)
        final[p] = onehot(jnp.concatenate([slot_at == col for col in slot_cols], axis=0))
        return carry

    lax.fori_loop(0, PLANES, build_final, 0)

    for k in ORDER:
        arrived("meta", (PLANES - k) % PLANES)
    ids = jnp.sum(rmeta[...].reshape(16, 4, 128), axis=1)
    place, starts = sorted_places(ids)
    place_cols = turned(place)

    def build(p, carry):
        rows_of = plane_rows(place, p)
        gather[p] = onehot(jnp.concatenate([iota((TOK, 128), 0) == r for r in rows_of], axis=1))
        cols_of = plane_cols(place_cols, p)
        ungather[p] = onehot(jnp.concatenate([iota((128, TOK), 1) == c for c in cols_of], axis=0))
        return carry

    lax.fori_loop(0, PLANES, build, 0)

    at = iota((BLOCKS, 128), 0) * 128.0 + iota((BLOCKS, 128), 1)
    first = jnp.zeros((BLOCKS, 128), F32)
    for c in range(1, CL_DEV):
        first = jnp.where(at >= starts[c], starts[c], first)
    first_cols = turned(first)

    def collect(kind, matrix):
        _, _, dst, _ = kinds[kind]
        width = dst.shape[-1]
        for i, k in enumerate(ORDER):
            p = arrived(kind, (PLANES - k) % PLANES)
            part = dot(matrix[p], plane_of(dst, p))
            if i == PLANES - 1:
                return acc[:, :width] + part
            acc[:, :width] = part if i == 0 else acc[:, :width] + part

    front = pl.ds(0, 128)
    body = pl.ds(128, TOK)
    xqk[front] = jnp.zeros((128, 2 * HD), BF16)
    xv[front] = jnp.zeros((128, HD), BF16)

    xqk[body] = collect("qk", gather).astype(BF16)
    for b in range(BLOCKS):
        query = xqk[pl.ds(128 * (b + 1), 128), :HD]
        keys = xqk[pl.ds(128 * b, 256), HD:]
        scores = dot_nt(query, keys) * scale
        key_at = iota((128, 256), 1) + 128.0 * (b - 1)
        query_at = iota((128, 256), 0) + 128.0 * b
        allowed = (key_at <= query_at) & (key_at >= first_cols[:, b : b + 1])
        scores = jnp.where(allowed, scores, -1e30)
        weights = jnp.exp(scores - jnp.max(scores, axis=-1, keepdims=True))
        probs_ref[b] = weights / jnp.sum(weights, axis=-1, keepdims=True)

    start_rows = jnp.concatenate(starts, axis=0)
    end_rows = jnp.concatenate(starts[1:] + [jnp.full((1, 128), float(TOK), F32)], axis=0)
    sums = jnp.zeros((CL_DEV, HD), F32)
    for b in range(BLOCKS):
        row_at = iota((CL_DEV, 128), 1) + 128.0 * b
        owned = onehot((row_at >= start_rows) & (row_at < end_rows))
        sums = sums + dot(owned, xqk[pl.ds(128 * (b + 1), 128), HD:])
    blended = 0.5 * old_ref[...] + 0.5 * sums / (end_rows - start_rows)
    power = jnp.mean(blended * blended, axis=-1, keepdims=True)
    cent_ref[...] = blended * lax.rsqrt(power + 1e-6)

    xv[body] = collect("v", gather).astype(BF16)
    attn = [
        dot(probs_ref[b].astype(BF16), xv[pl.ds(128 * b, 256)]).astype(BF16) for b in range(BLOCKS)
    ]
    outs = jnp.concatenate(attn, axis=0)
    res[:, :HD] = outs
    for k in ORDER:
        p = lax.rem(my_plane + k, PLANES)
        put_plane(sa, p, dot(ungather[p], outs))
        start_plane("a", k)
    keep_own("a")

    xg[...] = collect("g", gather).astype(BF16)
    key_tail, value_tail = None, None
    for b in range(BLOCKS):
        mine = pl.ds(128 * b, 128)
        window = pl.ds(128 * b, 256)
        query = xqk[pl.ds(128 * (b + 1), 128), :HD]
        keys = xqk[window, HD:]
        grad = xg[mine]
        probs = probs_ref[b]
        delta = jnp.sum(
            grad.astype(F32) * res[mine, :HD].astype(F32), axis=-1, keepdims=True
        )
        dprobs = dot_nt(grad, xv[window])
        dscores = (probs * (dprobs - delta) * scale).astype(BF16)
        res[mine, HD : 2 * HD] = dot(dscores, keys).astype(BF16)
        dkeys = dot_tn(dscores, query)
        dvals = dot_tn(probs.astype(BF16), grad)
        if b > 0:
            before = pl.ds(128 * (b - 1), 128)
            res[before, 2 * HD : 3 * HD] = (key_tail + dkeys[:128]).astype(BF16)
            res[before, 3 * HD :] = (value_tail + dvals[:128]).astype(BF16)
        key_tail, value_tail = dkeys[128:], dvals[128:]
    last = pl.ds(128 * (BLOCKS - 1), 128)
    res[last, 2 * HD : 3 * HD] = key_tail.astype(BF16)
    res[last, 3 * HD :] = value_tail.astype(BF16)

    grads = res[:, HD:]
    for k in ORDER:
        p = lax.rem(my_plane + k, PLANES)
        put_plane(sd, p, dot(ungather[p], grads))
        start_plane("d", k)
    keep_own("d")
    for kind in ("meta", "qk", "v", "g"):
        sent(kind)

    o_ref[...] = collect("a", final).astype(BF16)
    sent("a")
    found = collect("d", final).astype(BF16)
    dq_ref[...] = found[:, :HD]
    dk_ref[...] = found[:, HD : 2 * HD]
    dv_ref[...] = found[:, 2 * HD :]
    sent("d")


def seated_rank(seats, member):
    n = seats
    counted = dot(jnp.concatenate([onehot(m) for m in member], axis=0), prefix_and_total())
    running = jnp.zeros((n, 128), F32)
    ranks = []
    for b in range(BLOCKS):
        part = counted[n * b : n * (b + 1)]
        ranks.append(
            jnp.sum(jnp.where(member[b], part[:, :128] + running, 0.0), axis=0, keepdims=True)
        )
        running = running + part[:, 128:]
    return jnp.concatenate(ranks, axis=1)


def split_features(block, rows):
    f = block.shape[1] // HD
    return [block[:, HD * j : HD * (j + 1)].reshape(-1, rows, HD) for j in range(f)]


def kernel_fast(
    q_ref, k_ref, v_ref, g_ref, id_ref, owner_ref, old_ref,
    o_ref, dq_ref, dk_ref, dv_ref, cent_ref, flag_ref,
    rows_in, load_sem, smeta, rmeta, smx, rmx, sx, rx, sbuf, rbuf, sa, ra, sc, rc, sd, rd, sy, ry, sw, rw, sflag, rflag,
    gather, ungather, final, xgather, xungather, wide, xqk, xv, xg, acc, probs_ref, res,
    column_sem, send_sem, meta_sem, qk_sem, v_sem, g_sem, a_sem, c_sem, d_sem, one_sem,
):
    me = lax.axis_index("seq")
    my_part = lax.axis_index("dp")
    my_plane = me // PLANE
    my_place = lax.rem(me, PLANE)
    scale = 1.0 / math.sqrt(HD)
    UNIT = 65536.0
    NONE = 8388608.0

    def peer_at(k, j):
        return lax.rem(my_plane + k, PLANES) * PLANE + lax.rem(my_place + j, PLANE)

    def part_at(i):
        return lax.rem(my_part + i, PARTS)

    def signal(sem, k, j):
        pl.semaphore_signal(sem, inc=1, device_id={"seq": peer_at(k, j)}, device_id_type=MESH)

    rmeta[...] = jnp.zeros_like(rmeta)
    loads = [
        pltpu.make_async_copy(ref, rows_in.at[:, pl.ds(HD * f, HD)], load_sem.at[f])
        for f, ref in enumerate((q_ref, k_ref, v_ref, g_ref))
    ]
    for load in loads:
        load.start()
    barrier = pltpu.get_barrier_semaphore()
    for k in ORDER[:-1]:
        signal(barrier, k, 0)
    for j in range(1, PLANE):
        signal(barrier, 0, j)
    for i in range(1, PARTS):
        pl.semaphore_signal(barrier, inc=1, device_id={"dp": part_at(i)}, device_id_type=MESH)

    kinds = {
        "meta": (0, smeta, rmeta, meta_sem, 0, 1),
        "qk": (1, sbuf, rbuf, qk_sem, 0, 2 * SEATS),
        "v": (2, sbuf, rbuf, v_sem, 2 * SEATS, 32),
        "g": (3, sbuf, rbuf, g_sem, 2 * SEATS + 32, 16),
        "a": (4, sa, ra, a_sem, 0, 16),
        "c": (13, sc, rc, c_sem, 0, 2 * SEATS - 16),
        "d": (5, sd, rd, d_sem, 0, 2 * SEATS),
    }

    def start(kind, k, first, last):
        index, src, dst, sem, low, count = kinds[kind]
        some = pl.ds(low, count)

        half = pl.ds(pl.multiple_of(my_place // 4 * 128, 128), 128)

        def body(j, carry):
            peer = peer_at(k, j)
            key = kind == "meta"
            pltpu.make_async_remote_copy(
                src_ref=src.at[peer, some, half] if key else src.at[peer, some],
                dst_ref=dst.at[me, some, half] if key else dst.at[me, some],
                send_sem=send_sem.at[index], recv_sem=sem.at[my_plane],
                device_id={"seq": peer}, device_id_type=MESH,
            ).start()
            return carry

        lax.fori_loop(first, last, body, 0)

    def start_plane(kind, k):
        start(kind, k, 1 if k == 0 else 0, PLANE)

    def arrived(kind, k):
        _, _, dst, sem, low, count = kinds[kind]
        p = lax.rem(my_plane + k, PLANES)
        some = dst.at[pl.ds(p * PLANE, PLANE - 1 if k == 0 else PLANE), pl.ds(low, count)]
        if kind == "meta":
            some = some.at[:, :, pl.ds(0, 128)]
        pltpu.make_async_copy(some, some, sem.at[p]).wait()
        return p

    def sent(kind):
        index, src, _, _, low, count = kinds[kind]
        some = src.at[pl.ds(0, DEVS - 1), pl.ds(low, count)]
        if kind == "meta":
            some = some.at[:, :, pl.ds(0, 128)]
        pltpu.make_async_copy(some, some, send_sem.at[index]).wait()

    ones = {
        "x": (6, sx, rx.at[my_place], 0),
        "mx": (7, smx, rmx.at[my_place], 1),
        "fx": (8, rx, rx, 2),
        "fm": (9, rmx, rmx, 3),
        "y": (10, sy, ry, 4),
        "w": (11, sw, rw, 5),
        "flag": (12, sflag, rflag, 6),
    }

    def column(kind):
        index, src, dst, sem = ones[kind]
        for k in ORDER[:-1]:
            p = lax.rem(my_plane + k, PLANES)
            pltpu.make_async_remote_copy(
                src_ref=src.at[p], dst_ref=dst.at[my_plane], send_sem=send_sem.at[index],
                recv_sem=one_sem.at[sem], device_id={"seq": peer_at(k, 0)}, device_id_type=MESH,
            ).start()

    def across(kind, forward, first=0, last=PLANES):
        index, src, dst, sem = ones[kind]
        some = pl.ds(first, last - first)
        for j in range(1, PLANE):
            seat = lax.rem(my_place + j, PLANE)
            pltpu.make_async_remote_copy(
                src_ref=src.at[my_place if forward else seat, some],
                dst_ref=dst.at[my_place, some],
                send_sem=send_sem.at[index], recv_sem=one_sem.at[sem],
                device_id={"seq": peer_at(0, j)}, device_id_type=MESH,
            ).start()

    def one_wait(kind, n, sending):
        index, src, dst, sem = ones[kind]
        some = (src if sending else dst).at[pl.ds(0, n)]
        pltpu.make_async_copy(
            some, some, send_sem.at[index] if sending else one_sem.at[sem]
        ).wait()

    target, local, rank = token_slots(id_ref, owner_ref)
    plane_row = jnp.floor(target * (1.0 / PLANE))
    seat_row = target - plane_row * float(PLANE)
    direct = rank < float(SEATS)
    slot = jnp.where(direct, target * float(SEATS) + rank, -1.0)
    member = [
        (iota((PLANES, 128), 0) == plane_row[:, 128 * b : 128 * (b + 1)])
        & (rank[:, 128 * b : 128 * (b + 1)] >= float(SEATS))
        for b in range(BLOCKS)
    ]
    extra = seated_rank(PLANES, member)
    fits = (rank >= float(SEATS)) & (extra < float(EXTRA))
    xslot = jnp.where(fits, plane_row * float(EXTRA) + extra, -1.0)
    lost = jnp.max(jnp.where(extra >= float(EXTRA), 1.0, 0.0), axis=1, keepdims=True)

    for load in loads:
        load.wait()
    rows = rows_in[...]

    def fill(k):
        p = lax.rem(my_plane + k, PLANES)
        pick = onehot(iota((PLANE * SEATS, TOK), 0) + (p * PLANE * SEATS).astype(F32) == slot)
        parts = split_features(dot(pick, rows), SEATS)
        sbuf[pl.ds(p * PLANE, PLANE)] = jnp.concatenate(parts, axis=1).astype(BF16)

    fill(ORDER[0])
    pl.semaphore_wait(barrier, 2 * PLANE - 2 + PARTS - 1)
    for k in ORDER[:-1]:
        signal(column_sem, k, 0)
    for i, k in enumerate(ORDER[:-1]):
        for kind in ("qk", "v", "g"):
            start(kind, k, 0, 1)
        fill(ORDER[i + 1])
    block = dot(onehot(iota((PLANES * EXTRA, TOK), 0) == xslot), rows)
    sx[...] = jnp.concatenate(split_features(block, EXTRA), axis=1).astype(BF16)
    column("x")
    rx[my_place, my_plane] = sx[my_plane]

    when = iota((1, TOK), 1)
    when_high = jnp.floor(when * (1.0 / 32))
    when_low = when - 32.0 * when_high
    here = (me * TOK).astype(F32)

    def keys_of(rows_at, label, lanes_at):
        n = rows_at.shape[0]
        stack = [jnp.where(rows_at, r, 0.0) for r in (label, when_high, when_low)]
        found = dot_nt(jnp.concatenate(stack, axis=0).astype(BF16), onehot(lanes_at))
        label = found[:n]
        key = label * UNIT + 32.0 * found[n : 2 * n] + found[2 * n :]
        return key + jnp.where(label > 0.0, here, 0.0)

    tile = my_place // 4 * 128
    lane = jnp.where(direct, rank + (tile + lax.rem(my_place, 4) * SEATS).astype(F32), -1.0)
    key = keys_of(iota((DEVS, TOK), 0) == target, local + 1.0, iota((256, TOK), 0) == lane)
    key = jnp.where(iota((DEVS, 256), 1) == (tile + 127).astype(F32), lost, key)
    smeta[...] = key.reshape(DEVS, 1, 256)
    first_lane = my_plane * EXTRA + lax.rem(my_place, 2) * 64
    lane = jnp.where(fits, extra + first_lane.astype(F32), -1.0)
    label = local + 1.0 + seat_row * float(CL_DEV)
    key = keys_of(iota((PLANES, TOK), 0) == plane_row, label, iota((128, TOK), 0) == lane)
    smx[...] = key.reshape(PLANES, 1, 128)

    column("mx")
    rmx[my_place, my_plane] = smx[my_plane]
    pl.semaphore_wait(column_sem, PLANE - 1)
    for k in LATE:
        start_plane("meta", k)
    for k in ORDER[:3]:
        start("qk", k, 1, PLANE)
    rbuf[me] = sbuf[me]
    rmeta[me] = smeta[me]
    one_wait("x", PLANES - 1, False)
    one_wait("mx", PLANES - 1, False)
    across("fm", True)
    for k, first, last in zip(ORDER[3:], (0, 2, 4, 6, 7), (2, 4, 6, 7, 8)):
        start("qk", k, 1, PLANE)
        across("fx", True, first, last)
    for kind in ("v", "g"):
        for k in LATE:
            start(kind, k, 1, PLANE)

    slot_cols = turned(jnp.concatenate([slot[:, 128 * b : 128 * (b + 1)] for b in range(8)], axis=0))
    slot_cols = [slot_cols[:, b : b + 1] for b in range(BLOCKS)]

    def build_final(p, carry):
        slot_at = iota((128, 256), 1) + (p * PLANE * SEATS).astype(F32)
        final[p] = onehot(jnp.concatenate([slot_at == col for col in slot_cols], axis=0))
        return carry

    lax.fori_loop(0, PLANES, build_final, 0)

    for k in LATE:
        arrived("meta", (PLANES - k) % PLANES)
    got = jnp.sum(rmeta[...].reshape(PLANES, PLANE, 256), axis=1)
    lost_any = jnp.max(got[:, 127:128] + got[:, 255:256], axis=0, keepdims=True)
    sflag[0] = jnp.broadcast_to(lost_any, (1, 128))
    for i in range(1, PARTS):
        pltpu.make_async_remote_copy(
            src_ref=sflag.at[0], dst_ref=rflag.at[my_part], send_sem=send_sem.at[12],
            recv_sem=one_sem.at[6], device_id={"dp": part_at(i)}, device_id_type=MESH,
        ).start()
    rflag[my_part] = sflag[0]

    one_wait("fm", PLANE - 1, False)
    got_extra = jnp.sum(rmx[...].reshape(PLANE, PLANES, 128), axis=1)
    base = (my_place * CL_DEV).astype(F32) * UNIT
    got_extra = got_extra - base
    mine = (got_extra >= UNIT) & (got_extra < (1.0 + CL_DEV) * UNIT)
    got_extra = jnp.where(mine, got_extra, 0.0)
    got_extra = jnp.sum(got_extra.reshape(PLANE // 2, 2, 128), axis=1)
    keys_all = jnp.concatenate([got[:, :128], got[:, 128:], got_extra], axis=0)
    keys_all = jnp.where(keys_all < UNIT, NONE, keys_all)
    key_cols = turned(keys_all)
    n_rows = 2 * PLANES + PLANE // 2
    for r in range(n_rows):
        wide[r] = jnp.broadcast_to(key_cols[:, r : r + 1], (128, 128))

    def count(r, sums):
        less = wide[r]
        out = []
        for c in range(n_rows):
            hit = jnp.where(less < keys_all[c : c + 1], 1.0, 0.0)
            out.append(sums[c] + jnp.sum(hit.reshape(16, 8, 128), axis=0))
        return tuple(out)

    zero = jnp.zeros((8, 128), F32)
    counts = lax.fori_loop(0, n_rows, count, (zero,) * n_rows)
    place = jnp.concatenate([jnp.sum(c, axis=0, keepdims=True) for c in counts], axis=0)
    place = jnp.where(keys_all == NONE, 4096.0, place)
    place_cols = turned(place)
    starts = [jnp.zeros((1, 128), F32)]
    for c in range(1, CL_DEV):
        below = jnp.where(keys_all < (1.0 + c) * UNIT, 1.0, 0.0)
        below = jnp.sum(jnp.sum(below, axis=0, keepdims=True), axis=1, keepdims=True)
        starts.append(jnp.broadcast_to(below, (1, 128)))

    def build(p, carry):
        at = lax.broadcasted_iota(jnp.int32, (n_rows, 128), 0)
        first, second = (
            jnp.sum(jnp.where(at == p + PLANES * h, place, 0.0), axis=0, keepdims=True)
            for h in range(2)
        )
        both = jnp.concatenate([first[:, :96], second[:, :96]], axis=1)
        gather[p] = onehot(iota((TOK, PLANE * SEATS), 0) == both)
        at = lax.broadcasted_iota(jnp.int32, (128, 128), 1)
        first, second = (
            jnp.sum(jnp.where(at == p + PLANES * h, place_cols, 0.0), axis=1, keepdims=True)
            for h in range(2)
        )
        ungather[p, 0:96] = onehot(iota((96, TOK), 1) == first[:96])
        ungather[p, 96:192] = onehot(iota((96, TOK), 1) == second[:96])
        return carry

    lax.fori_loop(0, PLANES, build, 0)
    for u in range(PLANE // 2):
        r = 2 * PLANES + u
        xgather[:, 128 * u : 128 * (u + 1)] = onehot(iota((TOK, 128), 0) == place[r : r + 1])
        xungather[128 * u : 128 * (u + 1)] = onehot(iota((128, TOK), 1) == place_cols[:, r : r + 1])

    at = iota((BLOCKS, 128), 0) * 128.0 + iota((BLOCKS, 128), 1)
    first = jnp.zeros((BLOCKS, 128), F32)
    for c in range(1, CL_DEV):
        first = jnp.where(at >= starts[c], starts[c], first)
    first_cols = turned(first)

    def together(parts):
        return jnp.concatenate([p.reshape(-1, HD) for p in parts], axis=1).astype(BF16)

    def extras(ref, features):
        low = EXTRA * features[0] // 16 * 16
        block = ref[:, :, low : max(low + 16, EXTRA * (features[-1] + 1))].astype(F32)
        cuts = [block[:, :, EXTRA * f - low : EXTRA * (f + 1) - low] for f in features]
        return together(cuts)

    def collect(kind, features, cut):
        width = HD * len(features)
        acc[:, :width] = dot(xgather[...], extras(rx, features))
        for k in LATE:
            p = arrived(kind, (PLANES - k) % PLANES)
            part = dot(gather[p], together(cut(pl.ds(p * PLANE, PLANE))))
            if k == LATE[-1]:
                return acc[:, :width] + part
            acc[:, :width] += part

    def cut_qk(at):
        block = rbuf[at, 0 : 2 * SEATS].astype(F32)
        return [block[:, :SEATS], block[:, SEATS:]]

    def cut_v(at):
        return [rbuf[at, 2 * SEATS : 2 * SEATS + 32].astype(F32)[:, :SEATS]]

    def cut_g(at):
        return [rbuf[at, 4 * SEATS - 32 : 4 * SEATS].astype(F32)[:, 32 - SEATS :]]

    front = pl.ds(0, 128)
    body = pl.ds(128, TOK)
    xqk[front] = jnp.zeros((128, 2 * HD), BF16)
    xv[front] = jnp.zeros((128, HD), BF16)

    one_wait("fx", PLANE - 1, False)
    xqk[body] = collect("qk", (0, 1), cut_qk).astype(BF16)
    for b in range(BLOCKS):
        query = xqk[pl.ds(128 * (b + 1), 128), :HD]
        keys = xqk[pl.ds(128 * b, 256), HD:]
        scores = dot_nt(query, keys) * scale
        key_at = iota((128, 256), 1) + 128.0 * (b - 1)
        query_at = iota((128, 256), 0) + 128.0 * b
        allowed = (key_at <= query_at) & (key_at >= first_cols[:, b : b + 1])
        scores = jnp.where(allowed, scores, -1e30)
        weights = jnp.exp(scores - jnp.max(scores, axis=-1, keepdims=True))
        probs_ref[b] = weights / jnp.sum(weights, axis=-1, keepdims=True)

    start_rows = jnp.concatenate(starts, axis=0)
    end_rows = jnp.concatenate(starts[1:] + [jnp.full((1, 128), float(TOK), F32)], axis=0)
    sums = jnp.zeros((CL_DEV, HD), F32)
    for b in range(BLOCKS):
        row_at = iota((CL_DEV, 128), 1) + 128.0 * b
        owned = onehot((row_at >= start_rows) & (row_at < end_rows))
        sums = sums + dot(owned, xqk[pl.ds(128 * (b + 1), 128), HD:])
    blended = 0.5 * old_ref[...] + 0.5 * sums / (end_rows - start_rows)
    power = jnp.mean(blended * blended, axis=-1, keepdims=True)
    cent_ref[...] = blended * lax.rsqrt(power + 1e-6)

    xv[body] = collect("v", (2,), cut_v).astype(BF16)
    attn = [
        dot(probs_ref[b].astype(BF16), xv[pl.ds(128 * b, 256)]).astype(BF16) for b in range(BLOCKS)
    ]
    outs = jnp.concatenate(attn, axis=0)
    res[:, :HD] = outs
    for k in LATE:
        p = lax.rem(my_plane + k, PLANES)
        block = dot(ungather[p], outs).reshape(PLANE, SEATS, HD)
        sa[pl.ds(p * PLANE, PLANE)] = block[:, :16].astype(BF16)
        start_plane("a", k)
    ra[me] = sa[me]

    xg[...] = collect("g", (3,), cut_g).astype(BF16)
    value_tail = None
    for b in range(BLOCKS):
        dvals = dot_tn(probs_ref[b].astype(BF16), xg[pl.ds(128 * b, 128)])
        if b > 0:
            res[pl.ds(128 * (b - 1), 128), 3 * HD :] = (value_tail + dvals[:128]).astype(BF16)
        value_tail = dvals[128:]
    res[pl.ds(128 * (BLOCKS - 1), 128), 3 * HD :] = value_tail.astype(BF16)

    for k in LATE:
        p = lax.rem(my_plane + k, PLANES)
        parts = [
            dot(ungather[p], res[:, at]).reshape(PLANE, SEATS, HD)
            for at in (slice(0, HD), slice(3 * HD, 4 * HD))
        ]
        block = jnp.concatenate([parts[0][:, 16:], parts[1]], axis=1).astype(BF16)
        sc[pl.ds(p * PLANE, PLANE)] = block
        start_plane("c", k)

    key_tail = None
    for b in range(BLOCKS):
        mine = pl.ds(128 * b, 128)
        window = pl.ds(128 * b, 256)
        query = xqk[pl.ds(128 * (b + 1), 128), :HD]
        keys = xqk[window, HD:]
        grad = xg[mine]
        probs = probs_ref[b]
        delta = jnp.sum(grad.astype(F32) * res[mine, :HD].astype(F32), axis=-1, keepdims=True)
        dprobs = dot_nt(grad, xv[window])
        dscores = (probs * (dprobs - delta) * scale).astype(BF16)
        res[mine, HD : 2 * HD] = dot(dscores, keys).astype(BF16)
        dkeys = dot_tn(dscores, query)
        if b > 0:
            before = pl.ds(128 * (b - 1), 128)
            res[before, 2 * HD : 3 * HD] = (key_tail + dkeys[:128]).astype(BF16)
        key_tail = dkeys[128:]
    last = pl.ds(128 * (BLOCKS - 1), 128)
    res[last, 2 * HD : 3 * HD] = key_tail.astype(BF16)

    for i, k in enumerate(LATE):
        if i == 2:
            back = dot(xungather[...], res[...])
            back = [
                back[:, HD * f : HD * (f + 1)].reshape(PLANE, PLANES, EXTRA, HD) for f in range(4)
            ]
            sy[...] = jnp.concatenate(back, axis=2).astype(BF16)
            ry[my_place] = sy[my_place]
        p = lax.rem(my_plane + k, PLANES)
        parts = split_features(dot(ungather[p], res[:, HD : 3 * HD]), SEATS)
        block = jnp.concatenate(parts, axis=1).astype(BF16)
        sd[pl.ds(p * PLANE, PLANE)] = block
        start_plane("d", k)
        if 2 <= i < 6:
            across("y", False, 2 * i - 4, 2 * i - 2)
    rc[me] = sc[me]
    rd[me] = sd[me]
    one_wait("y", PLANE - 1, False)
    sw[...] = jnp.sum(ry[...].astype(F32), axis=0).astype(BF16)
    column("w")
    rw[my_plane] = sw[my_plane]

    for kind in ("meta", "qk", "v", "g", "a", "c"):
        sent(kind)
    for kind, n in (("x", 7), ("mx", 7), ("fx", 7), ("fm", 7), ("y", 7)):
        one_wait(kind, n, True)

    one_wait("flag", PARTS - 1, False)
    flag_ref[...] = jnp.max(rflag[...], axis=0)
    one_wait("flag", PARTS - 1, True)

    def cut_back(at):
        head = ra[at].astype(F32)
        rest = rc[at].astype(F32)
        keys = rd[at].astype(F32)
        outs = jnp.concatenate([head, rest[:, : SEATS - 16]], axis=1)
        return [outs, keys[:, :SEATS], keys[:, SEATS:], rest[:, SEATS - 16 :]]

    for kind in ("a", "c"):
        for k in LATE:
            arrived(kind, (PLANES - k) % PLANES)
    for k in LATE:
        p = arrived("d", (PLANES - k) % PLANES)
        part = dot(final[p, :, : PLANE * SEATS], together(cut_back(pl.ds(p * PLANE, PLANE))))
        if k == LATE[0]:
            acc[...] = part
        else:
            acc[...] += part
    xslot_cols = turned(
        jnp.concatenate([xslot[:, 128 * b : 128 * (b + 1)] for b in range(8)], axis=0)
    )
    pick = onehot(
        jnp.concatenate(
            [iota((128, PLANES * EXTRA), 1) == xslot_cols[:, b : b + 1] for b in range(BLOCKS)],
            axis=0,
        )
    )
    one_wait("w", PLANES - 1, False)
    block = rw[...].astype(F32)
    late = together([block[:, EXTRA * f : EXTRA * (f + 1)] for f in range(4)])
    found = (acc[...] + dot(pick, late)).astype(BF16)
    o_ref[...] = found[:, :HD]
    dq_ref[...] = found[:, HD : 2 * HD]
    dk_ref[...] = found[:, 2 * HD : 3 * HD]
    dv_ref[...] = found[:, 3 * HD :]
    sent("d")
    one_wait("w", 7, True)


def hand_over(*refs):
    n = len(refs) // 2
    for src, dst in zip(refs[:n], refs[n:]):
        dst[...] = src[...]


def shards(queries, key_rows, values, out_grad, cluster_id, cluster_owner, old_centroids):
    vmem = pl.BlockSpec(memory_space=pltpu.VMEM)
    row_out = jax.ShapeDtypeStruct((TOK, HD), BF16)
    out_shape = (row_out, row_out, row_out, row_out, jax.ShapeDtypeStruct((CL_DEV, HD), F32))
    by_plane = [pltpu.SemaphoreType.DMA((PLANES,))] * 7
    args = (queries, key_rows, values, out_grad, cluster_id, cluster_owner, old_centroids[0])

    def pair(rows, width, n=DEVS, dtype=BF16):
        return [pltpu.VMEM((n, rows, width), dtype)] * 2

    def params(ident):
        return pltpu.CompilerParams(
            collective_id=ident, has_side_effects=True, vmem_limit_bytes=56 << 20
        )

    sorted_rows = [
        pltpu.VMEM((TOK + 128, 2 * HD), BF16),
        pltpu.VMEM((TOK + 128, HD), BF16),
        pltpu.VMEM((TOK, HD), BF16),
    ]
    work = [
        pltpu.VMEM((BLOCKS, 128, 256), F32),
        pltpu.VMEM((TOK, 4 * HD), BF16),
        pltpu.SemaphoreType.REGULAR,
    ]

    def general(*args):
        return pl.pallas_call(
            kernel,
            out_shape=out_shape,
            in_specs=[vmem] * 7,
            out_specs=(vmem,) * 5,
            scratch_shapes=[
                *pair(1, 128, dtype=F32),
                *pair(ROOM, 2 * HD), *pair(ROOM, HD), *pair(ROOM, HD),
                *pair(ROOM, HD), *pair(ROOM, 3 * HD),
                pltpu.VMEM((PLANES, TOK, CHUNK), BF16),
                pltpu.VMEM((PLANES, CHUNK, TOK), BF16),
                pltpu.VMEM((PLANES, TOK, CHUNK), BF16),
                *sorted_rows,
                pltpu.VMEM((TOK, 3 * HD), F32),
                *work,
                pltpu.SemaphoreType.DMA((6,)),
                *by_plane[:6],
            ],
            compiler_params=params(1),
        )(*args)

    extra_rows = pltpu.VMEM((PLANE, PLANES, 4 * EXTRA, HD), BF16)
    *outs, flag = pl.pallas_call(
        kernel_fast,
        out_shape=out_shape + (jax.ShapeDtypeStruct((1, 128), F32),),
        in_specs=[pl.BlockSpec(memory_space=pl.ANY)] * 4 + [vmem] * 3,
        out_specs=(vmem,) * 6,
        scratch_shapes=[
            pltpu.VMEM((TOK, 4 * HD), BF16),
            pltpu.SemaphoreType.DMA((4,)),
            *pair(1, 256, dtype=F32),
            pltpu.VMEM((PLANES, 1, 128), F32),
            pltpu.VMEM((PLANE, PLANES, 1, 128), F32),
            pltpu.VMEM((PLANES, 4 * EXTRA, HD), BF16),
            extra_rows,
            *pair(4 * SEATS, HD), *pair(16, HD),
            *pair(2 * SEATS - 16, HD), *pair(2 * SEATS, HD),
            extra_rows, extra_rows,
            *pair(4 * EXTRA, HD, PLANES),
            *pair(1, 128, PARTS, F32),
            pltpu.VMEM((PLANES, TOK, PLANE * SEATS), BF16),
            pltpu.VMEM((PLANES, PLANE * SEATS, TOK), BF16),
            pltpu.VMEM((PLANES, TOK, 256), BF16),
            pltpu.VMEM((TOK, DEVS * EXTRA), BF16),
            pltpu.VMEM((DEVS * EXTRA, TOK), BF16),
            pltpu.VMEM((2 * PLANES + PLANE // 2, 128, 128), F32),
            *sorted_rows,
            pltpu.VMEM((TOK, 4 * HD), F32),
            *work,
            pltpu.SemaphoreType.DMA((14,)),
            *by_plane,
            pltpu.SemaphoreType.DMA((7,)),
        ],
        compiler_params=params(0),
    )(*args)

    outs = lax.cond(
        flag[0, 0] > 0.0, lambda args, outs: general(*args), lambda args, outs: outs, args, tuple(outs)
    )
    outs = pl.pallas_call(
        hand_over, out_shape=out_shape, in_specs=[vmem] * 5, out_specs=(vmem,) * 5
    )(*outs)
    return outs[0], outs[1], outs[2], outs[3], outs[4][None]


def solution(mesh):
    return jax.shard_map(
        shards,
        mesh=mesh,
        in_specs=(
            P(("dp", "seq"), None),
            P(("dp", "seq"), None),
            P(("dp", "seq"), None),
            P(("dp", "seq"), None),
            P("dp", "seq"),
            P("dp", None),
            P("dp", "seq", None),
        ),
        out_specs=(
            P(("dp", "seq"), None),
            P(("dp", "seq"), None),
            P(("dp", "seq"), None),
            P(("dp", "seq"), None),
            P("dp", "seq", None),
        ),
        check_vma=False,
    )
```
